32 devices in a mesh: dp: 8 (over z, y), fsdp: 4 (over x, core).
Axes of the slice: x: 2, y: 2, z: 4, core: 2. Of those that a mesh axis runs over, the one named last changes fastest.
Arguments:
- features: bfloat16 [32768, 768], P(('dp', 'fsdp')), may hold values from -6 to 6
- cotangent: bfloat16 [32768, 768], P(('dp', 'fsdp')), may hold values from -6 to 6
- segment_ids: int32 [32768], P(('dp', 'fsdp')), may hold values from -1 to 7, as said below
- attn_weights: float32 [3072, 768], P(('dp', 'fsdp')), may hold values from -0.8660254 to 0.8660254
- ffn_weights: float32 [2, 3072, 768], P(None, ('dp', 'fsdp')), may hold values from -0.21875 to 0.21875
- small_params: float32 [9216], P(('dp', 'fsdp')), may hold values from -0.8 to 1.4
- attn_first: float32 [3072, 768], P(('dp', 'fsdp')), may hold values from -162.9174 to 162.9174
- ffn_first: float32 [2, 3072, 768], P(None, ('dp', 'fsdp')), may hold values from -41.63445 to 41.63445
- small_first: float32 [9216], P(('dp', 'fsdp')), may hold values from -162.9174 to 162.9174
- attn_second: float32 [3072, 768], P(('dp', 'fsdp')), may hold values from 98.304 to 10813.44
- ffn_second: float32 [2, 3072, 768], P(None, ('dp', 'fsdp')), may hold values from 163.84 to 688.128
- small_second: float32 [9216], P(('dp', 'fsdp')), may hold values from 163.84 to 10813.44
- attn_ema: float32 [3072, 768], P(('dp', 'fsdp')), may hold values from -0.21875 to 0.21875
- ffn_ema: float32 [2, 3072, 768], P(None, ('dp', 'fsdp')), may hold values from -0.21875 to 0.21875
- small_ema: float32 [9216], P(('dp', 'fsdp')), may hold values from -3 to 3
Outputs:
- outputs: bfloat16 [32768, 768], P(('dp', 'fsdp'))
- input_grad: float32 [32768, 768], P(('dp', 'fsdp'))
- attn_new: float32 [3072, 768], P(('dp', 'fsdp'))
- ffn_new: float32 [2, 3072, 768], P(None, ('dp', 'fsdp'))
- small_new: float32 [9216], P(('dp', 'fsdp'))
- attn_first_new: float32 [3072, 768], P(('dp', 'fsdp'))
- ffn_first_new: float32 [2, 3072, 768], P(None, ('dp', 'fsdp'))
- small_first_new: float32 [9216], P(('dp', 'fsdp'))
- attn_second_new: float32 [3072, 768], P(('dp', 'fsdp'))
- ffn_second_new: float32 [2, 3072, 768], P(None, ('dp', 'fsdp'))
- small_second_new: float32 [9216], P(('dp', 'fsdp'))
- attn_ema_new: float32 [3072, 768], P(('dp', 'fsdp'))
- ffn_ema_new: float32 [2, 3072, 768], P(None, ('dp', 'fsdp'))
- small_ema_new: float32 [9216], P(('dp', 'fsdp'))
The draws below stay inside these ranges and needn't reach their ends.
Inputs may be any that keep to these rules, and one draw needn't show every extreme that they name: `segment_ids`: each aligned block of 1024 slots (one device's) holds whole utterances of 128 to 1024 frames, numbered 0, 1, 2, ... in order from the block's start, then padding marked -1 to the block's end; block 0 is one utterance of exactly 1024 frames; the last block holds utterances of exactly 128 frames.
All inputs are finite; a program needn't handle non-finite values.
Results may differ from the reference program's by a relative error of at most 0.015.
The reference program's roundings to bfloat16 on the way count: a program that leaves them out, or rounds other values in their place, can miss the bound.
Values may be sent and summed in bfloat16 or wider, within the bound.
A program may use at most 256 MiB of HBM per device.

```python
import math
import jax
import jax.numpy as jnp
from jax import lax

D = 768
HEADS = 12
FF = 3072
TOK_DEV = 1024
UTT_MAX = 1024
MINLEN = 128
STEP = 10
TOKENS = 32768
SMALL_N = 9216


def draw_segment_ids(key, part):
    blocks = TOKENS // TOK_DEV
    candidates = TOK_DEV // MINLEN + 1
    lengths = jax.random.randint(key, (blocks, candidates), MINLEN, UTT_MAX + 1)
    lengths = lengths.at[blocks - 1].set(MINLEN)
    lengths = lengths.at[0, 0].set(UTT_MAX)
    ends = jnp.cumsum(lengths, axis=1)
    fitting = ends <= TOK_DEV
    filled = jnp.max(jnp.where(fitting, ends, 0), axis=1)
    places = jnp.arange(TOK_DEV)
    passed = (ends[:, None, :] <= places[None, :, None]) & fitting[:, None, :]
    number = jnp.sum(passed.astype(jnp.int32), axis=2)
    result = jnp.where(places[None, :] < filled[:, None], number, -1)
    return result.reshape(-1).astype(jnp.int32)


def draw_attn_weights(key, part):
    base = jax.random.truncated_normal(key, -4.0, 4.0, (4 * D, D), jnp.float32)
    section = jnp.arange(4 * D) // D
    factor = jnp.where(section < 2, 1.5, jnp.where(section == 2, 1.0, 6.0))
    return base * factor[:, None] / math.sqrt(D)


def draw_small_params(key, part):
    key_gain = jax.random.fold_in(key, 11)
    key_bias = jax.random.fold_in(key, 23)
    total = 8 * D + FF
    position = jnp.arange(total)
    gains = jax.random.uniform(key_gain, (total,), jnp.float32, 0.6, 1.4)
    biases = 0.2 * jax.random.truncated_normal(key_bias, -4.0, 4.0, (total,), jnp.float32)
    is_gain = (position < D) | (position >= 2 * D) & (position < 3 * D)
    return jnp.where(is_gain, gains, biases)


def attn_grad_scale():
    section = jnp.arange(4 * D) // D
    return jnp.where(section < 3, 2.0, 0.4)[:, None] * math.sqrt(TOKENS) * jnp.ones((4 * D, D), jnp.float32)


def ffn_grad_scale():
    return 0.5 * math.sqrt(TOKENS) * jnp.ones((2, FF, D), jnp.float32)


def small_grad_scale():
    total = 8 * D + FF
    segment = jnp.minimum(jnp.arange(total) // D, 8)
    table = jnp.array([1.0, 1.4, 1.0, 1.0, 2.0, 2.0, 1.4, 1.0, 0.5], jnp.float32)
    return table[segment] * math.sqrt(TOKENS)


def first_from(key, scale_arr):
    base = jax.random.truncated_normal(key, -4.0, 4.0, scale_arr.shape, jnp.float32)
    return 0.111 * base * scale_arr


def second_from(key, scale_arr):
    spread = jax.random.uniform(key, scale_arr.shape, jnp.float32, math.log(0.02), math.log(0.08))
    return jnp.exp(spread) * scale_arr * scale_arr


def draw_attn_first(key, part):
    return first_from(jax.random.fold_in(key, 31), attn_grad_scale())


def draw_ffn_first(key, part):
    return first_from(jax.random.fold_in(key, 37), ffn_grad_scale())


def draw_small_first(key, part):
    return first_from(jax.random.fold_in(key, 41), small_grad_scale())


def draw_attn_second(key, part):
    return second_from(jax.random.fold_in(key, 43), attn_grad_scale())


def draw_ffn_second(key, part):
    return second_from(jax.random.fold_in(key, 47), ffn_grad_scale())


def draw_small_second(key, part):
    return second_from(jax.random.fold_in(key, 53), small_grad_scale())


def shard_levels(stream_key, shape, split, smallest, top_value):
    def one(dim, blocks):
        draws = jax.random.uniform(jax.random.fold_in(jax.random.fold_in(stream_key, 6), dim), (blocks,), jnp.float32, smallest / len(split), top_value / len(split))
        return jnp.repeat(jnp.exp(draws), shape[dim] // blocks).reshape((-1,) + (1,) * (len(shape) - dim - 1))

    gain = one(*split[0])
    for cut in split[1:]:
        gain = gain * one(*cut)
    return gain


def bell_draw(key, dims, scale, most, cuts=(), kind=jnp.bfloat16):
    values = jax.random.normal(key, dims, jnp.float32) * scale
    if len(cuts) > 0:
        values = shard_levels(key, dims, cuts, -0.22, 0.18) * values
    return jnp.clip(values, min=-most, max=most).astype(kind)


def setup_inputs(seed: int = 0) -> dict:
    splits = jax.random.split(jax.random.key(seed), 16)
    return {
        "features": bell_draw(splits[0], (TOKENS, D), 1.0, 6.0, ((0, 32),)),
        "cotangent": bell_draw(splits[1], (TOKENS, D), 1.0, 6.0, ((0, 32),)),
        "segment_ids": draw_segment_ids(jax.random.fold_in(splits[15], 71), 0),
        "attn_weights": draw_attn_weights(jax.random.fold_in(splits[15], 71), 0),
        "ffn_weights": bell_draw(splits[4], (2, FF, D), D ** -0.5, 0.21875, ((1, 32),), jnp.float32),
        "small_params": draw_small_params(jax.random.fold_in(splits[15], 71), 0),
        "attn_first": draw_attn_first(jax.random.fold_in(splits[15], 71), 0),
        "ffn_first": draw_ffn_first(jax.random.fold_in(splits[15], 71), 0),
        "small_first": draw_small_first(jax.random.fold_in(splits[15], 71), 0),
        "attn_second": draw_attn_second(jax.random.fold_in(splits[15], 71), 0),
        "ffn_second": draw_ffn_second(jax.random.fold_in(splits[15], 71), 0),
        "small_second": draw_small_second(jax.random.fold_in(splits[15], 71), 0),
        "attn_ema": bell_draw(splits[12], (4 * D, D), D ** -0.5, 0.21875, ((0, 32),), jnp.float32),
        "ffn_ema": bell_draw(splits[13], (2, FF, D), D ** -0.5, 0.21875, ((1, 32),), jnp.float32),
        "small_ema": bell_draw(splits[14], (SMALL_N,), 0.5, 3.0, ((0, 32),), jnp.float32),
    }


@jax.custom_vjp
def low(v):
    return lax.optimization_barrier(v.astype(jnp.bfloat16)).astype(jnp.float32)

@jax.custom_vjp
def low_back(v):
    return v

def low_keep(v):
    return (low(v), None)

def low_pass(kept, grad):
    return (grad,)

def back_keep(v):
    return (v, None)

def back_low(kept, grad):
    return (low(grad),)
low.defvjp(low_keep, low_pass)
low_back.defvjp(back_keep, back_low)

def exact_dot(left_arg, right_arg):
    return jnp.dot(left_arg, right_arg, precision=lax.Precision.HIGHEST)

def layer_norm(residual, gain_vec, bias_vec):
    centre = residual - lax.optimization_barrier(jnp.mean(residual, axis=-1, keepdims=True))
    spread = lax.optimization_barrier(jnp.mean(centre * centre, axis=-1, keepdims=True))
    return centre * lax.rsqrt(spread + 1e-05) * gain_vec + bias_vec

def block_forward(frames, block_ids, attn_full, ffn_full, small_full):
    weights = low(attn_full)
    hidden_w = low(ffn_full)
    smalls = low(small_full)
    vectors = smalls[:8 * D].reshape(8, D)
    hidden_bias = smalls[8 * D:]
    rows_here = frames.shape[0]
    head_dim = D // HEADS
    score_scale = 1.0 / math.sqrt(head_dim)
    queries = low_back(low(exact_dot(frames, weights[:D].T) + vectors[4]))
    keys_all = low_back(low(exact_dot(frames, weights[D:2 * D].T)))
    values_all = low_back(low(exact_dot(frames, weights[2 * D:3 * D].T) + vectors[5]))
    key_heads = keys_all.reshape(rows_here, HEADS, head_dim)
    value_heads = values_all.reshape(rows_here, HEADS, head_dim)
    block_rows = min(512, rows_here)
    block_count = rows_here // block_rows

    def attend(block_item):
        query_block, id_block = block_item
        scores = low_back(jnp.einsum('qhd,khd->hqk', query_block, key_heads, precision=lax.Precision.HIGHEST) * score_scale)
        same_utt = (id_block[:, None] == block_ids[None, :])[None]
        scores = jnp.where(same_utt, scores, -1000000000.0)
        weights_attn = low(jax.nn.softmax(scores, axis=-1))
        return jnp.einsum('hqk,khd->qhd', weights_attn, value_heads, precision=lax.Precision.HIGHEST)
    mixed_heads = lax.map(jax.checkpoint(attend), (queries.reshape(block_count, block_rows, HEADS, head_dim), block_ids.reshape(block_count, block_rows)))
    mixed_heads = low_back(low(mixed_heads.reshape(rows_here, D)))
    branch = low_back(exact_dot(mixed_heads, weights[3 * D:].T)) + vectors[6]
    normed_one = layer_norm(frames + branch, vectors[0], vectors[1])
    hidden = low_back(exact_dot(low(normed_one), hidden_w[0].T)) + hidden_bias
    active = low(jax.nn.gelu(hidden, approximate=False))
    residual_two = normed_one + low_back(exact_dot(active, hidden_w[1])) + vectors[7]
    return layer_norm(residual_two, vectors[2], vectors[3])

def adam_step(weight, grad_sum, first_mom, second_mom, average, decay, rate):
    first_new = 0.9 * first_mom + 0.1 * grad_sum
    second_new = 0.98 * second_mom + 0.02 * grad_sum * grad_sum
    corrected = first_new / (1.0 - 0.9 ** STEP)
    denominator = jnp.sqrt(second_new / (1.0 - 0.98 ** STEP)) + 1e-06
    weight_new = weight - rate * (corrected / denominator + decay * weight)
    average_new = 0.75 * average + 0.25 * weight_new
    return (weight_new, first_new, second_new, average_new)

def reference(features, cotangent, segment_ids, attn_weights, ffn_weights, small_params, attn_first, ffn_first, small_first, attn_second, ffn_second, small_second, attn_ema, ffn_ema, small_ema):
    block_count = features.shape[0] // TOK_DEV
    frame_blocks = features.astype(jnp.float32).reshape(block_count, TOK_DEV, D)
    grad_blocks = cotangent.astype(jnp.float32).reshape(block_count, TOK_DEV, D)
    id_blocks = segment_ids.reshape(block_count, TOK_DEV)

    def one_block(totals, block_item):
        frames, grads_out, block_ids = block_item

        def forward(frame_arg, attn_arg, ffn_arg, small_arg):
            return block_forward(frame_arg, block_ids, attn_arg, ffn_arg, small_arg)
        result, pullback = jax.vjp(forward, frames, attn_weights, ffn_weights, small_params)
        valid = (block_ids >= 0).astype(jnp.float32)[:, None]
        input_part, attn_part, ffn_part, small_part = pullback(grads_out * valid)
        totals = (totals[0] + attn_part, totals[1] + ffn_part, totals[2] + small_part)
        return (totals, (result.astype(jnp.bfloat16), input_part))
    zero_sums = (jnp.zeros_like(attn_weights), jnp.zeros_like(ffn_weights), jnp.zeros_like(small_params))
    totals, (outputs, input_grad) = lax.scan(one_block, zero_sums, (frame_blocks, grad_blocks, id_blocks))
    outputs = outputs.reshape(-1, D)
    input_grad = input_grad.reshape(-1, D)
    attn_new, attn_first_new, attn_second_new, attn_ema_new = adam_step(attn_weights, totals[0], attn_first, attn_second, attn_ema, 0.01, 0.05)
    ffn_new, ffn_first_new, ffn_second_new, ffn_ema_new = adam_step(ffn_weights, totals[1], ffn_first, ffn_second, ffn_ema, 0.01, 0.05)
    small_new, small_first_new, small_second_new, small_ema_new = adam_step(small_params, totals[2], small_first, small_second, small_ema, 0.0, 0.3)
    return (outputs, input_grad, attn_new, ffn_new, small_new, attn_first_new, ffn_first_new, small_first_new, attn_second_new, ffn_second_new, small_second_new, attn_ema_new, ffn_ema_new, small_ema_new)
```

```python
from functools import partial

import jax
import jax.numpy as jnp
from jax import lax
from jax.experimental import pallas as pl
from jax.experimental.pallas import tpu as pltpu
from jax.sharding import PartitionSpec as P

D = 768
HEADS = 12
HD = D // HEADS
STEP = 10
LOG2E = 1.4426950408889634
INV_SQRT2 = 0.7071067811865476
INV_SQRT2PI = 0.3989422804014327
BIG = 2.0**30
VMEM_LIMIT = 60 * 1024 * 1024

bf = jnp.bfloat16
f32 = jnp.float32
TN = (((0,), (0,)), ((), ()))
NN = (((1,), (0,)), ((), ()))
NT = (((1,), (1,)), ((), ()))


def dot(left, right, dims):
    return lax.dot_general(left, right, dims, preferred_element_type=f32)


def rows_at(i, size):
    return pl.ds(pl.multiple_of(i * size, size), size)


def column(row):
    return jnp.transpose(jnp.broadcast_to(row, (128, row.shape[1])))


def widen(col, width):
    return jnp.concatenate([col] * (width // 128), axis=1) if width > 128 else col


def lane_fold(x):
    total = x[:, :128]
    for i in range(1, x.shape[1] // 128):
        total = total + x[:, 128 * i : 128 * (i + 1)]
    return total


def fold_row(part):
    return jnp.sum(jnp.transpose(part), axis=0, keepdims=True)


def segment_rows(seg):
    ids = lax.broadcasted_iota(jnp.int32, (16, seg.shape[1]), 0) - 1
    same = jnp.where(ids == seg, 1.0, 0.0)
    return ((same - 1.0) * BIG).astype(bf), same.astype(bf)


def forward_kernel(x_ref, seg_ref, w_ref, sm_ref, qkv_ref, o_ref, l_ref):
    t = x_ref.shape[0]
    block = 256

    def project_block(i, _):
        rows = rows_at(i, block)
        sec = i // (D // block)
        off = i - sec * (D // block)
        bias = sm_ref[:, pl.ds(pl.multiple_of((4 + sec // 2) * D + off * block, block), block)]
        keep = jnp.where(sec == 1, 0.0, 1.0)
        col = column(bias.astype(f32) * keep)
        qkv_ref[rows, :] = (dot(w_ref[rows, :], x_ref[...], NT) + widen(col, t)).astype(bf)
        return 0

    lax.fori_loop(0, 3 * D // block, project_block, 0)
    q_rows, k_rows = segment_rows(seg_ref[...])

    def head(h, _):
        rows = rows_at(h, HD)
        q = qkv_ref[rows, :] * bf(0.125)
        k = qkv_ref[pl.ds(pl.multiple_of(D + h * HD, HD), HD), :]
        v = qkv_ref[pl.ds(pl.multiple_of(2 * D + h * HD, HD), HD), :]
        s = dot(jnp.concatenate([k, k_rows], 0), jnp.concatenate([q, q_rows], 0), TN)
        top = jnp.max(s, axis=0, keepdims=True)
        e = jnp.exp2((s - top) * LOG2E)
        total = jnp.sum(e, axis=0, keepdims=True)
        o_ref[rows, :] = (dot(v, e.astype(bf), NN) * (1.0 / total)).astype(bf)
        l_ref[h] = top + jnp.log(total)
        return 0

    lax.fori_loop(0, HEADS, head, 0)


def gelu_both(h):
    cdf = 0.5 + 0.5 * lax.erf(h * INV_SQRT2)
    pdf = jnp.exp(h * h * -0.5) * INV_SQRT2PI
    return h * cdf, cdf + h * pdf


VECS = (0, 1, 2, 3, 6, 7)


def middle_kernel(
    x_ref, o_ref, cot_ref, seg_ref, wo_ref, w1_ref, w2_ref, sm_ref,
    out_ref, dr1_ref, do_ref, dwo_ref, dw1_ref, dw2_ref, sg_ref,
    a1_ref, xh_ref, act_ref, gp_ref, rs_ref, low_ref, df_ref, vec_ref, part_ref,
):
    t = x_ref.shape[0]
    ff = w1_ref.shape[0]
    block, lanes = 256, 256
    for n, i in enumerate(VECS):
        vec_ref[n] = column(sm_ref[:, D * i : D * (i + 1)].astype(f32))
    part_ref[...] = jnp.zeros_like(part_ref)

    def vec(i):
        return widen(vec_ref[VECS.index(i)], lanes)

    def over_lanes(step):
        def body(c, _):
            step(rows_at(c, lanes))
            return 0

        lax.fori_loop(0, t // lanes, body, 0)

    def norm(r):
        centre = r - jnp.mean(r, axis=0, keepdims=True)
        scale = lax.rsqrt(jnp.mean(centre * centre, axis=0, keepdims=True) + 1e-5)
        return centre * scale, scale

    def norm_back(dy, xh, scale, gain):
        dx = dy * gain
        mean_one = jnp.mean(dx, axis=0, keepdims=True)
        mean_two = jnp.mean(dx * xh, axis=0, keepdims=True)
        return scale * (dx - mean_one - xh * mean_two)

    def first_norm(cs):
        r1 = jnp.transpose(x_ref[cs, :]).astype(f32) + dot(wo_ref[...], o_ref[:, cs], NN) + vec(6)
        xh, scale = norm(r1)
        xh_ref[:, cs] = xh
        rs_ref[:, cs] = scale
        a1 = xh * vec(0) + vec(1)
        a1_ref[:, cs] = a1 + vec(7)
        low_ref[:, cs] = a1.astype(bf)

    over_lanes(first_norm)

    def up_down(j, _):
        rows = rows_at(j, block)
        bias = sm_ref[:, pl.ds(pl.multiple_of(8 * D + j * block, block), block)]
        hid = dot(w1_ref[rows, :], low_ref[...], NN) + widen(column(bias.astype(f32)), t)
        act, slope = gelu_both(hid)
        act = act.astype(bf)
        act_ref[rows, :] = act
        gp_ref[rows, :] = slope.astype(gp_ref.dtype)
        a1_ref[...] += dot(w2_ref[rows, :], act, TN)
        return 0

    lax.fori_loop(0, ff // block, up_down, 0)

    def second_norm(cs):
        xh, scale = norm(a1_ref[:, cs])
        out_ref[cs, :] = jnp.transpose((xh * vec(2) + vec(3)).astype(bf))
        valid = jnp.where(seg_ref[:, cs] >= 0, 1.0, 0.0)
        dy = jnp.transpose(cot_ref[cs, :]).astype(f32) * valid
        dr = norm_back(dy, xh, scale, vec(2))
        a1_ref[:, cs] = dr
        df_ref[:, cs] = dr.astype(bf)
        part_ref[0] += lane_fold(dy * xh)
        part_ref[1] += lane_fold(dy)
        part_ref[2] += lane_fold(dr)

    over_lanes(second_norm)

    def back(j, _):
        rows = rows_at(j, block)
        dh = dot(w2_ref[rows, :], df_ref[...], NN) * gp_ref[rows, :].astype(f32)
        sg_ref[:, pl.ds(pl.multiple_of(8 * D + j * block, block), block)] = fold_row(lane_fold(dh))
        low = dh.astype(bf)
        dw2_ref[rows, :] = dot(act_ref[rows, :], df_ref[...], NT).astype(dw2_ref.dtype)
        dw1_ref[rows, :] = dot(low, low_ref[...], NT).astype(dw1_ref.dtype)
        a1_ref[...] += dot(w1_ref[rows, :], low, TN)
        return 0

    lax.fori_loop(0, ff // block, back, 0)

    def first_back(cs):
        dy = a1_ref[:, cs]
        xh = xh_ref[:, cs]
        dr = norm_back(dy, xh, rs_ref[:, cs], vec(0))
        dr1_ref[:, cs] = dr
        dz = dr.astype(bf)
        low_ref[:, cs] = dz
        part_ref[3] += lane_fold(dy * xh)
        part_ref[4] += lane_fold(dy)
        part_ref[5] += lane_fold(dr)
        do_ref[:, cs] = dot(wo_ref[...], dz, TN).astype(bf)

    over_lanes(first_back)
    dwo_ref[...] = dot(low_ref[...], o_ref[...], NT).astype(dwo_ref.dtype)
    for n, i in enumerate((2, 3, 7, 0, 1, 6)):
        sg_ref[:, D * i : D * (i + 1)] = fold_row(part_ref[n])
    sg_ref[:, 4 * D : 6 * D] = jnp.zeros((1, 2 * D), f32)


def backward_kernel(
    x_ref, seg_ref, w_ref, qkv_ref, o_ref, l_ref, do_ref, dr1_ref,
    dx_ref, dw_ref, db_ref,
    g_ref,
):
    t = x_ref.shape[0]
    q_rows, k_rows = segment_rows(seg_ref[...])

    def head(h, _):
        rows = rows_at(h, HD)
        krow = pl.ds(pl.multiple_of(D + h * HD, HD), HD)
        vrow = pl.ds(pl.multiple_of(2 * D + h * HD, HD), HD)
        q, k, v, do = qkv_ref[rows, :], qkv_ref[krow, :], qkv_ref[vrow, :], do_ref[rows, :]
        inner = jnp.sum(do.astype(f32) * o_ref[rows, :].astype(f32), axis=0, keepdims=True)
        s = dot(
            jnp.concatenate([k, k_rows], 0), jnp.concatenate([q * bf(0.125), q_rows], 0), TN
        )
        p = jnp.exp2((s - l_ref[h]) * LOG2E)
        dp = dot(v, do, TN)
        ds = (p * (dp - inner)).astype(bf)
        g_ref[vrow, :] = dot(do, p.astype(bf), NT).astype(bf)
        g_ref[krow, :] = (dot(q, ds, NT) * 0.125).astype(bf)
        g_ref[rows, :] = (dot(k, ds, NN) * 0.125).astype(bf)
        return 0

    lax.fori_loop(0, HEADS, head, 0)
    block = 256

    def weight_block(i, _):
        rows = rows_at(i, block)
        g = g_ref[rows, :]
        dw_ref[rows, :] = dot(g, x_ref[...], NN).astype(dw_ref.dtype)
        db_ref[:, rows] = fold_row(lane_fold(g.astype(f32)))
        return 0

    lax.fori_loop(0, 3 * D // block, weight_block, 0)

    def input_block(i, _):
        rows = rows_at(i, block)
        dx_ref[rows, :] = jnp.transpose(dr1_ref[:, rows]) + dot(g_ref[:, rows], w_ref[...], TN)
        return 0

    lax.fori_loop(0, t // block, input_block, 0)


def call(kernel, name, outs, scratch, *args):
    return pl.pallas_call(
        kernel,
        out_shape=[jax.ShapeDtypeStruct(s, d) for s, d in outs],
        scratch_shapes=[pltpu.VMEM(s, d) for s, d in scratch],
        compiler_params=pltpu.CompilerParams(vmem_limit_bytes=VMEM_LIMIT),
        name=name,
    )(*args)


def adam_step(weight, grad_sum, first_mom, second_mom, average, decay, rate):
    first_new = 0.9 * first_mom + 0.1 * grad_sum
    second_new = 0.98 * second_mom + 0.02 * grad_sum * grad_sum
    corrected = first_new / (1.0 - 0.9**STEP)
    denominator = jnp.sqrt(second_new / (1.0 - 0.98**STEP)) + 1e-06
    weight_new = weight - rate * (corrected / denominator + decay * weight)
    average_new = 0.75 * average + 0.25 * weight_new
    return (weight_new, first_new, second_new, average_new)


def local(
    features, cotangent, segment_ids, attn_weights, ffn_weights, small_params,
    attn_first, ffn_first, small_first, attn_second, ffn_second, small_second,
    attn_ema, ffn_ema, small_ema,
):
    axes = ("dp", "fsdp")
    t = features.shape[0]
    attn_full = lax.all_gather(attn_weights.astype(bf), axes, axis=0, tiled=True)
    ffn_full = lax.all_gather(ffn_weights.astype(bf), axes, axis=1, tiled=True)
    small_full = lax.all_gather(small_params.astype(bf), axes, axis=0, tiled=True)
    ff = ffn_full.shape[1]
    smalls = small_full.reshape(1, -1)
    seg = segment_ids.reshape(1, t)
    qkv, mixed, logs = call(
        forward_kernel, "attend_forward",
        [((3 * D, t), bf), ((D, t), bf), ((HEADS, 1, t), f32)], [],
        features, seg, attn_full[: 3 * D], smalls,
    )
    outputs, dr1, do, dwo, dw1, dw2, small_grad = call(
        middle_kernel, "middle",
        [((t, D), bf), ((D, t), f32), ((D, t), bf), ((D, D), bf), ((ff, D), bf), ((ff, D), bf),
         ((1, smalls.shape[1]), f32)],
        [((D, t), f32), ((D, t), f32), ((ff, t), bf), ((ff, t), bf), ((1, t), f32), ((D, t), bf),
         ((D, t), bf), ((6, D, 128), f32), ((6, D, 128), f32)],
        features, mixed, cotangent, seg, attn_full[3 * D :], ffn_full[0], ffn_full[1], smalls,
    )
    input_grad, dqkv, bias_grad = call(
        backward_kernel, "attend_backward",
        [((t, D), f32), ((3 * D, D), bf), ((1, 3 * D), f32)], [((3 * D, t), bf)],
        features, seg, attn_full[: 3 * D], qkv, mixed, logs, do, dr1,
    )
    small_grad = small_grad.reshape(-1)
    small_grad = jnp.concatenate(
        [small_grad[: 4 * D], bias_grad[0, :D], bias_grad[0, 2 * D :], small_grad[6 * D :]]
    )
    attn_sum, ffn_sum, small_sum = (
        lax.psum_scatter(jnp.concatenate([dqkv, dwo]), axes, scatter_dimension=0, tiled=True),
        lax.psum_scatter(jnp.stack([dw1, dw2]), axes, scatter_dimension=1, tiled=True),
        lax.psum_scatter(small_grad, axes, scatter_dimension=0, tiled=True),
    )
    attn = adam_step(
        attn_weights, attn_sum.astype(f32), attn_first, attn_second, attn_ema, 0.01, 0.05
    )
    ffn = adam_step(ffn_weights, ffn_sum.astype(f32), ffn_first, ffn_second, ffn_ema, 0.01, 0.05)
    small = adam_step(
        small_params, small_sum, small_first, small_second, small_ema, 0.0, 0.3
    )
    return (outputs, input_grad) + tuple(x for trio in zip(attn, ffn, small) for x in trio)


def solution(mesh):
    row = P(("dp", "fsdp"), None)
    wide = P(None, ("dp", "fsdp"), None)
    flat = P(("dp", "fsdp"))
    state = (row, wide, flat)
    return jax.shard_map(
        local,
        mesh=mesh,
        in_specs=(row, row, flat) + state * 4,
        out_specs=(row, row) + state * 4,
        check_vma=False,
    )
```

```python
from functools import partial

import jax
import jax.numpy as jnp
from jax import lax
from jax.experimental import pallas as pl
from jax.experimental.pallas import tpu as pltpu
from jax.sharding import PartitionSpec as P

D = 768
HEADS = 12
HD = D // HEADS
STEP = 10
LOG2E = 1.4426950408889634
INV_SQRT2 = 0.7071067811865476
INV_SQRT2PI = 0.3989422804014327
BIG = 2.0**30
VMEM_LIMIT = 60 * 1024 * 1024

bf = jnp.bfloat16
f32 = jnp.float32
TN = (((0,), (0,)), ((), ()))
NN = (((1,), (0,)), ((), ()))
NT = (((1,), (1,)), ((), ()))


def dot(left, right, dims):
    return lax.dot_general(left, right, dims, preferred_element_type=f32)


def rows_at(i, size):
    return pl.ds(pl.multiple_of(i * size, size), size)


def column(row):
    return jnp.transpose(jnp.broadcast_to(row, (128, row.shape[1])))


def widen(col, width):
    return jnp.concatenate([col] * (width // 128), axis=1) if width > 128 else col


def lane_fold(x):
    total = x[:, :128]
    for i in range(1, x.shape[1] // 128):
        total = total + x[:, 128 * i : 128 * (i + 1)]
    return total


def fold_row(part):
    return jnp.sum(jnp.transpose(part), axis=0, keepdims=True)


def segment_rows(seg):
    ids = lax.broadcasted_iota(jnp.int32, (16, seg.shape[1]), 0) - 1
    same = jnp.where(ids == seg, 1.0, 0.0)
    return ((same - 1.0) * BIG).astype(bf), same.astype(bf)


def plain_forward_kernel(x_ref, seg_ref, w_ref, sm_ref, qkv_ref, o_ref, l_ref):
    t = x_ref.shape[0]
    block = 256

    def project_block(i, _):
        rows = rows_at(i, block)
        sec = i // (D // block)
        off = i - sec * (D // block)
        bias = sm_ref[:, pl.ds(pl.multiple_of((4 + sec // 2) * D + off * block, block), block)]
        keep = jnp.where(sec == 1, 0.0, 1.0)
        col = column(bias.astype(f32) * keep)
        qkv_ref[rows, :] = (dot(w_ref[rows, :], x_ref[...], NT) + widen(col, t)).astype(bf)
        return 0

    lax.fori_loop(0, 3 * D // block, project_block, 0)
    q_rows, k_rows = segment_rows(seg_ref[...])

    def head(h, _):
        rows = rows_at(h, HD)
        q = qkv_ref[rows, :] * bf(0.125)
        k = qkv_ref[pl.ds(pl.multiple_of(D + h * HD, HD), HD), :]
        v = qkv_ref[pl.ds(pl.multiple_of(2 * D + h * HD, HD), HD), :]
        s = dot(jnp.concatenate([k, k_rows], 0), jnp.concatenate([q, q_rows], 0), TN)
        top = jnp.max(s, axis=0, keepdims=True)
        e = jnp.exp2((s - top) * LOG2E)
        total = jnp.sum(e, axis=0, keepdims=True)
        o_ref[rows, :] = (dot(v, e.astype(bf), NN) * (1.0 / total)).astype(bf)
        l_ref[h] = top + jnp.log(total)
        return 0

    lax.fori_loop(0, HEADS, head, 0)


def gelu_both(h):
    cdf = 0.5 + 0.5 * lax.erf(h * INV_SQRT2)
    pdf = jnp.exp(h * h * -0.5) * INV_SQRT2PI
    return h * cdf, cdf + h * pdf


PLAIN_VECS = (0, 1, 2, 3, 6, 7)


def plain_middle_kernel(
    x_ref, o_ref, cot_ref, seg_ref, wo_ref, w1_ref, w2_ref, sm_ref,
    out_ref, dr1_ref, do_ref, dwo_ref, dw1_ref, dw2_ref, sg_ref,
    a1_ref, xh_ref, act_ref, gp_ref, rs_ref, low_ref, df_ref, vec_ref, part_ref,
):
    t = x_ref.shape[0]
    ff = w1_ref.shape[0]
    block, lanes = 256, 256
    for n, i in enumerate(PLAIN_VECS):
        vec_ref[n] = column(sm_ref[:, D * i : D * (i + 1)].astype(f32))
    part_ref[...] = jnp.zeros_like(part_ref)

    def vec(i):
        return widen(vec_ref[PLAIN_VECS.index(i)], lanes)

    def over_lanes(step):
        def body(c, _):
            step(rows_at(c, lanes))
            return 0

        lax.fori_loop(0, t // lanes, body, 0)

    def norm(r):
        centre = r - jnp.mean(r, axis=0, keepdims=True)
        scale = lax.rsqrt(jnp.mean(centre * centre, axis=0, keepdims=True) + 1e-5)
        return centre * scale, scale

    def norm_back(dy, xh, scale, gain):
        dx = dy * gain
        mean_one = jnp.mean(dx, axis=0, keepdims=True)
        mean_two = jnp.mean(dx * xh, axis=0, keepdims=True)
        return scale * (dx - mean_one - xh * mean_two)

    def first_norm(cs):
        r1 = jnp.transpose(x_ref[cs, :]).astype(f32) + dot(wo_ref[...], o_ref[:, cs], NN) + vec(6)
        xh, scale = norm(r1)
        xh_ref[:, cs] = xh
        rs_ref[:, cs] = scale
        a1 = xh * vec(0) + vec(1)
        a1_ref[:, cs] = a1 + vec(7)
        low_ref[:, cs] = a1.astype(bf)

    over_lanes(first_norm)

    def up_down(j, _):
        rows = rows_at(j, block)
        bias = sm_ref[:, pl.ds(pl.multiple_of(8 * D + j * block, block), block)]
        hid = dot(w1_ref[rows, :], low_ref[...], NN) + widen(column(bias.astype(f32)), t)
        act, slope = gelu_both(hid)
        act = act.astype(bf)
        act_ref[rows, :] = act
        gp_ref[rows, :] = slope.astype(gp_ref.dtype)
        a1_ref[...] += dot(w2_ref[rows, :], act, TN)
        return 0

    lax.fori_loop(0, ff // block, up_down, 0)

    def second_norm(cs):
        xh, scale = norm(a1_ref[:, cs])
        out_ref[cs, :] = jnp.transpose((xh * vec(2) + vec(3)).astype(bf))
        valid = jnp.where(seg_ref[:, cs] >= 0, 1.0, 0.0)
        dy = jnp.transpose(cot_ref[cs, :]).astype(f32) * valid
        dr = norm_back(dy, xh, scale, vec(2))
        a1_ref[:, cs] = dr
        df_ref[:, cs] = dr.astype(bf)
        part_ref[0] += lane_fold(dy * xh)
        part_ref[1] += lane_fold(dy)
        part_ref[2] += lane_fold(dr)

    over_lanes(second_norm)

    def back(j, _):
        rows = rows_at(j, block)
        dh = dot(w2_ref[rows, :], df_ref[...], NN) * gp_ref[rows, :].astype(f32)
        sg_ref[:, pl.ds(pl.multiple_of(8 * D + j * block, block), block)] = fold_row(lane_fold(dh))
        low = dh.astype(bf)
        dw2_ref[rows, :] = dot(act_ref[rows, :], df_ref[...], NT).astype(dw2_ref.dtype)
        dw1_ref[rows, :] = dot(low, low_ref[...], NT).astype(dw1_ref.dtype)
        a1_ref[...] += dot(w1_ref[rows, :], low, TN)
        return 0

    lax.fori_loop(0, ff // block, back, 0)

    def first_back(cs):
        dy = a1_ref[:, cs]
        xh = xh_ref[:, cs]
        dr = norm_back(dy, xh, rs_ref[:, cs], vec(0))
        dr1_ref[:, cs] = dr
        dz = dr.astype(bf)
        low_ref[:, cs] = dz
        part_ref[3] += lane_fold(dy * xh)
        part_ref[4] += lane_fold(dy)
        part_ref[5] += lane_fold(dr)
        do_ref[:, cs] = dot(wo_ref[...], dz, TN).astype(bf)

    over_lanes(first_back)
    dwo_ref[...] = dot(low_ref[...], o_ref[...], NT).astype(dwo_ref.dtype)
    for n, i in enumerate((2, 3, 7, 0, 1, 6)):
        sg_ref[:, D * i : D * (i + 1)] = fold_row(part_ref[n])
    sg_ref[:, 4 * D : 6 * D] = jnp.zeros((1, 2 * D), f32)


def plain_backward_kernel(
    x_ref, seg_ref, w_ref, qkv_ref, o_ref, l_ref, do_ref, dr1_ref,
    dx_ref, dw_ref, db_ref,
    g_ref,
):
    t = x_ref.shape[0]
    q_rows, k_rows = segment_rows(seg_ref[...])

    def head(h, _):
        rows = rows_at(h, HD)
        krow = pl.ds(pl.multiple_of(D + h * HD, HD), HD)
        vrow = pl.ds(pl.multiple_of(2 * D + h * HD, HD), HD)
        q, k, v, do = qkv_ref[rows, :], qkv_ref[krow, :], qkv_ref[vrow, :], do_ref[rows, :]
        inner = jnp.sum(do.astype(f32) * o_ref[rows, :].astype(f32), axis=0, keepdims=True)
        s = dot(
            jnp.concatenate([k, k_rows], 0), jnp.concatenate([q * bf(0.125), q_rows], 0), TN
        )
        p = jnp.exp2((s - l_ref[h]) * LOG2E)
        dp = dot(v, do, TN)
        ds = (p * (dp - inner)).astype(bf)
        g_ref[vrow, :] = dot(do, p.astype(bf), NT).astype(bf)
        g_ref[krow, :] = (dot(q, ds, NT) * 0.125).astype(bf)
        g_ref[rows, :] = (dot(k, ds, NN) * 0.125).astype(bf)
        return 0

    lax.fori_loop(0, HEADS, head, 0)
    block = 256

    def weight_block(i, _):
        rows = rows_at(i, block)
        g = g_ref[rows, :]
        dw_ref[rows, :] = dot(g, x_ref[...], NN).astype(dw_ref.dtype)
        db_ref[:, rows] = fold_row(lane_fold(g.astype(f32)))
        return 0

    lax.fori_loop(0, 3 * D // block, weight_block, 0)

    def input_block(i, _):
        rows = rows_at(i, block)
        dx_ref[rows, :] = jnp.transpose(dr1_ref[:, rows]) + dot(g_ref[:, rows], w_ref[...], TN)
        return 0

    lax.fori_loop(0, t // block, input_block, 0)


def call(kernel, name, outs, scratch, *args):
    return pl.pallas_call(
        kernel,
        out_shape=[jax.ShapeDtypeStruct(s, d) for s, d in outs],
        scratch_shapes=[pltpu.VMEM(s, d) for s, d in scratch],
        compiler_params=pltpu.CompilerParams(vmem_limit_bytes=VMEM_LIMIT),
        name=name,
    )(*args)


def adam_step(weight, grad_sum, first_mom, second_mom, average, decay, rate):
    first_new = 0.9 * first_mom + 0.1 * grad_sum
    second_new = 0.98 * second_mom + 0.02 * grad_sum * grad_sum
    corrected = first_new / (1.0 - 0.9**STEP)
    denominator = jnp.sqrt(second_new / (1.0 - 0.98**STEP)) + 1e-06
    weight_new = weight - rate * (corrected / denominator + decay * weight)
    average_new = 0.75 * average + 0.25 * weight_new
    return (weight_new, first_new, second_new, average_new)


def gradients_general(features, cotangent, segment_ids, attn_weights, ffn_weights, small_params):
    axes = ("dp", "fsdp")
    t = features.shape[0]
    attn_full = lax.all_gather(attn_weights.astype(bf), axes, axis=0, tiled=True)
    ffn_full = lax.all_gather(ffn_weights.astype(bf), axes, axis=1, tiled=True)
    small_full = lax.all_gather(small_params.astype(bf), axes, axis=0, tiled=True)
    ff = ffn_full.shape[1]
    smalls = small_full.reshape(1, -1)
    seg = segment_ids.reshape(1, t)
    qkv, mixed, logs = call(
        plain_forward_kernel, "attend_forward",
        [((3 * D, t), bf), ((D, t), bf), ((HEADS, 1, t), f32)], [],
        features, seg, attn_full[: 3 * D], smalls,
    )
    outputs, dr1, do, dwo, dw1, dw2, small_grad = call(
        plain_middle_kernel, "plain_middle",
        [((t, D), bf), ((D, t), f32), ((D, t), bf), ((D, D), bf), ((ff, D), bf), ((ff, D), bf),
         ((1, smalls.shape[1]), f32)],
        [((D, t), f32), ((D, t), f32), ((ff, t), bf), ((ff, t), bf), ((1, t), f32), ((D, t), bf),
         ((D, t), bf), ((6, D, 128), f32), ((6, D, 128), f32)],
        features, mixed, cotangent, seg, attn_full[3 * D :], ffn_full[0], ffn_full[1], smalls,
    )
    input_grad, dqkv, bias_grad = call(
        plain_backward_kernel, "attend_backward",
        [((t, D), f32), ((3 * D, D), bf), ((1, 3 * D), f32)], [((3 * D, t), bf)],
        features, seg, attn_full[: 3 * D], qkv, mixed, logs, do, dr1,
    )
    small_grad = small_grad.reshape(-1)
    small_grad = jnp.concatenate(
        [small_grad[: 4 * D], bias_grad[0, :D], bias_grad[0, 2 * D :], small_grad[6 * D :]]
    )
    attn_sum, ffn_sum, small_sum = (
        lax.psum_scatter(jnp.concatenate([dqkv, dwo]), axes, scatter_dimension=0, tiled=True),
        lax.psum_scatter(jnp.stack([dw1, dw2]), axes, scatter_dimension=1, tiled=True),
        lax.psum_scatter(small_grad, axes, scatter_dimension=0, tiled=True),
    )
    return outputs, input_grad, attn_sum.astype(f32), ffn_sum.astype(f32), small_sum


MESH = pl.DeviceIdType.MESH
LAYERS = 4


class Place:
    def __init__(self):
        zy, xc = lax.axis_index("dp"), lax.axis_index("fsdp")
        self.z, self.y, self.x, self.c = zy // 2, zy % 2, xc // 2, xc % 2
        z, y, x, c = self.z, self.y, self.x, self.c
        self.n1 = (z * 2 + (y + c) % 2, ((x + 1 - c) % 2) * 2 + c)
        self.n2 = (z * 2 + (y + 1 - c) % 2, ((x + c) % 2) * 2 + c)
        self.sib = (z * 2 + y, x * 2 + 1 - c)
        self.n1_yx = ((y + c) % 2, (x + 1 - c) % 2)
        self.n2_yx = ((y + 1 - c) % 2, (x + c) % 2)
        self.far_yx = (1 - y, 1 - x)
        self.is_z = ((3 - z) // 3, (z % 2) * (1 - z // 2), ((z + 1) % 2) * (z // 2), z // 3)

    def pick(self, table):
        return sum(t * e for t, e in zip(table, self.is_z) if t)

    def at_layer(self, layer):
        return (layer * 2 + self.y, self.x * 2 + self.c)


def greet(peers):
    barrier = pltpu.get_barrier_semaphore()
    for peer in peers:
        pl.semaphore_signal(barrier, inc=1, device_id=peer, device_id_type=MESH)
    pl.semaphore_wait(barrier, len(peers))


class Gather:
    NEAR = ((0, 1, 2, 3), (1, 0, 1, 2), (2, 2, 3, 1), (3, 3, 0, 0))
    ONWARD = (None, (0, 2, 3, 0), (0, 0, 1, 0), (0, 0, 3, 0))

    def __init__(self, at, buf, send, recv):
        self.at, self.buf, self.send, self.recv = at, buf, send, recv
        self.layer = [at.pick(t) for t in self.NEAR]

    def copy(self, idx, src, dst, peer):
        ref = self.buf.at[idx]
        return pltpu.make_async_remote_copy(
            src_ref=ref, dst_ref=ref, send_sem=self.send.at[src], recv_sem=self.recv.at[dst],
            device_id=peer, device_id_type=MESH,
        )

    def mine(self, layer):
        return (layer, self.at.y, self.at.x, self.at.c)

    def up(self):
        at = self.at
        return self.copy(self.mine(at.z), 0, at.z, at.at_layer((at.z + 1) % LAYERS))

    def down(self):
        at = self.at
        return self.copy(self.mine(at.z), 1, at.z, at.at_layer((at.z + LAYERS - 1) % LAYERS))

    def onward(self, j):
        layer = self.layer[j]
        return self.copy(self.mine(layer), 1 + j, layer, self.at.at_layer(self.at.pick(self.ONWARD[j])))

    def first(self, j):
        layer = self.layer[j]
        return self.copy(self.mine(layer), 5 + j, 4 + layer, self.at.n1)

    def second(self, j):
        layer = self.layer[j]
        return self.copy(self.mine(layer), 9 + j, 8 + layer, self.at.n2)

    def third(self, j):
        layer = self.layer[j]
        return self.copy((layer,) + self.at.n1_yx + (self.at.c,), 13 + j, 12 + layer, self.at.n2)

    def across(self, j):
        layer = self.layer[j]
        return self.copy((layer, slice(None), slice(None), self.at.c), 17 + j, 16 + layer, self.at.sib)

    def arrived(self, idx, dst):
        self.copy(idx, 0, dst, self.at.sib).wait_recv()

    def start_z(self):
        pl.when(self.at.z < LAYERS - 1)(lambda: self.up().start())
        pl.when(self.at.z > 0)(lambda: self.down().start())

    def start_xy(self, j=0):
        self.first(j).start()
        self.second(j).start()

    def inner(self):
        return (self.at.z + 1) // 2 == 1

    def z_in(self, j):
        layer = self.layer[j]
        self.arrived(self.mine(layer), layer)
        pl.when(self.inner())(lambda: self.onward(j).start())

    def first_in(self, j):
        layer = self.layer[j]
        self.arrived((layer,) + self.at.n1_yx + (self.at.c,), 4 + layer)
        self.third(j).start()

    def second_in(self, j):
        layer = self.layer[j]
        self.arrived((layer,) + self.at.n2_yx + (self.at.c,), 8 + layer)
        self.arrived((layer,) + self.at.far_yx + (self.at.c,), 12 + layer)
        self.across(j).start()

    def done(self, j):
        layer = self.layer[j]
        self.arrived((layer, slice(None), slice(None), 1 - self.at.c), 16 + layer)

    def drain(self):
        pl.when(self.at.z < LAYERS - 1)(lambda: self.up().wait_send())
        pl.when(self.at.z > 0)(lambda: self.down().wait_send())
        for j in range(LAYERS):
            if j:
                pl.when(self.inner())(lambda j=j: self.onward(j).wait_send())
            for copy in (self.first, self.second, self.third, self.across):
                copy(j).wait_send()


def norm(r):
    centre = r - jnp.mean(r, axis=0, keepdims=True)
    scale = lax.rsqrt(jnp.mean(centre * centre, axis=0, keepdims=True) + 1e-5)
    return centre * scale, scale


def forward_kernel(
    x_ref, seg_ref, aw_ref, fw_ref, smw_ref,
    aout, fout, sm_ref, qkv_out, o_ref, l_ref, xh_out, rs_ref, low_ref, r2_ref, act_out, gp_out,
    abuf, fbuf, qkv_ref, xh_ref, act_ref, gp_ref, vec_ref, asend, arecv, fsend, frecv, local_sem,
):
    t = x_ref.shape[0]
    rows = aw_ref.shape[0]
    n_small = smw_ref.shape[1]
    at = Place()
    me = (at.z, at.y, at.x, at.c)
    abuf[me + (slice(0, rows),)] = aw_ref[...].astype(bf)
    small = jnp.concatenate([smw_ref[...], jnp.zeros((1, D - n_small), f32)], axis=1)
    abuf[me + (slice(rows, rows + 16),)] = jnp.broadcast_to(small, (16, D)).astype(bf)
    attn = Gather(at, abuf, asend, arecv)
    ffn = Gather(at, fbuf, fsend, frecv)
    up, down = at.at_layer((at.z + 1) % LAYERS), at.at_layer((at.z + LAYERS - 1) % LAYERS)
    greet([up, down, at.n1, at.n2, at.sib])
    attn.start_z()
    attn.start_xy()
    fbuf[me + (slice(0, rows),)] = fw_ref[0].astype(bf)
    fbuf[me + (slice(rows, 2 * rows),)] = fw_ref[1].astype(bf)

    def layer_in(g, j):
        g.z_in(j)
        g.start_xy(j)

    layer_in(attn, 1)
    attn.first_in(0)
    layer_in(attn, 2)
    attn.second_in(0)
    attn.first_in(1)
    layer_in(attn, 3)
    attn.done(0)
    ffn.start_z()
    attn.second_in(1)
    attn.first_in(2)
    attn.done(1)
    attn.second_in(2)
    attn.first_in(3)
    ffn.start_xy()
    attn.done(2)
    attn.second_in(3)
    layer_in(ffn, 1)
    attn.done(3)
    for i in range(32):
        z, y, x, c = i // 8, (i // 4) % 2, (i // 2) % 2, i % 2
        piece = abuf[z, y, x, c, rows : rows + 16, 0:n_small]
        sm_ref[:, n_small * i : n_small * (i + 1)] = piece[0:1].astype(f32)
    aout_copy = pltpu.make_async_copy(abuf, aout, local_sem.at[0])
    aout_copy.start()
    for sec in range(3):
        w = abuf[sec, :, :, :, 0:rows, :].reshape(D, D)
        p = dot(w, x_ref[...], NT)
        if sec != 1:
            o = (4 if sec == 0 else 5) * D
            p = p + widen(column(sm_ref[:, o : o + D]), t)
        qkv_ref[sec * D : (sec + 1) * D, :] = p.astype(bf)
    qkv_copy = pltpu.make_async_copy(qkv_ref, qkv_out, local_sem.at[1])
    qkv_copy.start()
    q_rows, k_rows = segment_rows(seg_ref[...])
    ticks = {
        2: [lambda: ffn.first_in(0)],
        3: [lambda: layer_in(ffn, 2)],
        4: [lambda: ffn.second_in(0)],
        5: [lambda: ffn.first_in(1), lambda: ffn.done(0)],
        7: [lambda: layer_in(ffn, 3)],
        8: [lambda: ffn.second_in(1)],
        10: [lambda: ffn.first_in(2), lambda: ffn.done(1)],
    }

    def head(h, _):
        for k, events in ticks.items():

            @pl.when(h == k)
            def _(events=events):
                for event in events:
                    event()

        r = rows_at(h, HD)
        q = qkv_ref[r, :] * bf(0.125)
        k = qkv_ref[pl.ds(pl.multiple_of(D + h * HD, HD), HD), :]
        v = qkv_ref[pl.ds(pl.multiple_of(2 * D + h * HD, HD), HD), :]
        s = dot(jnp.concatenate([k, k_rows], 0), jnp.concatenate([q, q_rows], 0), TN)
        top = jnp.max(s, axis=0, keepdims=True)
        e = jnp.exp2((s - top) * LOG2E)
        total = jnp.sum(e, axis=0, keepdims=True)
        o_ref[r, :] = (dot(v, e.astype(bf), NN) * (1.0 / total)).astype(bf)
        l_ref[h] = top + jnp.log(total)
        return 0

    lax.fori_loop(0, HEADS, head, 0)
    for n, i in enumerate((0, 1, 6, 7)):
        vec_ref[n] = column(sm_ref[:, D * i : D * (i + 1)])
    lanes = 256

    def first_norm(i, _):
        cs = rows_at(i, lanes)
        wo = abuf[3, :, :, :, 0:rows, :].reshape(D, D)
        vec = [widen(vec_ref[n], lanes) for n in range(4)]
        r1 = jnp.transpose(x_ref[cs, :]).astype(f32) + dot(wo, o_ref[:, cs], NN) + vec[2]
        xh, scale = norm(r1)
        xh_ref[:, cs] = xh
        rs_ref[:, cs] = scale
        a1 = xh * vec[0] + vec[1]
        r2_ref[:, cs] = a1 + vec[3]
        low_ref[:, cs] = a1.astype(bf)
        return 0

    lax.fori_loop(0, t // lanes, first_norm, 0)
    xh_copy = pltpu.make_async_copy(xh_ref, xh_out, local_sem.at[2])
    xh_copy.start()
    half = 4 * rows

    def write_back(j, y):
        slot = (2 * j + y) % 2
        where = pl.ds(pl.multiple_of(ffn.layer[j] * 2 * half + y * half, half), half)
        return [
            pltpu.make_async_copy(act_ref.at[slot], act_out.at[where], local_sem.at[3 + slot]),
            pltpu.make_async_copy(gp_ref.at[slot], gp_out.at[where], local_sem.at[5 + slot]),
        ]

    fout_copies = []
    for j in range(LAYERS):
        layer = ffn.layer[j]
        if j == 0:
            ffn.second_in(2)
            ffn.first_in(3)
        if j == 1:
            ffn.done(2)
        if j == 2:
            ffn.second_in(3)
        if j == 3:
            ffn.done(3)
        fout_copies.append(pltpu.make_async_copy(fbuf.at[layer], fout.at[layer], local_sem.at[7 + j]))
        fout_copies[-1].start()
        for y in range(2):
            slot = (2 * j + y) % 2
            w1 = fbuf[layer, y, :, :, 0:rows, :].reshape(half, D)
            w2 = fbuf[layer, y, :, :, rows : 2 * rows, :].reshape(half, D)
            bias = sm_ref[:, pl.ds(pl.multiple_of(8 * D + layer * 2 * half + y * half, 128), half)]
            hid = dot(w1, low_ref[...], NN) + widen(column(bias), t)
            act, slope = gelu_both(hid)
            act = act.astype(bf)
            if 2 * j + y >= 2:
                for copy in write_back((2 * j + y - 2) // 2, y):
                    copy.wait()
            act_ref[slot] = act
            gp_ref[slot] = slope.astype(bf)
            for copy in write_back(j, y):
                copy.start()
            r2_ref[...] += dot(w2, act, TN)
    for y in range(2):
        for copy in write_back(LAYERS - 1, y):
            copy.wait()
    attn.drain()
    ffn.drain()
    for copy in [aout_copy, qkv_copy, xh_copy] + fout_copies:
        copy.wait()


def forward_call(x, seg, aw, fw, smw):
    t, rows = x.shape[0], aw.shape[0]
    ff = 32 * rows
    n = 32 * smw.shape[1]
    vm, anyw = pl.BlockSpec(memory_space=pltpu.VMEM), pl.BlockSpec(memory_space=pl.ANY)
    shape = jax.ShapeDtypeStruct
    sems = pltpu.SemaphoreType.DMA
    return pl.pallas_call(
        forward_kernel,
        name="gather_forward",
        in_specs=[vm] * 5,
        out_specs=[anyw, anyw, vm, anyw, vm, vm, anyw, vm, vm, vm, anyw, anyw],
        out_shape=[
            shape((4, 2, 2, 2, rows + 16, D), bf), shape((4, 2, 2, 2, 2 * rows, D), bf), shape((1, n), f32),
            shape((3 * D, t), bf), shape((D, t), bf), shape((HEADS, 1, t), f32), shape((D, t), f32),
            shape((1, t), f32), shape((D, t), bf), shape((D, t), f32), shape((ff, t), bf), shape((ff, t), bf),
        ],
        scratch_shapes=[
            pltpu.VMEM((4, 2, 2, 2, rows + 16, D), bf), pltpu.VMEM((4, 2, 2, 2, 2 * rows, D), bf),
            pltpu.VMEM((3 * D, t), bf), pltpu.VMEM((D, t), f32), pltpu.VMEM((2, 4 * rows, t), bf),
            pltpu.VMEM((2, 4 * rows, t), bf), pltpu.VMEM((4, D, 128), f32),
            sems((21,)), sems((20,)), sems((21,)), sems((20,)), sems((11,)),
        ],
        compiler_params=pltpu.CompilerParams(
            vmem_limit_bytes=VMEM_LIMIT, collective_id=0, has_side_effects=True
        ),
    )(x, seg, aw, fw, smw)


def norm_back(dy, xh, scale, gain):
    dx = dy * gain
    mean_one = jnp.mean(dx, axis=0, keepdims=True)
    mean_two = jnp.mean(dx * xh, axis=0, keepdims=True)
    return scale * (dx - mean_one - xh * mean_two)


VECS = (0, 2, 3)


def middle_kernel(
    cot_ref, seg_ref, o_ref, xh_ref, rs_ref, low_ref, r2_ref, sm_ref, wo_ref, w_ref, act_ref, gp_ref,
    out_ref, dr1_ref, do_ref, dwo_ref, dw_ref, sg_ref,
    acc_ref, df_ref, vec_ref, part_ref,
):
    step = pl.program_id(0)
    t = cot_ref.shape[0]
    rows = w_ref.shape[4] // 2
    half = 4 * rows
    lanes = 256

    def vec(i):
        return widen(vec_ref[VECS.index(i)], lanes)

    def over_lanes(piece):
        def body(c, _):
            piece(rows_at(c, lanes))
            return 0

        lax.fori_loop(0, t // lanes, body, 0)

    @pl.when(step == 0)
    def _():
        for n, i in enumerate(VECS):
            vec_ref[n] = column(sm_ref[:, D * i : D * (i + 1)])
        part_ref[...] = jnp.zeros_like(part_ref)

        def second_norm(cs):
            xh, scale = norm(r2_ref[:, cs])
            out_ref[cs, :] = jnp.transpose((xh * vec(2) + vec(3)).astype(bf))
            valid = jnp.where(seg_ref[:, cs] >= 0, 1.0, 0.0)
            dy = jnp.transpose(cot_ref[cs, :]).astype(f32) * valid
            dr = norm_back(dy, xh, scale, vec(2))
            acc_ref[:, cs] = dr
            df_ref[:, cs] = dr.astype(bf)
            part_ref[0] += lane_fold(dy * xh)
            part_ref[1] += lane_fold(dy)
            part_ref[2] += lane_fold(dr)

        over_lanes(second_norm)

    w1 = w_ref[0, 0, :, :, 0:rows, :].reshape(half, D)
    w2 = w_ref[0, 0, :, :, rows : 2 * rows, :].reshape(half, D)
    dh = dot(w2, df_ref[...], NN) * gp_ref[...].astype(f32)
    sg_ref[:, pl.ds(pl.multiple_of(8 * D + step * half, 128), half)] = fold_row(lane_fold(dh))
    low = dh.astype(bf)
    dw2 = dot(act_ref[...], df_ref[...], NT).astype(bf)
    dw1 = dot(low, low_ref[...], NT).astype(bf)
    for x in range(2):
        for c in range(2):
            at = slice((2 * x + c) * rows, (2 * x + c + 1) * rows)
            dw_ref[0, 0, x, c, 0:rows, :] = dw1[at]
            dw_ref[0, 0, x, c, rows : 2 * rows, :] = dw2[at]
    acc_ref[...] += dot(w1, low, TN)

    @pl.when(step == pl.num_programs(0) - 1)
    def _():
        wo = wo_ref[0, :, :, :, 0:rows, :].reshape(D, D)

        def first_back(cs):
            dy = acc_ref[:, cs]
            xh = xh_ref[:, cs]
            dr = norm_back(dy, xh, rs_ref[:, cs], vec(0))
            dr1_ref[:, cs] = dr
            dz = dr.astype(bf)
            df_ref[:, cs] = dz
            part_ref[3] += lane_fold(dy * xh)
            part_ref[4] += lane_fold(dy)
            part_ref[5] += lane_fold(dr)
            do_ref[:, cs] = dot(wo, dz, TN).astype(bf)

        over_lanes(first_back)
        dwo_ref[...] = dot(df_ref[...], o_ref[...], NT).astype(bf)
        for n, i in enumerate((2, 3, 7, 0, 1, 6)):
            sg_ref[:, D * i : D * (i + 1)] = fold_row(part_ref[n])
        sg_ref[:, 4 * D : 6 * D] = jnp.zeros((1, 2 * D), f32)


def middle_call(cot, seg, o, xh, rs, low, r2, sm, abuf, fbuf, act, gp):
    t = cot.shape[0]
    rows = fbuf.shape[4] // 2
    half = 4 * rows
    shape = jax.ShapeDtypeStruct

    def whole(a):
        return pl.BlockSpec(a.shape, lambda j: (0,) * len(a.shape))

    wspec = pl.BlockSpec((1, 1, 2, 2, 2 * rows, D), lambda j: (j // 2, j % 2, 0, 0, 0, 0))
    rspec = pl.BlockSpec((half, t), lambda j: (j, 0))
    outs = [
        shape((t, D), bf), shape((D, t), f32), shape((D, t), bf), shape((D, D), bf), shape(fbuf.shape, bf),
        shape(sm.shape, f32),
    ]
    return pl.pallas_call(
        middle_kernel,
        name="middle",
        grid=(8,),
        in_specs=[whole(a) for a in (cot, seg, o, xh, rs, low, r2, sm)]
        + [pl.BlockSpec((1,) + abuf.shape[1:], lambda j: (3, 0, 0, 0, 0, 0)), wspec, rspec, rspec],
        out_specs=[whole(a) for a in outs[:4]] + [wspec, whole(outs[5])],
        out_shape=outs,
        scratch_shapes=[
            pltpu.VMEM((D, t), f32), pltpu.VMEM((D, t), bf), pltpu.VMEM((3, D, 128), f32),
            pltpu.VMEM((6, D, 128), f32),
        ],
        compiler_params=pltpu.CompilerParams(vmem_limit_bytes=VMEM_LIMIT),
    )(cot, seg, o, xh, rs, low, r2, sm, abuf, fbuf, act, gp)


class Scatter:
    def __init__(self, at, own, cross, pair, single, along, send, recv):
        self.at, self.own, self.cross, self.pair, self.single, self.along = at, own, cross, pair, single, along
        self.send, self.recv = send, recv
        self.p = (1 - at.c) * at.x + at.c * at.y

    def copy(self, src, dst, kind, layer, peer, land=None):
        land = layer if land is None else land
        return pltpu.make_async_remote_copy(
            src_ref=src, dst_ref=dst, send_sem=self.send.at[kind * LAYERS + layer],
            recv_sem=self.recv.at[kind * LAYERS + land], device_id=peer, device_id_type=MESH,
        )

    def across(self, layer, src):
        return self.copy(src, self.cross.at[layer], 0, layer, self.at.sib)

    def far(self, layer):
        return self.copy(
            self.own.at[(layer,) + self.at.far_yx], self.pair.at[layer, 1 - self.p], 1, layer, self.at.n2
        )

    def near(self, layer):
        return self.copy(self.own.at[(layer,) + self.at.n2_yx], self.pair.at[layer, self.p], 2, layer, self.at.n2)

    def first(self, layer):
        return self.copy(self.own.at[(layer,) + self.at.n1_yx], self.single.at[layer], 3, layer, self.at.n1)

    def to_layer(self, layer):
        return self.copy(
            self.own.at[layer, self.at.y, self.at.x], self.along.at[self.at.z], 4, layer,
            self.at.at_layer(layer), self.at.z,
        )

    def add(self, where, ref):
        self.own[where] = (self.own[where].astype(f32) + ref[...].astype(f32)).astype(bf)

    def cross_in(self, layer):
        self.across(layer, self.cross.at[layer]).wait_recv()
        for yx in (self.at.far_yx, self.at.n2_yx, self.at.n1_yx, (self.at.y, self.at.x)):
            self.add((layer,) + yx, self.cross.at[(layer,) + yx])
            if yx is self.at.far_yx:
                self.far(layer).start()
            if yx is self.at.n2_yx:
                self.near(layer).start()

    def pair_in(self, layer):
        self.far(layer).wait_recv()
        self.add((layer,) + self.at.n1_yx, self.pair.at[layer, 1 - self.p])
        self.first(layer).start()
        self.near(layer).wait_recv()
        self.add((layer, self.at.y, self.at.x), self.pair.at[layer, self.p])

    def single_in(self, layer):
        self.first(layer).wait_recv()
        self.add((layer, self.at.y, self.at.x), self.single.at[layer])
        pl.when(layer != self.at.z)(lambda: self.to_layer(layer).start())

    def finish(self):
        at = self.at
        total = self.own[at.z, at.y, at.x].astype(f32)
        for d in (1, 2, 3):
            layer = (at.z + d) % LAYERS
            self.copy(self.along.at[layer], self.along.at[layer], 4, layer, at.sib).wait_recv()
            total = total + self.along[layer].astype(f32)
        return total

    def drain(self, layer, src):
        self.across(layer, src).wait_send()
        self.far(layer).wait_send()
        self.near(layer).wait_send()
        self.first(layer).wait_send()
        pl.when(layer != self.at.z)(lambda: self.to_layer(layer).wait_send())


CQ = 512


def backward_kernel(
    x_ref, seg_ref, qkv_ref, o_ref, l_ref, do_ref, dwo_ref, sg_ref, dwf, abuf, dr1,
    dx, gf_ref, ga_ref,
    g_ref, dwa, w_ref, dr1_ref, dx_ref, small_ref,
    fown, fcross, fpair, fsingle, falong, across_ref, apair, asingle, aalong, aown,
    fsend, frecv, asend, arecv, local_sem,
):
    t = x_ref.shape[0]
    at = Place()
    rows = w_ref.shape[4]
    n_small = small_ref.shape[1] // 32
    z_layers = [(at.z + d) % LAYERS for d in range(LAYERS)]
    order = [z_layers[d] for d in (2, 1, 3, 0)]
    ffn = Scatter(at, fown, fcross, fpair, fsingle, falong, fsend, frecv)
    attn = Scatter(at, aown, across_ref, apair, asingle, aalong, asend, arecv)

    def ffn_src(layer):
        return dwf.at[layer, :, :, 1 - at.c]

    def attn_src(layer):
        return dwa.at[layer, :, :, 1 - at.c]

    loads = []
    for n, layer in enumerate(order):
        loads.append(pltpu.make_async_copy(dwf.at[layer, :, :, at.c], fown.at[layer], local_sem.at[n]))
        loads[-1].start()
    w_copy = pltpu.make_async_copy(abuf.at[0:3, :, :, :, 0:rows, :], w_ref, local_sem.at[4])
    w_copy.start()
    dr1_copy = pltpu.make_async_copy(dr1, dr1_ref, local_sem.at[5])
    dr1_copy.start()
    greet([at.at_layer(layer) for layer in z_layers[1:]] + [at.n1, at.n2, at.sib])
    for layer in order:
        ffn.across(layer, ffn_src(layer)).start()

    def small_rows(layer, y, x, c):
        i = layer * 8 + y * 4 + x * 2 + c
        piece = jnp.concatenate(
            [small_ref[:, i * n_small : (i + 1) * n_small], jnp.zeros((1, D - n_small), f32)], axis=1
        )
        return jnp.broadcast_to(piece, (16, D)).astype(bf)

    def fill(layer, dw):
        for y in range(2):
            for x in range(2):
                for c in range(2):
                    i = y * 4 + x * 2 + c
                    dwa[layer, y, x, c, 0:rows, :] = dw[i * rows : (i + 1) * rows]
                    dwa[layer, y, x, c, rows : rows + 16, :] = small_rows(layer, y, x, c)
        aown[layer] = dwa[layer, :, :, pl.ds(at.c, 1)].reshape(2, 2, rows + 16, D)
        attn.across(layer, attn_src(layer)).start()

    small_ref[...] = sg_ref[...]
    fill(3, dwo_ref[...])
    q_rows, k_rows = segment_rows(seg_ref[...])

    def ffn_cross(n):
        loads[n].wait()
        ffn.cross_in(order[n])

    ticks = {
        1: [lambda: ffn_cross(0)],
        2: [lambda: ffn_cross(1)],
        3: [lambda: ffn.pair_in(order[0]), lambda: ffn_cross(2)],
        4: [lambda: ffn_cross(3)],
        5: [lambda: ffn.single_in(order[0]), lambda: ffn.pair_in(order[1])],
        7: [lambda: ffn.single_in(order[1]), lambda: ffn.pair_in(order[2])],
        9: [lambda: ffn.single_in(order[2]), lambda: ffn.pair_in(order[3])],
        10: [lambda: attn.cross_in(3)],
        11: [lambda: ffn.single_in(order[3])],
    }

    def head(h, _):
        for k, events in ticks.items():

            @pl.when(h == k)
            def _(events=events):
                for event in events:
                    event()

        hrows = rows_at(h, HD)
        krow = pl.ds(pl.multiple_of(D + h * HD, HD), HD)
        vrow = pl.ds(pl.multiple_of(2 * D + h * HD, HD), HD)
        q, k, v, do = qkv_ref[hrows, :], qkv_ref[krow, :], qkv_ref[vrow, :], do_ref[hrows, :]
        inner = jnp.sum(do.astype(f32) * o_ref[hrows, :].astype(f32), axis=0, keepdims=True)
        lrow = l_ref[h]
        keys = jnp.concatenate([k, k_rows], 0)
        queries = jnp.concatenate([q * bf(0.125), q_rows], 0)
        dv = dk = 0.0
        for i in range(t // CQ):
            cs = slice(i * CQ, (i + 1) * CQ)
            s = dot(keys, queries[:, cs], TN)
            p = jnp.exp2((s - lrow[:, cs]) * LOG2E)
            dp = dot(v, do[:, cs], TN)
            ds = (p * (dp - inner[:, cs])).astype(bf)
            dv = dv + dot(do[:, cs], p.astype(bf), NT)
            dk = dk + dot(q[:, cs], ds, NT)
            g_ref[hrows, cs] = (dot(k, ds, NN) * 0.125).astype(bf)
        g_ref[vrow, :] = dv.astype(bf)
        g_ref[krow, :] = (dk * 0.125).astype(bf)
        return 0

    lax.fori_loop(0, HEADS, head, 0)
    for sec in (0, 2):
        part = lane_fold(g_ref[sec * D : (sec + 1) * D, :].astype(f32))
        o = (4 if sec == 0 else 5) * D
        small_ref[:, o : o + D] = fold_row(part)
    for layer in range(3):
        fill(layer, dot(g_ref[layer * D : (layer + 1) * D, :], x_ref[...], NN).astype(bf))
    attn.pair_in(3)
    for layer in range(3):
        attn.cross_in(layer)
    attn.single_in(3)
    w_copy.wait()
    dr1_copy.wait()
    lanes = 256

    def input_block(i, _):
        cs = rows_at(i, lanes)
        w = w_ref[...].reshape(3 * D, D)
        dx_ref[cs, :] = jnp.transpose(dr1_ref[:, cs]) + dot(g_ref[:, cs], w, TN)
        return 0

    lax.fori_loop(0, t // lanes, input_block, 0)
    dx_copy = pltpu.make_async_copy(dx_ref, dx, local_sem.at[6])
    dx_copy.start()
    gf_ref[...] = ffn.finish()
    for layer in range(3):
        attn.pair_in(layer)
    for layer in range(3):
        attn.single_in(layer)
    ga_ref[...] = attn.finish()
    for layer in range(LAYERS):
        ffn.drain(layer, ffn_src(layer))
        attn.drain(layer, attn_src(layer))
    dx_copy.wait()


def backward_call(x, seg, qkv, o, logs, do, dwo, sg, dwf, abuf, dr1):
    t = x.shape[0]
    ra, rf = abuf.shape[4], dwf.shape[4]
    vm, anyw = pl.BlockSpec(memory_space=pltpu.VMEM), pl.BlockSpec(memory_space=pl.ANY)
    shape = jax.ShapeDtypeStruct
    sems = pltpu.SemaphoreType.DMA

    def buffers(r):
        return [
            pltpu.VMEM((4, 2, 2, r, D), bf), pltpu.VMEM((4, 2, r, D), bf), pltpu.VMEM((4, r, D), bf),
            pltpu.VMEM((4, r, D), bf),
        ]

    return pl.pallas_call(
        backward_kernel,
        name="backward_scatter",
        in_specs=[vm] * 8 + [anyw] * 3,
        out_specs=[anyw, vm, vm],
        out_shape=[shape((t, D), f32), shape((rf, D), f32), shape((ra, D), f32)],
        scratch_shapes=[
            pltpu.VMEM((3 * D, t), bf), pltpu.VMEM(abuf.shape, bf), pltpu.VMEM((3, 2, 2, 2, ra - 16, D), bf),
            pltpu.VMEM((D, t), f32), pltpu.VMEM((t, D), f32), pltpu.VMEM(sg.shape, f32),
            pltpu.VMEM((4, 2, 2, rf, D), bf),
        ]
        + buffers(rf)
        + buffers(ra)
        + [pltpu.VMEM((4, 2, 2, ra, D), bf), sems((20,)), sems((20,)), sems((20,)), sems((20,)), sems((7,))],
        compiler_params=pltpu.CompilerParams(
            vmem_limit_bytes=VMEM_LIMIT, collective_id=1, has_side_effects=True
        ),
    )(x, seg, qkv, o, logs, do, dwo, sg, dwf, abuf, dr1)


def gradients_block(features, cotangent, segment_ids, attn_weights, ffn_weights, small_params):
    t, rows = features.shape[0], attn_weights.shape[0]
    seg = segment_ids.reshape(1, t)
    abuf, fbuf, sm, qkv, o, logs, xh, rs, low, r2, act, gp = forward_call(
        features, seg, attn_weights, ffn_weights, small_params.reshape(1, -1)
    )
    outputs, dr1, do, dwo, dwf, sg = middle_call(cotangent, seg, o, xh, rs, low, r2, sm, abuf, fbuf, act, gp)
    input_grad, gf, ga = backward_call(features, seg, qkv, o, logs, do, dwo, sg, dwf, abuf, dr1)
    small_sum = ga[rows, : small_params.shape[0]]
    return outputs, input_grad, ga[:rows], gf.reshape(2, rows, D), small_sum


def local(
    gradients,
    features, cotangent, segment_ids, attn_weights, ffn_weights, small_params,
    attn_first, ffn_first, small_first, attn_second, ffn_second, small_second,
    attn_ema, ffn_ema, small_ema,
):
    outputs, input_grad, attn_sum, ffn_sum, small_sum = gradients(
        features, cotangent, segment_ids, attn_weights, ffn_weights, small_params
    )
    attn = adam_step(attn_weights, attn_sum, attn_first, attn_second, attn_ema, 0.01, 0.05)
    ffn = adam_step(ffn_weights, ffn_sum, ffn_first, ffn_second, ffn_ema, 0.01, 0.05)
    small = adam_step(small_params, small_sum, small_first, small_second, small_ema, 0.0, 0.3)
    return (outputs, input_grad) + tuple(x for trio in zip(attn, ffn, small) for x in trio)


def solution(mesh):
    block = mesh.shape["dp"] == 8 and mesh.shape["fsdp"] == 4
    gradients = gradients_block if block else gradients_general
    row = P(("dp", "fsdp"), None)
    wide = P(None, ("dp", "fsdp"), None)
    flat = P(("dp", "fsdp"))
    state = (row, wide, flat)
    return jax.shard_map(
        partial(local, gradients),
        mesh=mesh,
        in_specs=(row, row, flat) + state * 4,
        out_specs=(row, row) + state * 4,
        check_vma=False,
    )
```

```python
from functools import partial

import jax
import jax.numpy as jnp
from jax import lax
from jax.experimental import pallas as pl
from jax.experimental.pallas import tpu as pltpu
from jax.sharding import PartitionSpec as P

D = 768
HEADS = 12
HD = D // HEADS
STEP = 10
LOG2E = 1.4426950408889634
INV_SQRT2 = 0.7071067811865476
INV_SQRT2PI = 0.3989422804014327
BIG = 2.0**30
VMEM_LIMIT = 60 * 1024 * 1024

bf = jnp.bfloat16
f32 = jnp.float32
TN = (((0,), (0,)), ((), ()))
NN = (((1,), (0,)), ((), ()))
NT = (((1,), (1,)), ((), ()))


def dot(left, right, dims):
    return lax.dot_general(left, right, dims, preferred_element_type=f32)


def rows_at(i, size):
    return pl.ds(pl.multiple_of(i * size, size), size)


def column(row):
    return jnp.transpose(jnp.broadcast_to(row, (128, row.shape[1])))


def widen(col, width):
    return jnp.concatenate([col] * (width // 128), axis=1) if width > 128 else col


def lane_fold(x):
    total = x[:, :128]
    for i in range(1, x.shape[1] // 128):
        total = total + x[:, 128 * i : 128 * (i + 1)]
    return total


def fold_row(part):
    return jnp.sum(jnp.transpose(part), axis=0, keepdims=True)


def segment_rows(seg):
    ids = lax.broadcasted_iota(jnp.int32, (16, seg.shape[1]), 0) - 1
    same = jnp.where(ids == seg, 1.0, 0.0)
    return ((same - 1.0) * BIG).astype(bf), same.astype(bf)


def plain_forward_kernel(x_ref, seg_ref, w_ref, sm_ref, qkv_ref, o_ref, l_ref):
    t = x_ref.shape[0]
    block = 256

    def project_block(i, _):
        rows = rows_at(i, block)
        sec = i // (D // block)
        off = i - sec * (D // block)
        bias = sm_ref[:, pl.ds(pl.multiple_of((4 + sec // 2) * D + off * block, block), block)]
        keep = jnp.where(sec == 1, 0.0, 1.0)
        col = column(bias.astype(f32) * keep)
        qkv_ref[rows, :] = (dot(w_ref[rows, :], x_ref[...], NT) + widen(col, t)).astype(bf)
        return 0

    lax.fori_loop(0, 3 * D // block, project_block, 0)
    q_rows, k_rows = segment_rows(seg_ref[...])

    def head(h, _):
        rows = rows_at(h, HD)
        q = qkv_ref[rows, :] * bf(0.125)
        k = qkv_ref[pl.ds(pl.multiple_of(D + h * HD, HD), HD), :]
        v = qkv_ref[pl.ds(pl.multiple_of(2 * D + h * HD, HD), HD), :]
        s = dot(jnp.concatenate([k, k_rows], 0), jnp.concatenate([q, q_rows], 0), TN)
        top = jnp.max(s, axis=0, keepdims=True)
        e = jnp.exp2((s - top) * LOG2E)
        total = jnp.sum(e, axis=0, keepdims=True)
        o_ref[rows, :] = (dot(v, e.astype(bf), NN) * (1.0 / total)).astype(bf)
        l_ref[h] = top + jnp.log(total)
        return 0

    lax.fori_loop(0, HEADS, head, 0)


def gelu_both(h):
    cdf = 0.5 + 0.5 * lax.erf(h * INV_SQRT2)
    pdf = jnp.exp(h * h * -0.5) * INV_SQRT2PI
    return h * cdf, cdf + h * pdf


PLAIN_VECS = (0, 1, 2, 3, 6, 7)


def plain_middle_kernel(
    x_ref, o_ref, cot_ref, seg_ref, wo_ref, w1_ref, w2_ref, sm_ref,
    out_ref, dr1_ref, do_ref, dwo_ref, dw1_ref, dw2_ref, sg_ref,
    a1_ref, xh_ref, act_ref, gp_ref, rs_ref, low_ref, df_ref, vec_ref, part_ref,
):
    t = x_ref.shape[0]
    ff = w1_ref.shape[0]
    block, lanes = 256, 256
    for n, i in enumerate(PLAIN_VECS):
        vec_ref[n] = column(sm_ref[:, D * i : D * (i + 1)].astype(f32))
    part_ref[...] = jnp.zeros_like(part_ref)

    def vec(i):
        return widen(vec_ref[PLAIN_VECS.index(i)], lanes)

    def over_lanes(step):
        def body(c, _):
            step(rows_at(c, lanes))
            return 0

        lax.fori_loop(0, t // lanes, body, 0)

    def norm(r):
        centre = r - jnp.mean(r, axis=0, keepdims=True)
        scale = lax.rsqrt(jnp.mean(centre * centre, axis=0, keepdims=True) + 1e-5)
        return centre * scale, scale

    def norm_back(dy, xh, scale, gain):
        dx = dy * gain
        mean_one = jnp.mean(dx, axis=0, keepdims=True)
        mean_two = jnp.mean(dx * xh, axis=0, keepdims=True)
        return scale * (dx - mean_one - xh * mean_two)

    def first_norm(cs):
        r1 = jnp.transpose(x_ref[cs, :]).astype(f32) + dot(wo_ref[...], o_ref[:, cs], NN) + vec(6)
        xh, scale = norm(r1)
        xh_ref[:, cs] = xh
        rs_ref[:, cs] = scale
        a1 = xh * vec(0) + vec(1)
        a1_ref[:, cs] = a1 + vec(7)
        low_ref[:, cs] = a1.astype(bf)

    over_lanes(first_norm)

    def up_down(j, _):
        rows = rows_at(j, block)
        bias = sm_ref[:, pl.ds(pl.multiple_of(8 * D + j * block, block), block)]
        hid = dot(w1_ref[rows, :], low_ref[...], NN) + widen(column(bias.astype(f32)), t)
        act, slope = gelu_both(hid)
        act = act.astype(bf)
        act_ref[rows, :] = act
        gp_ref[rows, :] = slope.astype(gp_ref.dtype)
        a1_ref[...] += dot(w2_ref[rows, :], act, TN)
        return 0

    lax.fori_loop(0, ff // block, up_down, 0)

    def second_norm(cs):
        xh, scale = norm(a1_ref[:, cs])
        out_ref[cs, :] = jnp.transpose((xh * vec(2) + vec(3)).astype(bf))
        valid = jnp.where(seg_ref[:, cs] >= 0, 1.0, 0.0)
        dy = jnp.transpose(cot_ref[cs, :]).astype(f32) * valid
        dr = norm_back(dy, xh, scale, vec(2))
        a1_ref[:, cs] = dr
        df_ref[:, cs] = dr.astype(bf)
        part_ref[0] += lane_fold(dy * xh)
        part_ref[1] += lane_fold(dy)
        part_ref[2] += lane_fold(dr)

    over_lanes(second_norm)

    def back(j, _):
        rows = rows_at(j, block)
        dh = dot(w2_ref[rows, :], df_ref[...], NN) * gp_ref[rows, :].astype(f32)
        sg_ref[:, pl.ds(pl.multiple_of(8 * D + j * block, block), block)] = fold_row(lane_fold(dh))
        low = dh.astype(bf)
        dw2_ref[rows, :] = dot(act_ref[rows, :], df_ref[...], NT).astype(dw2_ref.dtype)
        dw1_ref[rows, :] = dot(low, low_ref[...], NT).astype(dw1_ref.dtype)
        a1_ref[...] += dot(w1_ref[rows, :], low, TN)
        return 0

    lax.fori_loop(0, ff // block, back, 0)

    def first_back(cs):
        dy = a1_ref[:, cs]
        xh = xh_ref[:, cs]
        dr = norm_back(dy, xh, rs_ref[:, cs], vec(0))
        dr1_ref[:, cs] = dr
        dz = dr.astype(bf)
        low_ref[:, cs] = dz
        part_ref[3] += lane_fold(dy * xh)
        part_ref[4] += lane_fold(dy)
        part_ref[5] += lane_fold(dr)
        do_ref[:, cs] = dot(wo_ref[...], dz, TN).astype(bf)

    over_lanes(first_back)
    dwo_ref[...] = dot(low_ref[...], o_ref[...], NT).astype(dwo_ref.dtype)
    for n, i in enumerate((2, 3, 7, 0, 1, 6)):
        sg_ref[:, D * i : D * (i + 1)] = fold_row(part_ref[n])
    sg_ref[:, 4 * D : 6 * D] = jnp.zeros((1, 2 * D), f32)


def plain_backward_kernel(
    x_ref, seg_ref, w_ref, qkv_ref, o_ref, l_ref, do_ref, dr1_ref,
    dx_ref, dw_ref, db_ref,
    g_ref,
):
    t = x_ref.shape[0]
    q_rows, k_rows = segment_rows(seg_ref[...])

    def head(h, _):
        rows = rows_at(h, HD)
        krow = pl.ds(pl.multiple_of(D + h * HD, HD), HD)
        vrow = pl.ds(pl.multiple_of(2 * D + h * HD, HD), HD)
        q, k, v, do = qkv_ref[rows, :], qkv_ref[krow, :], qkv_ref[vrow, :], do_ref[rows, :]
        inner = jnp.sum(do.astype(f32) * o_ref[rows, :].astype(f32), axis=0, keepdims=True)
        s = dot(
            jnp.concatenate([k, k_rows], 0), jnp.concatenate([q * bf(0.125), q_rows], 0), TN
        )
        p = jnp.exp2((s - l_ref[h]) * LOG2E)
        dp = dot(v, do, TN)
        ds = (p * (dp - inner)).astype(bf)
        g_ref[vrow, :] = dot(do, p.astype(bf), NT).astype(bf)
        g_ref[krow, :] = (dot(q, ds, NT) * 0.125).astype(bf)
        g_ref[rows, :] = (dot(k, ds, NN) * 0.125).astype(bf)
        return 0

    lax.fori_loop(0, HEADS, head, 0)
    block = 256

    def weight_block(i, _):
        rows = rows_at(i, block)
        g = g_ref[rows, :]
        dw_ref[rows, :] = dot(g, x_ref[...], NN).astype(dw_ref.dtype)
        db_ref[:, rows] = fold_row(lane_fold(g.astype(f32)))
        return 0

    lax.fori_loop(0, 3 * D // block, weight_block, 0)

    def input_block(i, _):
        rows = rows_at(i, block)
        dx_ref[rows, :] = jnp.transpose(dr1_ref[:, rows]) + dot(g_ref[:, rows], w_ref[...], TN)
        return 0

    lax.fori_loop(0, t // block, input_block, 0)


def call(kernel, name, outs, scratch, *args):
    return pl.pallas_call(
        kernel,
        out_shape=[jax.ShapeDtypeStruct(s, d) for s, d in outs],
        scratch_shapes=[pltpu.VMEM(s, d) for s, d in scratch],
        compiler_params=pltpu.CompilerParams(vmem_limit_bytes=VMEM_LIMIT),
        name=name,
    )(*args)


def adam_step(weight, grad_sum, first_mom, second_mom, average, decay, rate):
    first_new = 0.9 * first_mom + 0.1 * grad_sum
    second_new = 0.98 * second_mom + 0.02 * grad_sum * grad_sum
    corrected = first_new / (1.0 - 0.9**STEP)
    denominator = jnp.sqrt(second_new / (1.0 - 0.98**STEP)) + 1e-06
    weight_new = weight - rate * (corrected / denominator + decay * weight)
    average_new = 0.75 * average + 0.25 * weight_new
    return (weight_new, first_new, second_new, average_new)


def gradients_general(features, cotangent, segment_ids, attn_weights, ffn_weights, small_params):
    axes = ("dp", "fsdp")
    t = features.shape[0]
    attn_full = lax.all_gather(attn_weights.astype(bf), axes, axis=0, tiled=True)
    ffn_full = lax.all_gather(ffn_weights.astype(bf), axes, axis=1, tiled=True)
    small_full = lax.all_gather(small_params.astype(bf), axes, axis=0, tiled=True)
    ff = ffn_full.shape[1]
    smalls = small_full.reshape(1, -1)
    seg = segment_ids.reshape(1, t)
    qkv, mixed, logs = call(
        plain_forward_kernel, "attend_forward",
        [((3 * D, t), bf), ((D, t), bf), ((HEADS, 1, t), f32)], [],
        features, seg, attn_full[: 3 * D], smalls,
    )
    outputs, dr1, do, dwo, dw1, dw2, small_grad = call(
        plain_middle_kernel, "plain_middle",
        [((t, D), bf), ((D, t), f32), ((D, t), bf), ((D, D), bf), ((ff, D), bf), ((ff, D), bf),
         ((1, smalls.shape[1]), f32)],
        [((D, t), f32), ((D, t), f32), ((ff, t), bf), ((ff, t), bf), ((1, t), f32), ((D, t), bf),
         ((D, t), bf), ((6, D, 128), f32), ((6, D, 128), f32)],
        features, mixed, cotangent, seg, attn_full[3 * D :], ffn_full[0], ffn_full[1], smalls,
    )
    input_grad, dqkv, bias_grad = call(
        plain_backward_kernel, "attend_backward",
        [((t, D), f32), ((3 * D, D), bf), ((1, 3 * D), f32)], [((3 * D, t), bf)],
        features, seg, attn_full[: 3 * D], qkv, mixed, logs, do, dr1,
    )
    small_grad = small_grad.reshape(-1)
    small_grad = jnp.concatenate(
        [small_grad[: 4 * D], bias_grad[0, :D], bias_grad[0, 2 * D :], small_grad[6 * D :]]
    )
    attn_sum, ffn_sum, small_sum = (
        lax.psum_scatter(jnp.concatenate([dqkv, dwo]), axes, scatter_dimension=0, tiled=True),
        lax.psum_scatter(jnp.stack([dw1, dw2]), axes, scatter_dimension=1, tiled=True),
        lax.psum_scatter(small_grad, axes, scatter_dimension=0, tiled=True),
    )
    return outputs, input_grad, attn_sum.astype(f32), ffn_sum.astype(f32), small_sum


MESH = pl.DeviceIdType.MESH
LAYERS = 4


class Place:
    def __init__(self):
        zy, xc = lax.axis_index("dp"), lax.axis_index("fsdp")
        self.z, self.y, self.x, self.c = zy // 2, zy % 2, xc // 2, xc % 2
        z, y, x, c = self.z, self.y, self.x, self.c
        self.n1 = (z * 2 + (y + c) % 2, ((x + 1 - c) % 2) * 2 + c)
        self.n2 = (z * 2 + (y + 1 - c) % 2, ((x + c) % 2) * 2 + c)
        self.sib = (z * 2 + y, x * 2 + 1 - c)
        self.n1_yx = ((y + c) % 2, (x + 1 - c) % 2)
        self.n2_yx = ((y + 1 - c) % 2, (x + c) % 2)
        self.far_yx = (1 - y, 1 - x)
        self.is_z = ((3 - z) // 3, (z % 2) * (1 - z // 2), ((z + 1) % 2) * (z // 2), z // 3)

    def pick(self, table):
        return sum(t * e for t, e in zip(table, self.is_z) if t)

    def at_layer(self, layer):
        return (layer * 2 + self.y, self.x * 2 + self.c)


def greet(peers):
    barrier = pltpu.get_barrier_semaphore()
    for peer in peers:
        pl.semaphore_signal(barrier, inc=1, device_id=peer, device_id_type=MESH)
    pl.semaphore_wait(barrier, len(peers))


def remote(src, dst, send, recv, peer):
    return pltpu.make_async_remote_copy(
        src_ref=src, dst_ref=dst, send_sem=send, recv_sem=recv, device_id=peer, device_id_type=MESH
    )


class Gather:
    NEAR = ((0, 1, 2, 3), (1, 0, 1, 2), (2, 2, 3, 1), (3, 3, 0, 0))
    ONWARD = (None, (0, 2, 3, 0), (0, 0, 1, 0), (0, 0, 3, 0))

    def __init__(self, at, buf, send, recv):
        self.at, self.buf, self.send, self.recv = at, buf, send, recv
        self.layer = [at.pick(t) for t in self.NEAR]
        self.columns = [(at.y, at.x), at.n1_yx, at.n2_yx, at.far_yx]

    def copy(self, idx, src, dst, peer):
        ref = self.buf.at[idx]
        return remote(ref, ref, self.send.at[src], self.recv.at[dst], peer)

    def slot(self, layer, column):
        return (layer,) + self.columns[column] + (self.at.c,)

    def up(self, column):
        at = self.at
        return self.copy(self.slot(at.z, column), column, 4 * column + at.z, at.at_layer((at.z + 1) % LAYERS))

    def down(self, column):
        at = self.at
        return self.copy(
            self.slot(at.z, column), 2 + column, 4 * column + at.z, at.at_layer((at.z + LAYERS - 1) % LAYERS)
        )

    def onward(self, j, column):
        layer = self.layer[j]
        return self.copy(
            self.slot(layer, column), 3 + j + 3 * column, 4 * column + layer,
            self.at.at_layer(self.at.pick(self.ONWARD[j])),
        )

    def first(self):
        return self.copy(self.slot(self.at.z, 0), 10, 4 + self.at.z, self.at.n1)

    def second(self, j, column):
        layer = self.layer[j]
        return self.copy(self.slot(layer, column), 11 + 4 * column + j, 8 + 4 * column + layer, self.at.n2)

    def across(self, j):
        layer = self.layer[j]
        return self.copy((layer, slice(None), slice(None), self.at.c), 19 + j, 16 + layer, self.at.sib)

    def arrived(self, idx, dst):
        self.copy(idx, 0, dst, self.at.sib).wait_recv()

    def spread(self, column):
        pl.when(self.at.z < LAYERS - 1)(lambda: self.up(column).start())
        pl.when(self.at.z > 0)(lambda: self.down(column).start())
        self.second(0, column).start()

    def start(self):
        self.first().start()
        self.spread(0)

    def inner(self):
        return (self.at.z + 1) // 2 == 1

    def first_in(self):
        self.arrived(self.slot(self.at.z, 1), 4 + self.at.z)
        self.spread(1)

    def z_in(self, j, column):
        layer = self.layer[j]
        self.arrived(self.slot(layer, column), 4 * column + layer)
        pl.when(self.inner())(lambda: self.onward(j, column).start())
        self.second(j, column).start()

    def second_in(self, j):
        layer = self.layer[j]
        self.arrived(self.slot(layer, 2), 8 + layer)
        self.arrived(self.slot(layer, 3), 12 + layer)
        self.across(j).start()

    def done(self, j):
        layer = self.layer[j]
        self.arrived((layer, slice(None), slice(None), 1 - self.at.c), 16 + layer)

    def drain(self):
        self.first().wait_send()
        for n in range(2):
            pl.when(self.at.z < LAYERS - 1)(lambda n=n: self.up(n).wait_send())
            pl.when(self.at.z > 0)(lambda n=n: self.down(n).wait_send())
            for j in range(1, LAYERS):
                pl.when(self.inner())(lambda j=j, n=n: self.onward(j, n).wait_send())
            for j in range(LAYERS):
                self.second(j, n).wait_send()
        for j in range(LAYERS):
            self.across(j).wait_send()


class ColumnGather:
    NEAR = ((0, 1, 2, 2), (1, 0, 1, 1), (2, 2, 0, 0))

    def __init__(self, at, buf, send, recv):
        self.at, self.buf, self.send, self.recv = at, buf, send, recv
        self.near = [at.pick(t) for t in self.NEAR]
        self.columns = [(at.y, at.x), at.n1_yx, at.n2_yx, at.far_yx]

    def copy(self, idx, src, dst, peer):
        ref = self.buf.at[idx]
        return pltpu.make_async_remote_copy(
            src_ref=ref, dst_ref=ref, send_sem=self.send.at[src], recv_sem=self.recv.at[dst],
            device_id=peer, device_id_type=MESH,
        )

    def slot(self, layer, column, core=None):
        return (layer,) + self.columns[column] + (self.at.c if core is None else core,)

    def up(self, layer):
        return self.copy(self.slot(layer, 0), layer, layer, self.at.at_layer((self.at.z + 1) % LAYERS))

    def down(self, layer):
        return self.copy(
            self.slot(layer, 0), 4 + layer, layer, self.at.at_layer((self.at.z + LAYERS - 1) % LAYERS)
        )

    def first(self, layer):
        return self.copy(self.slot(layer, 0), 8 + layer, 4 + layer, self.at.n1)

    def second(self, layer):
        return self.copy(self.slot(layer, 0), 12 + layer, 8 + layer, self.at.n2)

    def third(self, layer):
        return self.copy(self.slot(layer, 1), 16 + layer, 12 + layer, self.at.n2)

    def own(self, layer):
        return self.copy(self.slot(layer, 0), 20 + layer, 16 + layer, self.at.sib)

    def across(self, column):
        y, x = self.columns[column]
        return self.copy((slice(0, 3), y, x, self.at.c), 23 + column, 20 + 2 * y + x, self.at.sib)

    def across_last(self):
        return self.copy((3, slice(None), slice(None), self.at.c), 23, 19, self.at.sib)

    def arrived(self, idx, dst):
        self.copy(idx, 0, dst, self.at.sib).wait_recv()

    def goes_up(self, layer):
        return jnp.logical_and(self.at.z >= layer, self.at.z < LAYERS - 1)

    def goes_down(self, layer):
        return jnp.logical_and(self.at.z <= layer, self.at.z > 0)

    def along(self, layer):
        pl.when(self.goes_up(layer))(lambda: self.up(layer).start())
        pl.when(self.goes_down(layer))(lambda: self.down(layer).start())

    def spread(self, layer):
        self.own(layer).start()
        self.first(layer).start()
        self.second(layer).start()

    def z_in(self, layer):
        self.arrived(self.slot(layer, 0), layer)

    def first_in(self, layer):
        self.arrived(self.slot(layer, 1), 4 + layer)
        self.third(layer).start()

    def second_in(self, layer):
        self.arrived(self.slot(layer, 2), 8 + layer)

    def third_in(self, layer):
        self.arrived(self.slot(layer, 3), 12 + layer)

    def own_in(self, layer):
        self.arrived(self.slot(layer, 0, 1 - self.at.c), 16 + layer)

    def across_in(self, column):
        y, x = self.columns[column]
        self.arrived((slice(0, 3), y, x, 1 - self.at.c), 20 + 2 * y + x)

    def last_in(self):
        self.arrived((3, slice(None), slice(None), 1 - self.at.c), 19)

    def drain(self):
        for layer in range(LAYERS):
            pl.when(self.goes_up(layer))(lambda layer=layer: self.up(layer).wait_send())
            pl.when(self.goes_down(layer))(lambda layer=layer: self.down(layer).wait_send())
            self.first(layer).wait_send()
            self.second(layer).wait_send()
            self.third(layer).wait_send()
        for n in range(3):
            self.own(n).wait_send()
            self.across(n + 1).wait_send()
        self.across_last().wait_send()


class SmallGather:
    def __init__(self, at, buf, send, recv):
        self.at, self.buf, self.send, self.recv = at, buf, send, recv

    def copy(self, idx, src, dst, peer):
        ref = self.buf.at[idx]
        return pltpu.make_async_remote_copy(
            src_ref=ref, dst_ref=ref, send_sem=self.send.at[src], recv_sem=self.recv.at[dst],
            device_id=peer, device_id_type=MESH,
        )

    def along(self, d):
        at = self.at
        return self.copy((at.z, at.y, at.x, at.c), d - 1, d - 1, at.at_layer((at.z + d) % LAYERS))

    def first(self):
        return self.copy((slice(None), self.at.y, self.at.x, self.at.c), 3, 3, self.at.n1)

    def second(self):
        return self.copy((slice(None), self.at.y, self.at.x, self.at.c), 4, 4, self.at.n2)

    def third(self):
        return self.copy((slice(None),) + self.at.n1_yx + (self.at.c,), 5, 5, self.at.n2)

    def across(self):
        return self.copy((slice(None), slice(None), slice(None), self.at.c), 6, 6, self.at.sib)

    def start(self):
        for d in (1, 2, 3):
            self.along(d).start()

    def spread(self):
        for d in (1, 2, 3):
            self.along(d).wait_recv()
        self.first().start()
        self.second().start()

    def forward(self):
        self.first().wait_recv()
        self.third().start()

    def cross(self):
        self.second().wait_recv()
        self.third().wait_recv()
        self.across().start()

    def done(self):
        self.across().wait_recv()

    def drain(self):
        for d in (1, 2, 3):
            self.along(d).wait_send()
        for copy in (self.first, self.second, self.third, self.across):
            copy().wait_send()


def norm(r):
    centre = r - jnp.mean(r, axis=0, keepdims=True)
    scale = lax.rsqrt(jnp.mean(centre * centre, axis=0, keepdims=True) + 1e-5)
    return centre * scale, scale


def forward_kernel(
    seg_ref, aw_ref, smw_ref, x, fw,
    aout, fout, sm_ref, qkv_out, o_out, l_ref, xh_out, rs_ref, low_out, r2_out, act_out, gp_out,
    abuf, fbuf, sbuf, qkv_ref, xh_ref, act_ref, gp_ref, vec_ref, bias_ref, x_ref, fw_ref, o_ref, low_ref, r2_ref,
    asend, arecv, fsend, frecv, ssend, srecv, local_sem,
):
    t = x_ref.shape[0]
    rows = aw_ref.shape[0]
    n_small = smw_ref.shape[1]
    at = Place()
    me = (at.z, at.y, at.x, at.c)
    fw_copy = pltpu.make_async_copy(fw, fw_ref, local_sem.at[11])
    fw_copy.start()
    x_copy = pltpu.make_async_copy(x, x_ref, local_sem.at[12])
    x_copy.start()
    abuf[me] = aw_ref[...].astype(bf)
    pad = jnp.zeros((1, sbuf.shape[-1] - n_small), f32)
    sbuf[me] = jnp.concatenate([smw_ref[...], pad], axis=1)
    attn = ColumnGather(at, abuf, asend, arecv)
    ffn = Gather(at, fbuf, fsend, frecv)
    small = SmallGather(at, sbuf, ssend, srecv)
    near = attn.near
    greet([at.at_layer((at.z + d) % LAYERS) for d in (1, 2, 3)] + [at.n1, at.n2, at.sib])
    pl.when(at.z == 3)(lambda: attn.along(3))
    small.start()
    pl.when(at.z == 3)(lambda: attn.z_in(2))
    attn.along(near[0])
    attn.spread(near[0])
    fw_copy.wait()
    fbuf[me + (slice(0, rows),)] = fw_ref[0].astype(bf)
    fbuf[me + (slice(rows, 2 * rows),)] = fw_ref[1].astype(bf)
    small.spread()
    small.forward()
    attn.z_in(near[1])
    attn.along(near[1])
    attn.spread(near[1])
    attn.first_in(near[0])
    pl.when(at.z == 2)(lambda: attn.z_in(3))
    pl.when(at.z == 2)(lambda: attn.along(3))
    small.cross()
    attn.z_in(near[2])
    attn.along(near[2])
    attn.spread(near[2])
    attn.first_in(near[1])
    pl.when(at.z == 1)(lambda: attn.z_in(3))
    pl.when(at.z == 1)(lambda: attn.along(3))
    small.done()
    for i in range(32):
        z, y, x, c = i // 8, (i // 4) % 2, (i // 2) % 2, i % 2
        piece = sbuf[z, y, x, c]
        sm_ref[:, n_small * i : n_small * (i + 1)] = piece[:, 0:n_small].astype(bf).astype(f32)
    for n in range(2):
        bias_ref[n] = column(sm_ref[:, (4 + n) * D : (5 + n) * D])
    ffn.start()
    for layer in range(3):
        attn.own_in(layer)

    def last_z():
        pl.when(at.z == 0)(lambda: attn.z_in(3))
        attn.first(3).start()
        attn.second(3).start()

    def firsts():
        attn.first_in(near[2])
        attn.across(1).start()

    def seconds():
        for layer in near:
            attn.second_in(layer)
        attn.across(2).start()

    def thirds():
        for layer in near:
            attn.third_in(layer)
        attn.across(3).start()

    def last_across():
        attn.second_in(3)
        attn.third_in(3)
        attn.across_last().start()

    def inner(j, n):
        return lambda: pl.when(ffn.inner())(lambda: ffn.z_in(j, n))

    def outer(j, n):
        return lambda: pl.when(jnp.logical_not(ffn.inner()))(lambda: ffn.z_in(j, n))

    def inner_second(j):
        return lambda: pl.when(ffn.inner())(lambda: ffn.second_in(j))

    def outer_second(j):
        return lambda: pl.when(jnp.logical_not(ffn.inner()))(lambda: ffn.second_in(j))

    ticks = {
        (0, 0): [firsts],
        (0, 1): [last_z, lambda: ffn.z_in(1, 0), inner(2, 0), seconds],
        (0, 2): [thirds, ffn.first_in],
        (1, 0): [lambda: attn.first_in(3)],
        (1, 1): [inner(3, 0), outer(2, 0), last_across],
        (1, 2): [inner(1, 1), inner(2, 1), lambda: ffn.second_in(0)],
        (2, 0): [outer(1, 1)],
        (2, 1): [outer(3, 0)],
        (2, 2): [inner(3, 1), inner_second(1)],
        (3, 0): [inner_second(2), outer_second(1)],
        (3, 1): [outer(2, 1), lambda: ffn.done(0)],
        (3, 2): [inner_second(3)],
    }
    x_copy.wait()
    q_rows, k_rows = segment_rows(seg_ref[...])
    for g, (gy, gx) in enumerate(attn.columns):
        if g:
            attn.across_in(g)
        base = (2 * gy + gx) * 2 * rows
        w = abuf[0:3, gy, gx].reshape(6 * rows, D)
        p = dot(w, x_ref[...], NT)
        for sec in range(3):
            part = p[2 * rows * sec : 2 * rows * (sec + 1)]
            if sec != 1:
                part = part + widen(bias_ref[sec // 2, pl.ds(pl.multiple_of(base, HD), 2 * rows), :], t)
            qkv_ref[pl.ds(pl.multiple_of(sec * D + base, HD), 2 * rows), :] = part.astype(bf)

        def head(i, _, g=g, base=base):
            for k in range(3):

                @pl.when(i == k)
                def _(k=k):
                    for event in ticks[g, k]:
                        event()

            h = base // HD + i
            r = rows_at(h, HD)
            q = qkv_ref[r, :] * bf(0.125)
            k = qkv_ref[pl.ds(pl.multiple_of(D + h * HD, HD), HD), :]
            v = qkv_ref[pl.ds(pl.multiple_of(2 * D + h * HD, HD), HD), :]
            s = dot(jnp.concatenate([k, k_rows], 0), jnp.concatenate([q, q_rows], 0), TN)
            top = jnp.max(s, axis=0, keepdims=True)
            e = jnp.exp2((s - top) * LOG2E)
            total = jnp.sum(e, axis=0, keepdims=True)
            o_ref[r, :] = (dot(v, e.astype(bf), NN) * (1.0 / total)).astype(bf)
            l_ref[h] = top + jnp.log(total)
            return 0

        lax.fori_loop(0, 3, head, 0)
    qkv_copy = pltpu.make_async_copy(qkv_ref, qkv_out, local_sem.at[1])
    qkv_copy.start()
    o_copy = pltpu.make_async_copy(o_ref, o_out, local_sem.at[13])
    o_copy.start()
    attn.last_in()
    aout_copy = pltpu.make_async_copy(abuf, aout, local_sem.at[0])
    aout_copy.start()
    for n, i in enumerate((0, 1, 6, 7)):
        vec_ref[n] = column(sm_ref[:, D * i : D * (i + 1)])
    lanes = 256

    def first_norm(i, _):
        cs = rows_at(i, lanes)
        wo = abuf[3].reshape(D, D)
        vec = [widen(vec_ref[n], lanes) for n in range(4)]
        r1 = jnp.transpose(x_ref[cs, :]).astype(f32) + dot(wo, o_ref[:, cs], NN) + vec[2]
        xh, scale = norm(r1)
        xh_ref[:, cs] = xh
        rs_ref[:, cs] = scale
        a1 = xh * vec[0] + vec[1]
        r2_ref[:, cs] = a1 + vec[3]
        low_ref[:, cs] = a1.astype(bf)
        return 0

    lax.fori_loop(0, t // lanes, first_norm, 0)
    xh_copy = pltpu.make_async_copy(xh_ref, xh_out, local_sem.at[2])
    xh_copy.start()
    low_copy = pltpu.make_async_copy(low_ref, low_out, local_sem.at[14])
    low_copy.start()
    half = 4 * rows

    def write_back(j, y):
        slot = (2 * j + y) % 2
        where = pl.ds(pl.multiple_of(ffn.layer[j] * 2 * half + y * half, half), half)
        return [
            pltpu.make_async_copy(act_ref.at[slot], act_out.at[where], local_sem.at[3 + slot]),
            pltpu.make_async_copy(gp_ref.at[slot], gp_out.at[where], local_sem.at[5 + slot]),
        ]

    fout_copies = []
    for j in range(LAYERS):
        layer = ffn.layer[j]
        if j == 0:
            outer(3, 1)()
            outer_second(2)()
        if j == 1:
            outer_second(3)()
        if j:
            ffn.done(j)
        fout_copies.append(pltpu.make_async_copy(fbuf.at[layer], fout.at[layer], local_sem.at[7 + j]))
        fout_copies[-1].start()
        for y in range(2):
            slot = (2 * j + y) % 2
            w1 = fbuf[layer, y, :, :, 0:rows, :].reshape(half, D)
            w2 = fbuf[layer, y, :, :, rows : 2 * rows, :].reshape(half, D)
            bias = sm_ref[:, pl.ds(pl.multiple_of(8 * D + layer * 2 * half + y * half, 128), half)]
            hid = dot(w1, low_ref[...], NN) + widen(column(bias), t)
            act, slope = gelu_both(hid)
            act = act.astype(bf)
            if 2 * j + y >= 2:
                for copy in write_back((2 * j + y - 2) // 2, y):
                    copy.wait()
            act_ref[slot] = act
            gp_ref[slot] = slope.astype(bf)
            for copy in write_back(j, y):
                copy.start()
            r2_ref[...] += dot(w2, act, TN)
    r2_copy = pltpu.make_async_copy(r2_ref, r2_out, local_sem.at[15])
    r2_copy.start()
    for y in range(2):
        for copy in write_back(LAYERS - 1, y):
            copy.wait()
    attn.drain()
    ffn.drain()
    small.drain()
    for copy in [aout_copy, qkv_copy, xh_copy, o_copy, low_copy, r2_copy] + fout_copies:
        copy.wait()


def forward_call(x, seg, aw, fw, smw):
    t, rows = x.shape[0], aw.shape[0]
    ff = 32 * rows
    n = 32 * smw.shape[1]
    wide = -(-smw.shape[1] // 128) * 128
    vm, anyw = pl.BlockSpec(memory_space=pltpu.VMEM), pl.BlockSpec(memory_space=pl.ANY)
    shape = jax.ShapeDtypeStruct
    sems = pltpu.SemaphoreType.DMA
    return pl.pallas_call(
        forward_kernel,
        name="gather_forward",
        in_specs=[vm] * 3 + [anyw] * 2,
        out_specs=[anyw, anyw, vm, anyw, anyw, vm, anyw, vm, anyw, anyw, anyw, anyw],
        out_shape=[
            shape((4, 2, 2, 2, rows, D), bf), shape((4, 2, 2, 2, 2 * rows, D), bf), shape((1, n), f32),
            shape((3 * D, t), bf), shape((D, t), bf), shape((HEADS, 1, t), f32), shape((D, t), f32),
            shape((1, t), f32), shape((D, t), bf), shape((D, t), f32), shape((ff, t), bf), shape((ff, t), bf),
        ],
        scratch_shapes=[
            pltpu.VMEM((4, 2, 2, 2, rows, D), bf), pltpu.VMEM((4, 2, 2, 2, 2 * rows, D), bf),
            pltpu.VMEM((4, 2, 2, 2, 1, wide), f32),
            pltpu.VMEM((3 * D, t), bf), pltpu.VMEM((D, t), f32), pltpu.VMEM((2, 4 * rows, t), bf),
            pltpu.VMEM((2, 4 * rows, t), bf), pltpu.VMEM((4, D, 128), f32), pltpu.VMEM((2, D, 128), f32),
            pltpu.VMEM((t, D), bf), pltpu.VMEM((2, rows, D), f32), pltpu.VMEM((D, t), bf), pltpu.VMEM((D, t), bf),
            pltpu.VMEM((D, t), f32),
            sems((27,)), sems((24,)), sems((23,)), sems((20,)), sems((7,)), sems((7,)), sems((16,)),
        ],
        compiler_params=pltpu.CompilerParams(
            vmem_limit_bytes=VMEM_LIMIT, collective_id=0, has_side_effects=True
        ),
    )(seg, aw, smw, x, fw)


def norm_back(dy, xh, scale, gain):
    dx = dy * gain
    mean_one = jnp.mean(dx, axis=0, keepdims=True)
    mean_two = jnp.mean(dx * xh, axis=0, keepdims=True)
    return scale * (dx - mean_one - xh * mean_two)


def accumulate(ref, term):
    ref[...] = ref[...] + term[...]


class Scatter:
    def __init__(self, at, layers, own, cross, pair, single, column, send, recv):
        self.at, self.layers, self.own, self.cross, self.pair, self.single = at, layers, own, cross, pair, single
        self.column, self.send, self.recv = column, send, recv
        self.p = (1 - at.c) * at.x + at.c * at.y

    def copy(self, src, dst, kind, layer, peer):
        n = kind * len(self.layers) + self.layers.index(layer)
        return remote(src, dst, self.send.at[n], self.recv.at[n], peer)

    def across(self, layer, src=None):
        dst = self.cross.at[self.layers.index(layer)]
        return self.copy(dst if src is None else src, dst, 0, layer, self.at.sib)

    def far(self, layer):
        dst = self.pair.at[self.layers.index(layer), 1 - self.p]
        return self.copy(self.own(layer, self.at.far_yx), dst, 1, layer, self.at.n2)

    def near(self, layer):
        dst = self.pair.at[self.layers.index(layer), self.p]
        return self.copy(self.own(layer, self.at.n2_yx), dst, 2, layer, self.at.n2)

    def first(self, layer):
        dst = self.single.at[self.layers.index(layer)]
        return self.copy(self.own(layer, self.at.n1_yx), dst, 3, layer, self.at.n1)

    def cross_in(self, layer):
        at, i = self.at, self.layers.index(layer)
        self.across(layer).wait_recv()
        for yx, copy in ((at.far_yx, self.far), (at.n2_yx, self.near), (at.n1_yx, None), ((at.y, at.x), None)):
            accumulate(self.own(layer, yx), self.cross.at[(i,) + yx])
            if copy is not None:
                copy(layer).start()

    def pair_in(self, layer):
        i = self.layers.index(layer)
        self.far(layer).wait_recv()
        accumulate(self.own(layer, self.at.n1_yx), self.pair.at[i, 1 - self.p])
        self.first(layer).start()
        self.near(layer).wait_recv()
        accumulate(self.own(layer, (self.at.y, self.at.x)), self.pair.at[i, self.p])

    def single_in(self, layer):
        self.first(layer).wait_recv()
        own = self.own(layer, (self.at.y, self.at.x))
        total = own[...].astype(f32) + self.single[self.layers.index(layer)].astype(f32)
        self.column[self.layers.index(layer)] = total.astype(bf)

    def drain(self, layer, src):
        self.across(layer, src).wait_send()
        for copy in (self.far, self.near, self.first):
            copy(layer).wait_send()


class Along:
    def __init__(self, at, column, land, send, recv):
        self.at, self.column, self.land, self.send, self.recv = at, column, land, send, recv

    def copy(self, layer):
        return remote(
            self.column.at[layer], self.land.at[self.at.z], self.send.at[layer], self.recv.at[self.at.z],
            self.at.at_layer(layer),
        )

    def start(self, layer):
        pl.when(self.at.z != layer)(lambda: self.copy(layer).start())

    def finish(self):
        total = self.column[self.at.z].astype(f32)
        for d in (1, 2, 3):
            layer = (self.at.z + d) % LAYERS
            ref = self.land.at[layer]
            remote(ref, ref, self.send.at[layer], self.recv.at[layer], self.at.sib).wait_recv()
            total = total + ref[...].astype(f32)
        return total

    def drain(self):
        for layer in range(LAYERS):
            pl.when(self.at.z != layer)(lambda layer=layer: self.copy(layer).wait_send())


VECS = (0, 2, 3)
EARLY = (0, 1)
LATE = (2, 3)


def middle_kernel(
    cot_ref, seg_ref, o_ref, xh_ref, rs_ref, low_ref, r2_ref, sm_ref, wo_ref, w_ref, act_ref, gp_ref,
    out_ref, dr1_ref, do_ref, dwo_ref, dw_out, sg_ref, column_ref,
    acc_ref, df_ref, vec_ref, part_ref, stage, cross, pair, single, send, recv, local_sem,
):
    step = pl.program_id(0)
    t = cot_ref.shape[0]
    rows = w_ref.shape[4] // 2
    half = 4 * rows
    lanes = 256
    at = Place()

    def own(layer, yx):
        return stage.at[(layer,) + yx + (at.c,)]

    def source(layer):
        return stage.at[layer, :, :, 1 - at.c]

    ffn = Scatter(at, EARLY, own, cross, pair, single, column_ref, send, recv)
    late = [pltpu.make_async_copy(stage.at[layer], dw_out.at[layer - 2], local_sem.at[layer - 2]) for layer in LATE]

    def vec(i):
        return widen(vec_ref[VECS.index(i)], lanes)

    def over_lanes(piece):
        def body(c, _):
            piece(rows_at(c, lanes))
            return 0

        lax.fori_loop(0, t // lanes, body, 0)

    @pl.when(step == 0)
    def _():
        greet([at.n1, at.n2, at.sib])
        for n, i in enumerate(VECS):
            vec_ref[n] = column(sm_ref[:, D * i : D * (i + 1)])
        part_ref[...] = jnp.zeros_like(part_ref)

        def second_norm(cs):
            xh, scale = norm(r2_ref[:, cs])
            out_ref[cs, :] = jnp.transpose((xh * vec(2) + vec(3)).astype(bf))
            valid = jnp.where(seg_ref[:, cs] >= 0, 1.0, 0.0)
            dy = jnp.transpose(cot_ref[cs, :]).astype(f32) * valid
            dr = norm_back(dy, xh, scale, vec(2))
            acc_ref[:, cs] = dr
            df_ref[:, cs] = dr.astype(bf)
            part_ref[0] += lane_fold(dy * xh)
            part_ref[1] += lane_fold(dy)
            part_ref[2] += lane_fold(dr)

        over_lanes(second_norm)

    w1 = w_ref[0, 0, :, :, 0:rows, :].reshape(half, D)
    w2 = w_ref[0, 0, :, :, rows : 2 * rows, :].reshape(half, D)
    dh = dot(w2, df_ref[...], NN) * gp_ref[...].astype(f32)
    sg_ref[:, pl.ds(pl.multiple_of(8 * D + step * half, 128), half)] = fold_row(lane_fold(dh))
    low = dh.astype(bf)
    dw2 = dot(act_ref[...], df_ref[...], NT).astype(bf)
    dw1 = dot(low, low_ref[...], NT).astype(bf)

    for x in range(2):
        for c in range(2):
            part = slice((2 * x + c) * rows, (2 * x + c + 1) * rows)
            stage[step // 2, step % 2, x, c, 0:rows, :] = dw1[part]
            stage[step // 2, step % 2, x, c, rows : 2 * rows, :] = dw2[part]
    acc_ref[...] += dot(w1, low, TN)
    events = {
        1: [lambda: ffn.across(0, source(0)).start()],
        2: [lambda: ffn.cross_in(0)],
        3: [lambda: ffn.across(1, source(1)).start()],
        4: [lambda: ffn.pair_in(0), lambda: ffn.cross_in(1)],
        5: [lambda: ffn.single_in(0), late[0].start],
        6: [lambda: ffn.pair_in(1)],
        7: [late[1].start],
    }
    for k, todo in events.items():

        @pl.when(step == k)
        def _(todo=todo):
            for event in todo:
                event()

    @pl.when(step == pl.num_programs(0) - 1)
    def _():
        wo = wo_ref[0].reshape(D, D)

        def first_back(cs):
            dy = acc_ref[:, cs]
            xh = xh_ref[:, cs]
            dr = norm_back(dy, xh, rs_ref[:, cs], vec(0))
            dr1_ref[:, cs] = dr
            dz = dr.astype(bf)
            df_ref[:, cs] = dz
            part_ref[3] += lane_fold(dy * xh)
            part_ref[4] += lane_fold(dy)
            part_ref[5] += lane_fold(dr)
            do_ref[:, cs] = dot(wo, dz, TN).astype(bf)

        over_lanes(first_back)
        dwo_ref[...] = dot(df_ref[...], o_ref[...], NT).astype(bf)
        for n, i in enumerate((2, 3, 7, 0, 1, 6)):
            sg_ref[:, D * i : D * (i + 1)] = fold_row(part_ref[n])
        sg_ref[:, 4 * D : 6 * D] = jnp.zeros((1, 2 * D), f32)
        ffn.single_in(1)
        for copy in late:
            copy.wait()
        for layer in EARLY:
            ffn.drain(layer, source(layer))


def middle_call(cot, seg, o, xh, rs, low, r2, sm, abuf, fbuf, act, gp):
    t = cot.shape[0]
    rf = fbuf.shape[4]
    half = 2 * rf
    shape = jax.ShapeDtypeStruct
    sems = pltpu.SemaphoreType.DMA

    def whole(a):
        return pl.BlockSpec(a.shape, lambda j: (0,) * len(a.shape))

    wspec = pl.BlockSpec((1, 1, 2, 2, rf, D), lambda j: (j // 2, j % 2, 0, 0, 0, 0))
    rspec = pl.BlockSpec((half, t), lambda j: (j, 0))
    outs = [
        shape((t, D), bf), shape((D, t), f32), shape((D, t), bf), shape((D, D), bf),
        shape((2, 2, 2, 2, rf, D), bf), shape(sm.shape, f32), shape((2, rf, D), bf),
    ]
    return pl.pallas_call(
        middle_kernel,
        name="middle_scatter",
        grid=(8,),
        in_specs=[whole(a) for a in (cot, seg, o, xh, rs, low, r2, sm)]
        + [pl.BlockSpec((1,) + abuf.shape[1:], lambda j: (3, 0, 0, 0, 0, 0)), wspec, rspec, rspec],
        out_specs=[whole(a) for a in outs[:4]] + [pl.BlockSpec(memory_space=pl.ANY)] + [whole(a) for a in outs[5:]],
        out_shape=outs,
        scratch_shapes=[
            pltpu.VMEM((D, t), f32), pltpu.VMEM((D, t), bf), pltpu.VMEM((3, D, 128), f32),
            pltpu.VMEM((6, D, 128), f32), pltpu.VMEM((4, 2, 2, 2, rf, D), bf), pltpu.VMEM((2, 2, 2, rf, D), bf),
            pltpu.VMEM((2, 2, rf, D), bf), pltpu.VMEM((2, rf, D), bf), sems((8,)), sems((8,)), sems((2,)),
        ],
        compiler_params=pltpu.CompilerParams(
            vmem_limit_bytes=VMEM_LIMIT, collective_id=2, has_side_effects=True
        ),
    )(cot, seg, o, xh, rs, low, r2, sm, abuf, fbuf, act, gp)


class ColumnScatter:
    def __init__(self, at, own, cross, pair, single, column, along, send, recv):
        self.at, self.own, self.cross, self.pair, self.single = at, own, cross, pair, single
        self.column, self.along, self.send, self.recv = column, along, send, recv
        self.columns = [(1 - at.y, 1 - at.x), (at.y, 1 - at.x), (1 - at.y, at.x), (at.y, at.x)]

    def part(self, yx, core):
        return self.own.at[(slice(0, 3),) + yx + (core,)]

    def across(self, g):
        yx = self.columns[g]
        return remote(
            self.part(yx, 1 - self.at.c), self.cross.at[(slice(None),) + yx], self.send.at[g], self.recv.at[g],
            self.at.sib,
        )

    def hop(self, kind):
        at = self.at
        yx, dst, peer = (
            (at.far_yx, self.pair.at[0], at.n2), (at.n2_yx, self.pair.at[1], at.n2), (at.n1_yx, self.single, at.n1)
        )[kind]
        return remote(self.part(yx, at.c), dst, self.send.at[4 + kind], self.recv.at[4 + kind], peer)

    def add(self, yx, terms):
        for layer in range(3):
            accumulate(self.own.at[(layer,) + yx + (self.at.c,)], terms(layer))

    def cross_in(self, g):
        yx = self.columns[g]
        self.across(g).wait_recv()
        self.add(yx, lambda layer: self.cross.at[(layer,) + yx])

    def far_out(self):
        self.cross_in(0)
        self.hop(0).start()

    def first_out(self):
        self.hop(0).wait_recv()
        self.add(self.at.n1_yx, lambda layer: self.pair.at[0, layer])
        self.hop(2).start()

    def neighbour_out(self, g):
        self.cross_in(g)
        pl.when(self.at.c == g - 1)(self.first_out)
        pl.when(self.at.c != g - 1)(lambda: self.hop(1).start())

    def own_out(self):
        at = self.at
        self.across(3).wait_recv()
        self.hop(1).wait_recv()
        self.hop(2).wait_recv()
        for layer in range(3):
            total = self.own[layer, at.y, at.x, at.c].astype(f32) + self.cross[layer, at.y, at.x].astype(f32)
            total = total + self.pair[1, layer].astype(f32) + self.single[layer].astype(f32)
            self.column[layer] = total.astype(bf)
            self.along.start(layer)

    def drain(self):
        for g in range(4):
            self.across(g).wait_send()
        for kind in range(3):
            self.hop(kind).wait_send()


class SmallScatter:
    def __init__(self, at, own, cross, pair, single, land, send, recv):
        self.at, self.own, self.cross, self.pair, self.single, self.land = at, own, cross, pair, single, land
        self.send, self.recv = send, recv

    def part(self, yx, core):
        return self.own.at[(slice(None),) + yx + (core,)]

    def across(self):
        at = self.at
        return remote(
            self.own.at[:, :, :, 1 - at.c], self.cross, self.send.at[0], self.recv.at[0], at.sib
        )

    def far(self):
        return remote(self.part(self.at.far_yx, self.at.c), self.pair.at[0], self.send.at[1], self.recv.at[1], self.at.n2)

    def near(self):
        return remote(self.part(self.at.n2_yx, self.at.c), self.pair.at[1], self.send.at[2], self.recv.at[2], self.at.n2)

    def first(self):
        return remote(self.part(self.at.n1_yx, self.at.c), self.single, self.send.at[3], self.recv.at[3], self.at.n1)

    def along(self, d):
        at = self.at
        layer = (at.z + d) % LAYERS
        return remote(
            self.own.at[layer, at.y, at.x, at.c], self.land.at[d], self.send.at[3 + d], self.recv.at[3 + d],
            at.at_layer(layer),
        )

    def cross_in(self):
        at = self.at
        self.across().wait_recv()
        for yx in (at.far_yx, at.n2_yx, at.n1_yx, (at.y, at.x)):
            ref = self.part(yx, at.c)
            ref[...] += self.cross[(slice(None),) + yx]
        self.far().start()
        self.near().start()

    def pair_in(self):
        at = self.at
        self.far().wait_recv()
        ref = self.part(at.n1_yx, at.c)
        ref[...] += self.pair[0]
        self.first().start()
        self.near().wait_recv()
        ref = self.part((at.y, at.x), at.c)
        ref[...] += self.pair[1]

    def single_in(self):
        self.first().wait_recv()
        ref = self.part((self.at.y, self.at.x), self.at.c)
        ref[...] += self.single[...]
        for d in (1, 2, 3):
            self.along(d).start()

    def finish(self):
        at = self.at
        total = self.own[at.z, at.y, at.x, at.c]
        for d in (1, 2, 3):
            self.along(d).wait_recv()
            total = total + self.land[d]
        return total

    def drain(self):
        for copy in (self.across, self.far, self.near, self.first):
            copy().wait_send()
        for d in (1, 2, 3):
            self.along(d).wait_send()


CQ = 512


def backward_kernel(
    x_ref, seg_ref, qkv_ref, o_ref, l_ref, do_ref, dwo_ref, sg_ref, early_ref, dwf, abuf, dr1,
    dx, gf_ref, ga_ref, gs_ref,
    g_ref, dwa, w_ref, dr1_ref, dx_ref, small_ref,
    fown, fcross, fpair, fsingle, fcolumn, fland,
    across_ref, apair, asingle, acolumn, aland, wcross, wpair, wsingle,
    scross, spair, ssingle, sland,
    fsend, frecv, fzsend, fzrecv, asend, arecv, azsend, azrecv, wsend, wrecv, ssend, srecv, local_sem,
):
    t = x_ref.shape[0]
    at = Place()
    rows = w_ref.shape[4]
    n_small = sg_ref.shape[1] // 32
    f_along = Along(at, fcolumn, fland, fzsend, fzrecv)
    a_along = Along(at, acolumn, aland, azsend, azrecv)
    ffn = Scatter(
        at, LATE, lambda layer, yx: fown.at[(layer - 2,) + yx], fcross, fpair, fsingle, fcolumn.at[2:4], fsend, frecv
    )
    last = Scatter(
        at, (3,), lambda layer, yx: dwa.at[(3,) + yx + (at.c,)], wcross, wpair, wsingle, acolumn.at[3:4], wsend, wrecv
    )
    attn = ColumnScatter(at, dwa, across_ref, apair, asingle, acolumn, a_along, asend, arecv)
    small = SmallScatter(at, small_ref, scross, spair, ssingle, sland, ssend, srecv)

    def ffn_source(layer):
        return dwf.at[layer - 2, :, :, 1 - at.c]

    last_source = dwa.at[3, :, :, 1 - at.c]
    loads = [
        pltpu.make_async_copy(dwf.at[layer - 2, :, :, at.c], fown.at[layer - 2], local_sem.at[layer - 2])
        for layer in LATE
    ]
    for copy in loads:
        copy.start()
    w_copy = pltpu.make_async_copy(abuf.at[0:3], w_ref, local_sem.at[2])
    w_copy.start()
    dr1_copy = pltpu.make_async_copy(dr1, dr1_ref, local_sem.at[3])
    dr1_copy.start()
    fcolumn[0:2] = early_ref[...]
    greet([at.at_layer((at.z + d) % LAYERS) for d in (1, 2, 3)] + [at.n1, at.n2, at.sib])
    for layer in LATE:
        ffn.across(layer, ffn_source(layer)).start()
    for y in range(2):
        for x in range(2):
            for c in range(2):
                i = y * 4 + x * 2 + c
                dwa[3, y, x, c] = dwo_ref[i * rows : (i + 1) * rows]
    last.across(3, last_source).start()
    for layer in EARLY:
        f_along.start(layer)

    def ffn_cross(layer):
        loads[layer - 2].wait()
        ffn.cross_in(layer)

    def ffn_single(layer):
        ffn.single_in(layer)
        f_along.start(layer)

    def last_single():
        last.single_in(3)
        a_along.start(3)

    ticks = {
        (0, 1): [lambda: ffn_cross(2)],
        (0, 2): [lambda: ffn_cross(3)],
        (1, 1): [lambda: ffn.pair_in(2), attn.far_out],
        (1, 2): [lambda: last.cross_in(3)],
        (2, 0): [lambda: ffn.pair_in(3)],
        (2, 1): [lambda: ffn_single(2), lambda: attn.neighbour_out(1)],
        (2, 2): [lambda: last.pair_in(3)],
        (3, 0): [lambda: ffn_single(3)],
        (3, 1): [lambda: attn.neighbour_out(2), last_single],
    }
    q_rows, k_rows = segment_rows(seg_ref[...])
    for g, (gy, gx) in enumerate(attn.columns):
        base = (2 * gy + gx) * 2 * rows

        def head(i, _, g=g, base=base):
            for k in range(3):
                if (g, k) in ticks:

                    @pl.when(i == k)
                    def _(k=k):
                        for event in ticks[g, k]:
                            event()

            h = base // HD + i
            hrows = rows_at(h, HD)
            krow = pl.ds(pl.multiple_of(D + h * HD, HD), HD)
            vrow = pl.ds(pl.multiple_of(2 * D + h * HD, HD), HD)
            q, k, v, do = qkv_ref[hrows, :], qkv_ref[krow, :], qkv_ref[vrow, :], do_ref[hrows, :]
            inner = jnp.sum(do.astype(f32) * o_ref[hrows, :].astype(f32), axis=0, keepdims=True)
            lrow = l_ref[h]
            keys = jnp.concatenate([k, k_rows], 0)
            queries = jnp.concatenate([q * bf(0.125), q_rows], 0)
            dv = dk = 0.0
            for n in range(t // CQ):
                cs = slice(n * CQ, (n + 1) * CQ)
                s = dot(keys, queries[:, cs], TN)
                p = jnp.exp2((s - lrow[:, cs]) * LOG2E)
                dp = dot(v, do[:, cs], TN)
                ds = (p * (dp - inner[:, cs])).astype(bf)
                dv = dv + dot(do[:, cs], p.astype(bf), NT)
                dk = dk + dot(q[:, cs], ds, NT)
                g_ref[hrows, cs] = (dot(k, ds, NN) * 0.125).astype(bf)
            g_ref[vrow, :] = dv.astype(bf)
            g_ref[krow, :] = (dk * 0.125).astype(bf)
            return 0

        lax.fori_loop(0, 3, head, 0)
        for sec in range(3):
            grad = g_ref[pl.ds(pl.multiple_of(sec * D + base, HD), 2 * rows), :]
            dw = dot(grad, x_ref[...], NN).astype(bf)
            for c in range(2):
                dwa[sec, gy, gx, c] = dw[c * rows : (c + 1) * rows]
        attn.across(g).start()
    sums = [sg_ref[:, 0 : 4 * D]]
    for sec in (0, 2):
        sums.append(fold_row(lane_fold(g_ref[sec * D : (sec + 1) * D, :].astype(f32))))
    sums = jnp.concatenate(sums + [sg_ref[:, 6 * D :]], axis=1)
    pad = jnp.zeros((1, small_ref.shape[-1] - n_small), f32)
    for i in range(32):
        z, y, x, c = i // 8, (i // 4) % 2, (i // 2) % 2, i % 2
        small_ref[z, y, x, c] = jnp.concatenate([sums[:, i * n_small : (i + 1) * n_small], pad], axis=1)
    small.across().start()
    attn.own_out()
    w_copy.wait()
    dr1_copy.wait()
    lanes = 256

    def input_block(i, _):
        cs = rows_at(i, lanes)
        w = w_ref[...].reshape(3 * D, D)
        dx_ref[cs, :] = jnp.transpose(dr1_ref[:, cs]) + dot(g_ref[:, cs], w, TN)
        return 0

    lax.fori_loop(0, 1, input_block, 0)
    small.cross_in()
    lax.fori_loop(1, 2, input_block, 0)
    small.pair_in()
    lax.fori_loop(2, t // lanes, input_block, 0)
    small.single_in()
    dx_copy = pltpu.make_async_copy(dx_ref, dx, local_sem.at[4])
    dx_copy.start()
    gf_ref[...] = f_along.finish()
    ga_ref[...] = a_along.finish()
    gs_ref[...] = small.finish()
    for layer in LATE:
        ffn.drain(layer, ffn_source(layer))
    last.drain(3, last_source)
    for stage in (attn, f_along, a_along, small):
        stage.drain()
    dx_copy.wait()


def backward_call(x, seg, qkv, o, logs, do, dwo, sg, early, dwf, abuf, dr1):
    t = x.shape[0]
    ra, rf = abuf.shape[4], dwf.shape[4]
    wide = -(-(sg.shape[1] // 32) // 128) * 128
    vm, anyw = pl.BlockSpec(memory_space=pltpu.VMEM), pl.BlockSpec(memory_space=pl.ANY)
    shape = jax.ShapeDtypeStruct
    sems = pltpu.SemaphoreType.DMA

    def half(*dims):
        return pltpu.VMEM(dims + (D,), bf)

    def small(*dims):
        return pltpu.VMEM(dims + (1, wide), f32)

    return pl.pallas_call(
        backward_kernel,
        name="backward_scatter",
        in_specs=[vm] * 9 + [anyw] * 3,
        out_specs=[anyw, vm, vm, vm],
        out_shape=[shape((t, D), f32), shape((rf, D), f32), shape((ra, D), f32), shape((1, wide), f32)],
        scratch_shapes=[
            pltpu.VMEM((3 * D, t), bf), half(4, 2, 2, 2, ra), half(3, 2, 2, 2, ra), pltpu.VMEM((D, t), f32),
            pltpu.VMEM((t, D), f32), small(4, 2, 2, 2),
            half(2, 2, 2, rf), half(2, 2, 2, rf), half(2, 2, rf), half(2, rf), half(4, rf), half(4, rf),
            half(3, 2, 2, ra), half(2, 3, ra), half(3, ra), half(4, ra), half(4, ra), half(1, 2, 2, ra),
            half(1, 2, ra), half(1, ra),
            small(4, 2, 2), small(2, 4), small(4), small(4),
            sems((8,)), sems((8,)), sems((4,)), sems((4,)), sems((7,)), sems((7,)), sems((4,)), sems((4,)),
            sems((4,)), sems((4,)), sems((7,)), sems((7,)), sems((5,)),
        ],
        compiler_params=pltpu.CompilerParams(
            vmem_limit_bytes=VMEM_LIMIT, collective_id=1, has_side_effects=True
        ),
    )(x, seg, qkv, o, logs, do, dwo, sg, early, dwf, abuf, dr1)


def gradients_block(features, cotangent, segment_ids, attn_weights, ffn_weights, small_params):
    t, rows = features.shape[0], attn_weights.shape[0]
    seg = segment_ids.reshape(1, t)
    abuf, fbuf, sm, qkv, o, logs, xh, rs, low, r2, act, gp = forward_call(
        features, seg, attn_weights, ffn_weights, small_params.reshape(1, -1)
    )
    outputs, dr1, do, dwo, dwf, sg, early = middle_call(cotangent, seg, o, xh, rs, low, r2, sm, abuf, fbuf, act, gp)
    input_grad, gf, ga, gs = backward_call(
        features, seg, qkv, o, logs, do, dwo, sg, early, dwf, abuf, dr1
    )
    return outputs, input_grad, ga, gf.reshape(2, rows, D), gs[0, : small_params.shape[0]]


def local(
    gradients,
    features, cotangent, segment_ids, attn_weights, ffn_weights, small_params,
    attn_first, ffn_first, small_first, attn_second, ffn_second, small_second,
    attn_ema, ffn_ema, small_ema,
):
    outputs, input_grad, attn_sum, ffn_sum, small_sum = gradients(
        features, cotangent, segment_ids, attn_weights, ffn_weights, small_params
    )
    attn = adam_step(attn_weights, attn_sum, attn_first, attn_second, attn_ema, 0.01, 0.05)
    ffn = adam_step(ffn_weights, ffn_sum, ffn_first, ffn_second, ffn_ema, 0.01, 0.05)
    small = adam_step(small_params, small_sum, small_first, small_second, small_ema, 0.0, 0.3)
    return (outputs, input_grad) + tuple(x for trio in zip(attn, ffn, small) for x in trio)


def solution(mesh):
    block = mesh.shape["dp"] == 8 and mesh.shape["fsdp"] == 4
    gradients = gradients_block if block else gradients_general
    row = P(("dp", "fsdp"), None)
    wide = P(None, ("dp", "fsdp"), None)
    flat = P(("dp", "fsdp"))
    state = (row, wide, flat)
    return jax.shard_map(
        partial(local, gradients),
        mesh=mesh,
        in_specs=(row, row, flat) + state * 4,
        out_specs=(row, row) + state * 4,
        check_vma=False,
    )
```

```python
from functools import partial

import jax
import jax.numpy as jnp
from jax import lax
from jax.experimental import pallas as pl
from jax.experimental.pallas import tpu as pltpu
from jax.sharding import PartitionSpec as P

D = 768
HEADS = 12
HD = D // HEADS
STEP = 10
LOG2E = 1.4426950408889634
INV_SQRT2 = 0.7071067811865476
INV_SQRT2PI = 0.3989422804014327
BIG = 2.0**30
VMEM_LIMIT = 60 * 1024 * 1024

bf = jnp.bfloat16
f32 = jnp.float32
TN = (((0,), (0,)), ((), ()))
NN = (((1,), (0,)), ((), ()))
NT = (((1,), (1,)), ((), ()))


def dot(left, right, dims):
    return lax.dot_general(left, right, dims, preferred_element_type=f32)


def rows_at(i, size):
    return pl.ds(pl.multiple_of(i * size, size), size)


def column(row):
    return jnp.transpose(jnp.broadcast_to(row, (128, row.shape[1])))


def widen(col, width):
    return jnp.concatenate([col] * (width // 128), axis=1) if width > 128 else col


def lane_fold(x):
    total = x[:, :128]
    for i in range(1, x.shape[1] // 128):
        total = total + x[:, 128 * i : 128 * (i + 1)]
    return total


def fold_row(part):
    return jnp.sum(jnp.transpose(part), axis=0, keepdims=True)


def segment_rows(seg):
    ids = lax.broadcasted_iota(jnp.int32, (16, seg.shape[1]), 0) - 1
    same = jnp.where(ids == seg, 1.0, 0.0)
    return ((same - 1.0) * BIG).astype(bf), same.astype(bf)


def plain_forward_kernel(x_ref, seg_ref, w_ref, sm_ref, qkv_ref, o_ref, l_ref):
    t = x_ref.shape[0]
    block = 256

    def project_block(i, _):
        rows = rows_at(i, block)
        sec = i // (D // block)
        off = i - sec * (D // block)
        bias = sm_ref[:, pl.ds(pl.multiple_of((4 + sec // 2) * D + off * block, block), block)]
        keep = jnp.where(sec == 1, 0.0, 1.0)
        col = column(bias.astype(f32) * keep)
        qkv_ref[rows, :] = (dot(w_ref[rows, :], x_ref[...], NT) + widen(col, t)).astype(bf)
        return 0

    lax.fori_loop(0, 3 * D // block, project_block, 0)
    q_rows, k_rows = segment_rows(seg_ref[...])

    def head(h, _):
        rows = rows_at(h, HD)
        q = qkv_ref[rows, :] * bf(0.125)
        k = qkv_ref[pl.ds(pl.multiple_of(D + h * HD, HD), HD), :]
        v = qkv_ref[pl.ds(pl.multiple_of(2 * D + h * HD, HD), HD), :]
        s = dot(jnp.concatenate([k, k_rows], 0), jnp.concatenate([q, q_rows], 0), TN)
        top = jnp.max(s, axis=0, keepdims=True)
        e = jnp.exp2((s - top) * LOG2E)
        total = jnp.sum(e, axis=0, keepdims=True)
        o_ref[rows, :] = (dot(v, e.astype(bf), NN) * (1.0 / total)).astype(bf)
        l_ref[h] = top + jnp.log(total)
        return 0

    lax.fori_loop(0, HEADS, head, 0)


def gelu_both(h):
    cdf = 0.5 + 0.5 * lax.erf(h * INV_SQRT2)
    pdf = jnp.exp(h * h * -0.5) * INV_SQRT2PI
    return h * cdf, cdf + h * pdf


PLAIN_VECS = (0, 1, 2, 3, 6, 7)


def plain_middle_kernel(
    x_ref, o_ref, cot_ref, seg_ref, wo_ref, w1_ref, w2_ref, sm_ref,
    out_ref, dr1_ref, do_ref, dwo_ref, dw1_ref, dw2_ref, sg_ref,
    a1_ref, xh_ref, act_ref, gp_ref, rs_ref, low_ref, df_ref, vec_ref, part_ref,
):
    t = x_ref.shape[0]
    ff = w1_ref.shape[0]
    block, lanes = 256, 256
    for n, i in enumerate(PLAIN_VECS):
        vec_ref[n] = column(sm_ref[:, D * i : D * (i + 1)].astype(f32))
    part_ref[...] = jnp.zeros_like(part_ref)

    def vec(i):
        return widen(vec_ref[PLAIN_VECS.index(i)], lanes)

    def over_lanes(step):
        def body(c, _):
            step(rows_at(c, lanes))
            return 0

        lax.fori_loop(0, t // lanes, body, 0)

    def norm(r):
        centre = r - jnp.mean(r, axis=0, keepdims=True)
        scale = lax.rsqrt(jnp.mean(centre * centre, axis=0, keepdims=True) + 1e-5)
        return centre * scale, scale

    def norm_back(dy, xh, scale, gain):
        dx = dy * gain
        mean_one = jnp.mean(dx, axis=0, keepdims=True)
        mean_two = jnp.mean(dx * xh, axis=0, keepdims=True)
        return scale * (dx - mean_one - xh * mean_two)

    def first_norm(cs):
        r1 = jnp.transpose(x_ref[cs, :]).astype(f32) + dot(wo_ref[...], o_ref[:, cs], NN) + vec(6)
        xh, scale = norm(r1)
        xh_ref[:, cs] = xh
        rs_ref[:, cs] = scale
        a1 = xh * vec(0) + vec(1)
        a1_ref[:, cs] = a1 + vec(7)
        low_ref[:, cs] = a1.astype(bf)

    over_lanes(first_norm)

    def up_down(j, _):
        rows = rows_at(j, block)
        bias = sm_ref[:, pl.ds(pl.multiple_of(8 * D + j * block, block), block)]
        hid = dot(w1_ref[rows, :], low_ref[...], NN) + widen(column(bias.astype(f32)), t)
        act, slope = gelu_both(hid)
        act = act.astype(bf)
        act_ref[rows, :] = act
        gp_ref[rows, :] = slope.astype(gp_ref.dtype)
        a1_ref[...] += dot(w2_ref[rows, :], act, TN)
        return 0

    lax.fori_loop(0, ff // block, up_down, 0)

    def second_norm(cs):
        xh, scale = norm(a1_ref[:, cs])
        out_ref[cs, :] = jnp.transpose((xh * vec(2) + vec(3)).astype(bf))
        valid = jnp.where(seg_ref[:, cs] >= 0, 1.0, 0.0)
        dy = jnp.transpose(cot_ref[cs, :]).astype(f32) * valid
        dr = norm_back(dy, xh, scale, vec(2))
        a1_ref[:, cs] = dr
        df_ref[:, cs] = dr.astype(bf)
        part_ref[0] += lane_fold(dy * xh)
        part_ref[1] += lane_fold(dy)
        part_ref[2] += lane_fold(dr)

    over_lanes(second_norm)

    def back(j, _):
        rows = rows_at(j, block)
        dh = dot(w2_ref[rows, :], df_ref[...], NN) * gp_ref[rows, :].astype(f32)
        sg_ref[:, pl.ds(pl.multiple_of(8 * D + j * block, block), block)] = fold_row(lane_fold(dh))
        low = dh.astype(bf)
        dw2_ref[rows, :] = dot(act_ref[rows, :], df_ref[...], NT).astype(dw2_ref.dtype)
        dw1_ref[rows, :] = dot(low, low_ref[...], NT).astype(dw1_ref.dtype)
        a1_ref[...] += dot(w1_ref[rows, :], low, TN)
        return 0

    lax.fori_loop(0, ff // block, back, 0)

    def first_back(cs):
        dy = a1_ref[:, cs]
        xh = xh_ref[:, cs]
        dr = norm_back(dy, xh, rs_ref[:, cs], vec(0))
        dr1_ref[:, cs] = dr
        dz = dr.astype(bf)
        low_ref[:, cs] = dz
        part_ref[3] += lane_fold(dy * xh)
        part_ref[4] += lane_fold(dy)
        part_ref[5] += lane_fold(dr)
        do_ref[:, cs] = dot(wo_ref[...], dz, TN).astype(bf)

    over_lanes(first_back)
    dwo_ref[...] = dot(low_ref[...], o_ref[...], NT).astype(dwo_ref.dtype)
    for n, i in enumerate((2, 3, 7, 0, 1, 6)):
        sg_ref[:, D * i : D * (i + 1)] = fold_row(part_ref[n])
    sg_ref[:, 4 * D : 6 * D] = jnp.zeros((1, 2 * D), f32)


def plain_backward_kernel(
    x_ref, seg_ref, w_ref, qkv_ref, o_ref, l_ref, do_ref, dr1_ref,
    dx_ref, dw_ref, db_ref,
    g_ref,
):
    t = x_ref.shape[0]
    q_rows, k_rows = segment_rows(seg_ref[...])

    def head(h, _):
        rows = rows_at(h, HD)
        krow = pl.ds(pl.multiple_of(D + h * HD, HD), HD)
        vrow = pl.ds(pl.multiple_of(2 * D + h * HD, HD), HD)
        q, k, v, do = qkv_ref[rows, :], qkv_ref[krow, :], qkv_ref[vrow, :], do_ref[rows, :]
        inner = jnp.sum(do.astype(f32) * o_ref[rows, :].astype(f32), axis=0, keepdims=True)
        s = dot(
            jnp.concatenate([k, k_rows], 0), jnp.concatenate([q * bf(0.125), q_rows], 0), TN
        )
        p = jnp.exp2((s - l_ref[h]) * LOG2E)
        dp = dot(v, do, TN)
        ds = (p * (dp - inner)).astype(bf)
        g_ref[vrow, :] = dot(do, p.astype(bf), NT).astype(bf)
        g_ref[krow, :] = (dot(q, ds, NT) * 0.125).astype(bf)
        g_ref[rows, :] = (dot(k, ds, NN) * 0.125).astype(bf)
        return 0

    lax.fori_loop(0, HEADS, head, 0)
    block = 256

    def weight_block(i, _):
        rows = rows_at(i, block)
        g = g_ref[rows, :]
        dw_ref[rows, :] = dot(g, x_ref[...], NN).astype(dw_ref.dtype)
        db_ref[:, rows] = fold_row(lane_fold(g.astype(f32)))
        return 0

    lax.fori_loop(0, 3 * D // block, weight_block, 0)

    def input_block(i, _):
        rows = rows_at(i, block)
        dx_ref[rows, :] = jnp.transpose(dr1_ref[:, rows]) + dot(g_ref[:, rows], w_ref[...], TN)
        return 0

    lax.fori_loop(0, t // block, input_block, 0)


def call(kernel, name, outs, scratch, *args):
    return pl.pallas_call(
        kernel,
        out_shape=[jax.ShapeDtypeStruct(s, d) for s, d in outs],
        scratch_shapes=[pltpu.VMEM(s, d) for s, d in scratch],
        compiler_params=pltpu.CompilerParams(vmem_limit_bytes=VMEM_LIMIT),
        name=name,
    )(*args)


def adam_step(weight, grad_sum, first_mom, second_mom, average, decay, rate):
    first_new = 0.9 * first_mom + 0.1 * grad_sum
    second_new = 0.98 * second_mom + 0.02 * grad_sum * grad_sum
    corrected = first_new / (1.0 - 0.9**STEP)
    denominator = jnp.sqrt(second_new / (1.0 - 0.98**STEP)) + 1e-06
    weight_new = weight - rate * (corrected / denominator + decay * weight)
    average_new = 0.75 * average + 0.25 * weight_new
    return (weight_new, first_new, second_new, average_new)


def gradients_general(features, cotangent, segment_ids, attn_weights, ffn_weights, small_params):
    axes = ("dp", "fsdp")
    t = features.shape[0]
    attn_full = lax.all_gather(attn_weights.astype(bf), axes, axis=0, tiled=True)
    ffn_full = lax.all_gather(ffn_weights.astype(bf), axes, axis=1, tiled=True)
    small_full = lax.all_gather(small_params.astype(bf), axes, axis=0, tiled=True)
    ff = ffn_full.shape[1]
    smalls = small_full.reshape(1, -1)
    seg = segment_ids.reshape(1, t)
    qkv, mixed, logs = call(
        plain_forward_kernel, "attend_forward",
        [((3 * D, t), bf), ((D, t), bf), ((HEADS, 1, t), f32)], [],
        features, seg, attn_full[: 3 * D], smalls,
    )
    outputs, dr1, do, dwo, dw1, dw2, small_grad = call(
        plain_middle_kernel, "plain_middle",
        [((t, D), bf), ((D, t), f32), ((D, t), bf), ((D, D), bf), ((ff, D), bf), ((ff, D), bf),
         ((1, smalls.shape[1]), f32)],
        [((D, t), f32), ((D, t), f32), ((ff, t), bf), ((ff, t), bf), ((1, t), f32), ((D, t), bf),
         ((D, t), bf), ((6, D, 128), f32), ((6, D, 128), f32)],
        features, mixed, cotangent, seg, attn_full[3 * D :], ffn_full[0], ffn_full[1], smalls,
    )
    input_grad, dqkv, bias_grad = call(
        plain_backward_kernel, "attend_backward",
        [((t, D), f32), ((3 * D, D), bf), ((1, 3 * D), f32)], [((3 * D, t), bf)],
        features, seg, attn_full[: 3 * D], qkv, mixed, logs, do, dr1,
    )
    small_grad = small_grad.reshape(-1)
    small_grad = jnp.concatenate(
        [small_grad[: 4 * D], bias_grad[0, :D], bias_grad[0, 2 * D :], small_grad[6 * D :]]
    )
    attn_sum, ffn_sum, small_sum = (
        lax.psum_scatter(jnp.concatenate([dqkv, dwo]), axes, scatter_dimension=0, tiled=True),
        lax.psum_scatter(jnp.stack([dw1, dw2]), axes, scatter_dimension=1, tiled=True),
        lax.psum_scatter(small_grad, axes, scatter_dimension=0, tiled=True),
    )
    return outputs, input_grad, attn_sum.astype(f32), ffn_sum.astype(f32), small_sum


MESH = pl.DeviceIdType.MESH
LAYERS = 4


class Place:
    def __init__(self):
        zy, xc = lax.axis_index("dp"), lax.axis_index("fsdp")
        self.z, self.y, self.x, self.c = zy // 2, zy % 2, xc // 2, xc % 2
        z, y, x, c = self.z, self.y, self.x, self.c
        self.n1 = (z * 2 + (y + c) % 2, ((x + 1 - c) % 2) * 2 + c)
        self.n2 = (z * 2 + (y + 1 - c) % 2, ((x + c) % 2) * 2 + c)
        self.sib = (z * 2 + y, x * 2 + 1 - c)
        self.n1_yx = ((y + c) % 2, (x + 1 - c) % 2)
        self.n2_yx = ((y + 1 - c) % 2, (x + c) % 2)
        self.far_yx = (1 - y, 1 - x)
        self.is_z = ((3 - z) // 3, (z % 2) * (1 - z // 2), ((z + 1) % 2) * (z // 2), z // 3)

    def pick(self, table):
        return sum(t * e for t, e in zip(table, self.is_z) if t)

    def at_layer(self, layer):
        return (layer * 2 + self.y, self.x * 2 + self.c)


def greet(peers):
    barrier = pltpu.get_barrier_semaphore()
    for peer in peers:
        pl.semaphore_signal(barrier, inc=1, device_id=peer, device_id_type=MESH)
    pl.semaphore_wait(barrier, len(peers))


def remote(src, dst, send, recv, peer):
    return pltpu.make_async_remote_copy(
        src_ref=src, dst_ref=dst, send_sem=send, recv_sem=recv, device_id=peer, device_id_type=MESH
    )


class Gather:
    NEAR = ((0, 1, 2, 3), (1, 0, 1, 2), (2, 2, 3, 1), (3, 3, 0, 0))
    ONWARD = (None, (0, 2, 3, 0), (0, 0, 1, 0), (0, 0, 3, 0))

    def __init__(self, at, buf, send, recv):
        self.at, self.buf, self.send, self.recv = at, buf, send, recv
        self.layer = [at.pick(t) for t in self.NEAR]
        self.columns = [(at.y, at.x), at.n1_yx, at.n2_yx, at.far_yx]

    def copy(self, idx, src, dst, peer):
        ref = self.buf.at[idx]
        return remote(ref, ref, self.send.at[src], self.recv.at[dst], peer)

    def slot(self, layer, column):
        return (layer,) + self.columns[column] + (self.at.c,)

    def up(self, column):
        at = self.at
        return self.copy(self.slot(at.z, column), column, 4 * column + at.z, at.at_layer((at.z + 1) % LAYERS))

    def down(self, column):
        at = self.at
        return self.copy(
            self.slot(at.z, column), 2 + column, 4 * column + at.z, at.at_layer((at.z + LAYERS - 1) % LAYERS)
        )

    def onward(self, j, column):
        layer = self.layer[j]
        return self.copy(
            self.slot(layer, column), 3 + j + 3 * column, 4 * column + layer,
            self.at.at_layer(self.at.pick(self.ONWARD[j])),
        )

    def first(self):
        return self.copy(self.slot(self.at.z, 0), 10, 4 + self.at.z, self.at.n1)

    def second(self, j, column):
        layer = self.layer[j]
        return self.copy(self.slot(layer, column), 11 + 4 * column + j, 8 + 4 * column + layer, self.at.n2)

    def across(self, j):
        layer = self.layer[j]
        return self.copy((layer, slice(None), slice(None), self.at.c), 19 + j, 16 + layer, self.at.sib)

    def arrived(self, idx, dst):
        self.copy(idx, 0, dst, self.at.sib).wait_recv()

    def spread(self, column):
        pl.when(self.at.z < LAYERS - 1)(lambda: self.up(column).start())
        pl.when(self.at.z > 0)(lambda: self.down(column).start())
        self.second(0, column).start()

    def start(self):
        self.first().start()
        self.spread(0)

    def inner(self):
        return (self.at.z + 1) // 2 == 1

    def first_in(self):
        self.arrived(self.slot(self.at.z, 1), 4 + self.at.z)
        self.spread(1)

    def z_in(self, j, column):
        layer = self.layer[j]
        self.arrived(self.slot(layer, column), 4 * column + layer)
        pl.when(self.inner())(lambda: self.onward(j, column).start())
        self.second(j, column).start()

    def second_in(self, j):
        layer = self.layer[j]
        self.arrived(self.slot(layer, 2), 8 + layer)
        self.arrived(self.slot(layer, 3), 12 + layer)
        self.across(j).start()

    def done(self, j):
        layer = self.layer[j]
        self.arrived((layer, slice(None), slice(None), 1 - self.at.c), 16 + layer)

    def drain(self):
        self.first().wait_send()
        for n in range(2):
            pl.when(self.at.z < LAYERS - 1)(lambda n=n: self.up(n).wait_send())
            pl.when(self.at.z > 0)(lambda n=n: self.down(n).wait_send())
            for j in range(1, LAYERS):
                pl.when(self.inner())(lambda j=j, n=n: self.onward(j, n).wait_send())
            for j in range(LAYERS):
                self.second(j, n).wait_send()
        for j in range(LAYERS):
            self.across(j).wait_send()


class ColumnGather:
    NEAR = ((0, 1, 2, 2), (1, 0, 1, 1), (2, 2, 0, 0))

    def __init__(self, at, buf, send, recv):
        self.at, self.buf, self.send, self.recv = at, buf, send, recv
        self.near = [at.pick(t) for t in self.NEAR]
        self.columns = [(at.y, at.x), at.n1_yx, at.n2_yx, at.far_yx]

    def copy(self, idx, src, dst, peer):
        ref = self.buf.at[idx]
        return pltpu.make_async_remote_copy(
            src_ref=ref, dst_ref=ref, send_sem=self.send.at[src], recv_sem=self.recv.at[dst],
            device_id=peer, device_id_type=MESH,
        )

    def slot(self, layer, column, core=None):
        return (layer,) + self.columns[column] + (self.at.c if core is None else core,)

    def up(self, layer):
        return self.copy(self.slot(layer, 0), layer, layer, self.at.at_layer((self.at.z + 1) % LAYERS))

    def down(self, layer):
        return self.copy(
            self.slot(layer, 0), 4 + layer, layer, self.at.at_layer((self.at.z + LAYERS - 1) % LAYERS)
        )

    def first(self, layer):
        return self.copy(self.slot(layer, 0), 8 + layer, 4 + layer, self.at.n1)

    def second(self, layer):
        return self.copy(self.slot(layer, 0), 12 + layer, 8 + layer, self.at.n2)

    def third(self, layer):
        return self.copy(self.slot(layer, 1), 16 + layer, 12 + layer, self.at.n2)

    def own(self, layer):
        return self.copy(self.slot(layer, 0), 20 + layer, 16 + layer, self.at.sib)

    def across(self, column):
        y, x = self.columns[column]
        return self.copy((slice(0, 3), y, x, self.at.c), 23 + column, 20 + 2 * y + x, self.at.sib)

    def across_last(self):
        return self.copy((3, slice(None), slice(None), self.at.c), 23, 19, self.at.sib)

    def arrived(self, idx, dst):
        self.copy(idx, 0, dst, self.at.sib).wait_recv()

    def goes_up(self, layer):
        return jnp.logical_and(self.at.z >= layer, self.at.z < LAYERS - 1)

    def goes_down(self, layer):
        return jnp.logical_and(self.at.z <= layer, self.at.z > 0)

    def along(self, layer):
        pl.when(self.goes_up(layer))(lambda: self.up(layer).start())
        pl.when(self.goes_down(layer))(lambda: self.down(layer).start())

    def spread(self, layer):
        self.own(layer).start()
        self.first(layer).start()
        self.second(layer).start()

    def z_in(self, layer):
        self.arrived(self.slot(layer, 0), layer)

    def first_in(self, layer):
        self.arrived(self.slot(layer, 1), 4 + layer)
        self.third(layer).start()

    def second_in(self, layer):
        self.arrived(self.slot(layer, 2), 8 + layer)

    def third_in(self, layer):
        self.arrived(self.slot(layer, 3), 12 + layer)

    def own_in(self, layer):
        self.arrived(self.slot(layer, 0, 1 - self.at.c), 16 + layer)

    def across_in(self, column):
        y, x = self.columns[column]
        self.arrived((slice(0, 3), y, x, 1 - self.at.c), 20 + 2 * y + x)

    def last_in(self):
        self.arrived((3, slice(None), slice(None), 1 - self.at.c), 19)

    def drain(self):
        for layer in range(LAYERS):
            pl.when(self.goes_up(layer))(lambda layer=layer: self.up(layer).wait_send())
            pl.when(self.goes_down(layer))(lambda layer=layer: self.down(layer).wait_send())
            self.first(layer).wait_send()
            self.second(layer).wait_send()
            self.third(layer).wait_send()
        for n in range(3):
            self.own(n).wait_send()
            self.across(n + 1).wait_send()
        self.across_last().wait_send()


class SmallGather:
    def __init__(self, at, buf, send, recv):
        self.at, self.buf, self.send, self.recv = at, buf, send, recv

    def copy(self, idx, src, dst, peer):
        ref = self.buf.at[idx]
        return pltpu.make_async_remote_copy(
            src_ref=ref, dst_ref=ref, send_sem=self.send.at[src], recv_sem=self.recv.at[dst],
            device_id=peer, device_id_type=MESH,
        )

    def along(self, d):
        at = self.at
        return self.copy((at.z, at.y, at.x, at.c), d - 1, d - 1, at.at_layer((at.z + d) % LAYERS))

    def first(self):
        return self.copy((slice(None), self.at.y, self.at.x, self.at.c), 3, 3, self.at.n1)

    def second(self):
        return self.copy((slice(None), self.at.y, self.at.x, self.at.c), 4, 4, self.at.n2)

    def third(self):
        return self.copy((slice(None),) + self.at.n1_yx + (self.at.c,), 5, 5, self.at.n2)

    def across(self):
        return self.copy((slice(None), slice(None), slice(None), self.at.c), 6, 6, self.at.sib)

    def start(self):
        for d in (1, 2, 3):
            self.along(d).start()

    def spread(self):
        for d in (1, 2, 3):
            self.along(d).wait_recv()
        self.first().start()
        self.second().start()

    def forward(self):
        self.first().wait_recv()
        self.third().start()

    def cross(self):
        self.second().wait_recv()
        self.third().wait_recv()
        self.across().start()

    def done(self):
        self.across().wait_recv()

    def drain(self):
        for d in (1, 2, 3):
            self.along(d).wait_send()
        for copy in (self.first, self.second, self.third, self.across):
            copy().wait_send()


def norm(r):
    centre = r - jnp.mean(r, axis=0, keepdims=True)
    scale = lax.rsqrt(jnp.mean(centre * centre, axis=0, keepdims=True) + 1e-5)
    return centre * scale, scale


def forward_kernel(
    seg_ref, aw_ref, smw_ref, x, fw,
    aout, fout, sm_ref, qkv_out, o_out, l_ref, xh_out, rs_ref, low_out, r2_out, act_out, gp_out,
    abuf, fbuf, sbuf, qkv_ref, xh_ref, act_ref, gp_ref, vec_ref, bias_ref, x_ref, fw_ref, o_ref, low_ref, r2_ref,
    asend, arecv, fsend, frecv, ssend, srecv, local_sem,
):
    t = x_ref.shape[0]
    rows = aw_ref.shape[0]
    n_small = smw_ref.shape[1]
    at = Place()
    me = (at.z, at.y, at.x, at.c)
    fw_copy = pltpu.make_async_copy(fw, fw_ref, local_sem.at[11])
    fw_copy.start()
    x_copy = pltpu.make_async_copy(x, x_ref, local_sem.at[12])
    x_copy.start()
    abuf[me] = aw_ref[...].astype(bf)
    pad = jnp.zeros((1, sbuf.shape[-1] - n_small), f32)
    sbuf[me] = jnp.concatenate([smw_ref[...], pad], axis=1)
    attn = ColumnGather(at, abuf, asend, arecv)
    ffn = Gather(at, fbuf, fsend, frecv)
    small = SmallGather(at, sbuf, ssend, srecv)
    near = attn.near
    greet([at.at_layer((at.z + d) % LAYERS) for d in (1, 2, 3)] + [at.n1, at.n2, at.sib])
    pl.when(at.z == 3)(lambda: attn.along(3))
    small.start()
    pl.when(at.z == 3)(lambda: attn.z_in(2))
    attn.along(near[0])
    attn.spread(near[0])
    fw_copy.wait()
    fbuf[me + (slice(0, rows),)] = fw_ref[0].astype(bf)
    fbuf[me + (slice(rows, 2 * rows),)] = fw_ref[1].astype(bf)
    small.spread()
    small.forward()
    attn.z_in(near[1])
    attn.along(near[1])
    attn.spread(near[1])
    attn.first_in(near[0])
    pl.when(at.z == 2)(lambda: attn.z_in(3))
    pl.when(at.z == 2)(lambda: attn.along(3))
    small.cross()
    attn.z_in(near[2])
    attn.along(near[2])
    attn.spread(near[2])
    attn.first_in(near[1])
    pl.when(at.z == 1)(lambda: attn.z_in(3))
    pl.when(at.z == 1)(lambda: attn.along(3))
    small.done()
    for i in range(32):
        z, y, x, c = i // 8, (i // 4) % 2, (i // 2) % 2, i % 2
        piece = sbuf[z, y, x, c]
        sm_ref[:, n_small * i : n_small * (i + 1)] = piece[:, 0:n_small].astype(bf).astype(f32)
    for n in range(2):
        bias_ref[n] = column(sm_ref[:, (4 + n) * D : (5 + n) * D])
    ffn.start()
    for layer in range(3):
        attn.own_in(layer)

    def last_z():
        pl.when(at.z == 0)(lambda: attn.z_in(3))
        attn.first(3).start()
        attn.second(3).start()

    def firsts():
        attn.first_in(near[2])
        attn.across(1).start()

    def seconds():
        for layer in near:
            attn.second_in(layer)
        attn.across(2).start()

    def thirds():
        for layer in near:
            attn.third_in(layer)
        attn.across(3).start()

    def last_across():
        attn.second_in(3)
        attn.third_in(3)
        attn.across_last().start()

    def inner(j, n):
        return lambda: pl.when(ffn.inner())(lambda: ffn.z_in(j, n))

    def outer(j, n):
        return lambda: pl.when(jnp.logical_not(ffn.inner()))(lambda: ffn.z_in(j, n))

    def inner_second(j):
        return lambda: pl.when(ffn.inner())(lambda: ffn.second_in(j))

    def outer_second(j):
        return lambda: pl.when(jnp.logical_not(ffn.inner()))(lambda: ffn.second_in(j))

    ticks = {
        (0, 0): [firsts],
        (0, 1): [seconds, lambda: ffn.z_in(1, 0), inner(2, 0)],
        (0, 2): [last_z, ffn.first_in],
        (1, 0): [thirds],
        (1, 1): [inner(3, 0), lambda: attn.first_in(3), outer(2, 0)],
        (1, 2): [inner(1, 1), inner(2, 1)],
        (2, 0): [last_across, outer(1, 1), lambda: ffn.second_in(0)],
        (2, 1): [],
        (2, 2): [inner(3, 1), outer(3, 0)],
        (3, 0): [inner_second(1)],
        (3, 1): [outer_second(1), inner_second(2)],
        (3, 2): [outer(2, 1), lambda: ffn.done(0)],
    }
    x_copy.wait()
    q_rows, k_rows = segment_rows(seg_ref[...])
    for g, (gy, gx) in enumerate(attn.columns):
        if g:
            attn.across_in(g)
        base = (2 * gy + gx) * 2 * rows
        w = abuf[0:3, gy, gx].reshape(6 * rows, D)
        p = dot(w, x_ref[...], NT)
        for sec in range(3):
            part = p[2 * rows * sec : 2 * rows * (sec + 1)]
            if sec != 1:
                part = part + widen(bias_ref[sec // 2, pl.ds(pl.multiple_of(base, HD), 2 * rows), :], t)
            qkv_ref[pl.ds(pl.multiple_of(sec * D + base, HD), 2 * rows), :] = part.astype(bf)

        def head(i, _, g=g, base=base):
            for k in range(3):

                @pl.when(i == k)
                def _(k=k):
                    for event in ticks[g, k]:
                        event()

            h = base // HD + i
            r = rows_at(h, HD)
            q = qkv_ref[r, :] * bf(0.125)
            k = qkv_ref[pl.ds(pl.multiple_of(D + h * HD, HD), HD), :]
            v = qkv_ref[pl.ds(pl.multiple_of(2 * D + h * HD, HD), HD), :]
            s = dot(jnp.concatenate([k, k_rows], 0), jnp.concatenate([q, q_rows], 0), TN)
            top = jnp.max(s, axis=0, keepdims=True)
            e = jnp.exp2((s - top) * LOG2E)
            total = jnp.sum(e, axis=0, keepdims=True)
            o_ref[r, :] = (dot(v, e.astype(bf), NN) * (1.0 / total)).astype(bf)
            l_ref[h] = top + jnp.log(total)
            return 0

        lax.fori_loop(0, 3, head, 0)
    qkv_copy = pltpu.make_async_copy(qkv_ref, qkv_out, local_sem.at[1])
    qkv_copy.start()
    o_copy = pltpu.make_async_copy(o_ref, o_out, local_sem.at[13])
    o_copy.start()
    attn.last_in()
    aout_copy = pltpu.make_async_copy(abuf, aout, local_sem.at[0])
    aout_copy.start()
    for n, i in enumerate((0, 1, 6, 7)):
        vec_ref[n] = column(sm_ref[:, D * i : D * (i + 1)])
    lanes = 256

    def first_norm(i, _):
        cs = rows_at(i, lanes)
        wo = abuf[3].reshape(D, D)
        vec = [widen(vec_ref[n], lanes) for n in range(4)]
        r1 = jnp.transpose(x_ref[cs, :]).astype(f32) + dot(wo, o_ref[:, cs], NN) + vec[2]
        xh, scale = norm(r1)
        xh_ref[:, cs] = xh
        rs_ref[:, cs] = scale
        a1 = xh * vec[0] + vec[1]
        r2_ref[:, cs] = a1 + vec[3]
        low_ref[:, cs] = a1.astype(bf)
        return 0

    lax.fori_loop(0, t // lanes, first_norm, 0)
    xh_copy = pltpu.make_async_copy(xh_ref, xh_out, local_sem.at[2])
    xh_copy.start()
    low_copy = pltpu.make_async_copy(low_ref, low_out, local_sem.at[14])
    low_copy.start()
    half = 4 * rows

    def write_back(j, y):
        slot = (2 * j + y) % 2
        where = pl.ds(pl.multiple_of(ffn.layer[j] * 2 * half + y * half, half), half)
        return [
            pltpu.make_async_copy(act_ref.at[slot], act_out.at[where], local_sem.at[3 + slot]),
            pltpu.make_async_copy(gp_ref.at[slot], gp_out.at[where], local_sem.at[5 + slot]),
        ]

    fout_copies = []
    for j in range(LAYERS):
        layer = ffn.layer[j]
        if j == 1:
            inner_second(3)()
            outer_second(2)()
            outer(3, 1)()
        if j == 2:
            outer_second(3)()
        if j:
            ffn.done(j)
        fout_copies.append(pltpu.make_async_copy(fbuf.at[layer], fout.at[layer], local_sem.at[7 + j]))
        fout_copies[-1].start()
        for y in range(2):
            slot = (2 * j + y) % 2
            w1 = fbuf[layer, y, :, :, 0:rows, :].reshape(half, D)
            w2 = fbuf[layer, y, :, :, rows : 2 * rows, :].reshape(half, D)
            bias = sm_ref[:, pl.ds(pl.multiple_of(8 * D + layer * 2 * half + y * half, 128), half)]
            hid = dot(w1, low_ref[...], NN) + widen(column(bias), t)
            act, slope = gelu_both(hid)
            act = act.astype(bf)
            if 2 * j + y >= 2:
                for copy in write_back((2 * j + y - 2) // 2, y):
                    copy.wait()
            act_ref[slot] = act
            gp_ref[slot] = slope.astype(bf)
            for copy in write_back(j, y):
                copy.start()
            r2_ref[...] += dot(w2, act, TN)
    r2_copy = pltpu.make_async_copy(r2_ref, r2_out, local_sem.at[15])
    r2_copy.start()
    for y in range(2):
        for copy in write_back(LAYERS - 1, y):
            copy.wait()
    attn.drain()
    ffn.drain()
    small.drain()
    for copy in [aout_copy, qkv_copy, xh_copy, o_copy, low_copy, r2_copy] + fout_copies:
        copy.wait()


def forward_call(x, seg, aw, fw, smw):
    t, rows = x.shape[0], aw.shape[0]
    ff = 32 * rows
    n = 32 * smw.shape[1]
    wide = -(-smw.shape[1] // 128) * 128
    vm, anyw = pl.BlockSpec(memory_space=pltpu.VMEM), pl.BlockSpec(memory_space=pl.ANY)
    shape = jax.ShapeDtypeStruct
    sems = pltpu.SemaphoreType.DMA
    return pl.pallas_call(
        forward_kernel,
        name="gather_forward",
        in_specs=[vm] * 3 + [anyw] * 2,
        out_specs=[anyw, anyw, vm, anyw, anyw, vm, anyw, vm, anyw, anyw, anyw, anyw],
        out_shape=[
            shape((4, 2, 2, 2, rows, D), bf), shape((4, 2, 2, 2, 2 * rows, D), bf), shape((1, n), f32),
            shape((3 * D, t), bf), shape((D, t), bf), shape((HEADS, 1, t), f32), shape((D, t), f32),
            shape((1, t), f32), shape((D, t), bf), shape((D, t), f32), shape((ff, t), bf), shape((ff, t), bf),
        ],
        scratch_shapes=[
            pltpu.VMEM((4, 2, 2, 2, rows, D), bf), pltpu.VMEM((4, 2, 2, 2, 2 * rows, D), bf),
            pltpu.VMEM((4, 2, 2, 2, 1, wide), f32),
            pltpu.VMEM((3 * D, t), bf), pltpu.VMEM((D, t), f32), pltpu.VMEM((2, 4 * rows, t), bf),
            pltpu.VMEM((2, 4 * rows, t), bf), pltpu.VMEM((4, D, 128), f32), pltpu.VMEM((2, D, 128), f32),
            pltpu.VMEM((t, D), bf), pltpu.VMEM((2, rows, D), f32), pltpu.VMEM((D, t), bf), pltpu.VMEM((D, t), bf),
            pltpu.VMEM((D, t), f32),
            sems((27,)), sems((24,)), sems((23,)), sems((20,)), sems((7,)), sems((7,)), sems((16,)),
        ],
        compiler_params=pltpu.CompilerParams(
            vmem_limit_bytes=VMEM_LIMIT, collective_id=0, has_side_effects=True
        ),
    )(seg, aw, smw, x, fw)


def norm_back(dy, xh, scale, gain):
    dx = dy * gain
    mean_one = jnp.mean(dx, axis=0, keepdims=True)
    mean_two = jnp.mean(dx * xh, axis=0, keepdims=True)
    return scale * (dx - mean_one - xh * mean_two)


def accumulate(ref, term):
    ref[...] = ref[...] + term[...]


class Scatter:
    def __init__(self, at, layers, own, cross, pair, single, column, send, recv):
        self.at, self.layers, self.own, self.cross, self.pair, self.single = at, layers, own, cross, pair, single
        self.column, self.send, self.recv = column, send, recv
        self.p = (1 - at.c) * at.x + at.c * at.y

    def copy(self, src, dst, kind, layer, peer):
        n = kind * len(self.layers) + self.layers.index(layer)
        return remote(src, dst, self.send.at[n], self.recv.at[n], peer)

    def across(self, layer, src=None):
        dst = self.cross.at[self.layers.index(layer)]
        return self.copy(dst if src is None else src, dst, 0, layer, self.at.sib)

    def far(self, layer):
        dst = self.pair.at[self.layers.index(layer), 1 - self.p]
        return self.copy(self.own(layer, self.at.far_yx), dst, 1, layer, self.at.n2)

    def near(self, layer):
        dst = self.pair.at[self.layers.index(layer), self.p]
        return self.copy(self.own(layer, self.at.n2_yx), dst, 2, layer, self.at.n2)

    def first(self, layer):
        dst = self.single.at[self.layers.index(layer)]
        return self.copy(self.own(layer, self.at.n1_yx), dst, 3, layer, self.at.n1)

    def cross_in(self, layer):
        at, i = self.at, self.layers.index(layer)
        self.across(layer).wait_recv()
        for yx, copy in ((at.far_yx, self.far), (at.n2_yx, self.near), (at.n1_yx, None), ((at.y, at.x), None)):
            accumulate(self.own(layer, yx), self.cross.at[(i,) + yx])
            if copy is not None:
                copy(layer).start()

    def pair_in(self, layer):
        i = self.layers.index(layer)
        self.far(layer).wait_recv()
        accumulate(self.own(layer, self.at.n1_yx), self.pair.at[i, 1 - self.p])
        self.first(layer).start()
        self.near(layer).wait_recv()
        accumulate(self.own(layer, (self.at.y, self.at.x)), self.pair.at[i, self.p])

    def single_in(self, layer):
        self.first(layer).wait_recv()
        own = self.own(layer, (self.at.y, self.at.x))
        total = own[...].astype(f32) + self.single[self.layers.index(layer)].astype(f32)
        self.column[self.layers.index(layer)] = total.astype(bf)

    def drain(self, layer, src):
        self.across(layer, src).wait_send()
        for copy in (self.far, self.near, self.first):
            copy(layer).wait_send()


class Along:
    def __init__(self, at, column, land, send, recv):
        self.at, self.column, self.land, self.send, self.recv = at, column, land, send, recv

    def copy(self, layer):
        return remote(
            self.column.at[layer], self.land.at[self.at.z], self.send.at[layer], self.recv.at[self.at.z],
            self.at.at_layer(layer),
        )

    def start(self, layer):
        pl.when(self.at.z != layer)(lambda: self.copy(layer).start())

    def finish(self):
        total = self.column[self.at.z].astype(f32)
        for d in (1, 2, 3):
            layer = (self.at.z + d) % LAYERS
            ref = self.land.at[layer]
            remote(ref, ref, self.send.at[layer], self.recv.at[layer], self.at.sib).wait_recv()
            total = total + ref[...].astype(f32)
        return total

    def drain(self):
        for layer in range(LAYERS):
            pl.when(self.at.z != layer)(lambda layer=layer: self.copy(layer).wait_send())


VECS = (0, 2, 3)
EARLY = (0, 1)
LATE = (2, 3)


def middle_kernel(
    cot_ref, seg_ref, rs_ref, low_ref, r2_ref, sm_ref, w_ref, act_ref, gp_ref, o_in, xh_in, abuf,
    out_ref, dr1_ref, do_ref, dwo_ref, dw_out, sg_ref, column_ref,
    acc_ref, df_ref, vec_ref, part_ref, stage, cross, pair, single, o_ref, xh_ref, wo_ref,
    send, recv, local_sem,
):
    step = pl.program_id(0)
    t = cot_ref.shape[0]
    rows = w_ref.shape[4] // 2
    half = 4 * rows
    lanes = 256
    at = Place()

    def own(layer, yx):
        return stage.at[(layer,) + yx + (at.c,)]

    def source(layer):
        return stage.at[layer, :, :, 1 - at.c]

    ffn = Scatter(at, EARLY, own, cross, pair, single, column_ref, send, recv)
    late = [pltpu.make_async_copy(stage.at[layer], dw_out.at[layer - 2], local_sem.at[layer - 2]) for layer in LATE]

    tail_inputs = [
        pltpu.make_async_copy(o_in, o_ref, local_sem.at[2]), pltpu.make_async_copy(xh_in, xh_ref, local_sem.at[3]),
        pltpu.make_async_copy(abuf.at[3], wo_ref, local_sem.at[4]),
    ]

    def vec(i):
        return widen(vec_ref[VECS.index(i)], lanes)

    def over_lanes(piece):
        def body(c, _):
            piece(rows_at(c, lanes))
            return 0

        lax.fori_loop(0, t // lanes, body, 0)

    @pl.when(step == 0)
    def _():
        for copy in tail_inputs:
            copy.start()
        greet([at.n1, at.n2, at.sib])
        for n, i in enumerate(VECS):
            vec_ref[n] = column(sm_ref[:, D * i : D * (i + 1)])
        part_ref[...] = jnp.zeros_like(part_ref)

        def second_norm(cs):
            xh, scale = norm(r2_ref[:, cs])
            out_ref[cs, :] = jnp.transpose((xh * vec(2) + vec(3)).astype(bf))
            valid = jnp.where(seg_ref[:, cs] >= 0, 1.0, 0.0)
            dy = jnp.transpose(cot_ref[cs, :]).astype(f32) * valid
            dr = norm_back(dy, xh, scale, vec(2))
            acc_ref[:, cs] = dr
            df_ref[:, cs] = dr.astype(bf)
            part_ref[0] += lane_fold(dy * xh)
            part_ref[1] += lane_fold(dy)
            part_ref[2] += lane_fold(dr)

        over_lanes(second_norm)

    w1 = w_ref[0, 0, :, :, 0:rows, :].reshape(half, D)
    w2 = w_ref[0, 0, :, :, rows : 2 * rows, :].reshape(half, D)
    dh = dot(w2, df_ref[...], NN) * gp_ref[...].astype(f32)
    sg_ref[:, pl.ds(pl.multiple_of(8 * D + step * half, 128), half)] = fold_row(lane_fold(dh))
    low = dh.astype(bf)
    dw2 = dot(act_ref[...], df_ref[...], NT).astype(bf)
    dw1 = dot(low, low_ref[...], NT).astype(bf)

    for x in range(2):
        for c in range(2):
            part = slice((2 * x + c) * rows, (2 * x + c + 1) * rows)
            stage[step // 2, step % 2, x, c, 0:rows, :] = dw1[part]
            stage[step // 2, step % 2, x, c, rows : 2 * rows, :] = dw2[part]
    acc_ref[...] += dot(w1, low, TN)
    events = {
        1: [lambda: ffn.across(0, source(0)).start()],
        2: [lambda: ffn.cross_in(0)],
        3: [lambda: ffn.across(1, source(1)).start()],
        4: [lambda: ffn.pair_in(0), lambda: ffn.cross_in(1)],
        5: [lambda: ffn.single_in(0), late[0].start],
        6: [lambda: ffn.pair_in(1)],
        7: [late[1].start],
    }
    for k, todo in events.items():

        @pl.when(step == k)
        def _(todo=todo):
            for event in todo:
                event()

    @pl.when(step == pl.num_programs(0) - 1)
    def _():
        for copy in tail_inputs:
            copy.wait()
        wo = wo_ref[...].reshape(D, D)

        def first_back(cs):
            dy = acc_ref[:, cs]
            xh = xh_ref[:, cs]
            dr = norm_back(dy, xh, rs_ref[:, cs], vec(0))
            dr1_ref[:, cs] = dr
            dz = dr.astype(bf)
            df_ref[:, cs] = dz
            part_ref[3] += lane_fold(dy * xh)
            part_ref[4] += lane_fold(dy)
            part_ref[5] += lane_fold(dr)
            do_ref[:, cs] = dot(wo, dz, TN).astype(bf)

        over_lanes(first_back)
        dwo_ref[...] = dot(df_ref[...], o_ref[...], NT).astype(bf)
        for n, i in enumerate((2, 3, 7, 0, 1, 6)):
            sg_ref[:, D * i : D * (i + 1)] = fold_row(part_ref[n])
        sg_ref[:, 4 * D : 6 * D] = jnp.zeros((1, 2 * D), f32)
        ffn.single_in(1)
        for copy in late:
            copy.wait()
        for layer in EARLY:
            ffn.drain(layer, source(layer))


def middle_call(cot, seg, o, xh, rs, low, r2, sm, abuf, fbuf, act, gp):
    t = cot.shape[0]
    rf = fbuf.shape[4]
    half = 2 * rf
    shape = jax.ShapeDtypeStruct
    sems = pltpu.SemaphoreType.DMA

    def whole(a):
        return pl.BlockSpec(a.shape, lambda j: (0,) * len(a.shape))

    wspec = pl.BlockSpec((1, 1, 2, 2, rf, D), lambda j: (j // 2, j % 2, 0, 0, 0, 0))
    rspec = pl.BlockSpec((half, t), lambda j: (j, 0))
    outs = [
        shape((t, D), bf), shape((D, t), f32), shape((D, t), bf), shape((D, D), bf),
        shape((2, 2, 2, 2, rf, D), bf), shape(sm.shape, f32), shape((2, rf, D), bf),
    ]
    return pl.pallas_call(
        middle_kernel,
        name="middle_scatter",
        grid=(8,),
        in_specs=[whole(a) for a in (cot, seg, rs, low, r2, sm)]
        + [wspec, rspec, rspec]
        + [pl.BlockSpec(memory_space=pl.ANY)] * 3,
        out_specs=[whole(a) for a in outs[:4]] + [pl.BlockSpec(memory_space=pl.ANY)] + [whole(a) for a in outs[5:]],
        out_shape=outs,
        scratch_shapes=[
            pltpu.VMEM((D, t), f32), pltpu.VMEM((D, t), bf), pltpu.VMEM((3, D, 128), f32),
            pltpu.VMEM((6, D, 128), f32), pltpu.VMEM((4, 2, 2, 2, rf, D), bf), pltpu.VMEM((2, 2, 2, rf, D), bf),
            pltpu.VMEM((2, 2, rf, D), bf), pltpu.VMEM((2, rf, D), bf), pltpu.VMEM((D, t), bf), pltpu.VMEM((D, t), f32),
            pltpu.VMEM(abuf.shape[1:], bf), sems((8,)), sems((8,)), sems((5,)),
        ],
        compiler_params=pltpu.CompilerParams(
            vmem_limit_bytes=VMEM_LIMIT, collective_id=2, has_side_effects=True
        ),
    )(cot, seg, rs, low, r2, sm, fbuf, act, gp, o, xh, abuf)


class ColumnScatter:
    def __init__(self, at, own, cross, pair, single, column, along, send, recv):
        self.at, self.own, self.cross, self.pair, self.single = at, own, cross, pair, single
        self.column, self.along, self.send, self.recv = column, along, send, recv
        self.columns = [(1 - at.y, 1 - at.x), (at.y, 1 - at.x), (1 - at.y, at.x), (at.y, at.x)]

    def part(self, yx, core):
        return self.own.at[(slice(0, 3),) + yx + (core,)]

    def across(self, g):
        yx = self.columns[g]
        return remote(
            self.part(yx, 1 - self.at.c), self.cross.at[(slice(None),) + yx], self.send.at[g], self.recv.at[g],
            self.at.sib,
        )

    def hop(self, kind):
        at = self.at
        yx, dst, peer = (
            (at.far_yx, self.pair.at[0], at.n2), (at.n2_yx, self.pair.at[1], at.n2), (at.n1_yx, self.single, at.n1)
        )[kind]
        return remote(self.part(yx, at.c), dst, self.send.at[4 + kind], self.recv.at[4 + kind], peer)

    def add(self, yx, terms):
        for layer in range(3):
            accumulate(self.own.at[(layer,) + yx + (self.at.c,)], terms(layer))

    def cross_in(self, g):
        yx = self.columns[g]
        self.across(g).wait_recv()
        self.add(yx, lambda layer: self.cross.at[(layer,) + yx])

    def far_out(self):
        self.cross_in(0)
        self.hop(0).start()

    def first_out(self):
        self.hop(0).wait_recv()
        self.add(self.at.n1_yx, lambda layer: self.pair.at[0, layer])
        self.hop(2).start()

    def neighbour_out(self, g):
        self.cross_in(g)
        pl.when(self.at.c == g - 1)(self.first_out)
        pl.when(self.at.c != g - 1)(lambda: self.hop(1).start())

    def own_out(self):
        at = self.at
        self.across(3).wait_recv()
        self.hop(1).wait_recv()
        self.hop(2).wait_recv()
        for layer in range(3):
            total = self.own[layer, at.y, at.x, at.c].astype(f32) + self.cross[layer, at.y, at.x].astype(f32)
            total = total + self.pair[1, layer].astype(f32) + self.single[layer].astype(f32)
            self.column[layer] = total.astype(bf)
            self.along.start(layer)

    def drain(self):
        for g in range(4):
            self.across(g).wait_send()
        for kind in range(3):
            self.hop(kind).wait_send()


class SmallScatter:
    def __init__(self, at, own, cross, pair, single, land, send, recv):
        self.at, self.own, self.cross, self.pair, self.single, self.land = at, own, cross, pair, single, land
        self.send, self.recv = send, recv

    def part(self, yx, core):
        return self.own.at[(slice(None),) + yx + (core,)]

    def across(self):
        at = self.at
        return remote(
            self.own.at[:, :, :, 1 - at.c], self.cross, self.send.at[0], self.recv.at[0], at.sib
        )

    def far(self):
        return remote(self.part(self.at.far_yx, self.at.c), self.pair.at[0], self.send.at[1], self.recv.at[1], self.at.n2)

    def near(self):
        return remote(self.part(self.at.n2_yx, self.at.c), self.pair.at[1], self.send.at[2], self.recv.at[2], self.at.n2)

    def first(self):
        return remote(self.part(self.at.n1_yx, self.at.c), self.single, self.send.at[3], self.recv.at[3], self.at.n1)

    def along(self, d):
        at = self.at
        layer = (at.z + d) % LAYERS
        return remote(
            self.own.at[layer, at.y, at.x, at.c], self.land.at[d], self.send.at[3 + d], self.recv.at[3 + d],
            at.at_layer(layer),
        )

    def cross_in(self):
        at = self.at
        self.across().wait_recv()
        for yx in (at.far_yx, at.n2_yx, at.n1_yx, (at.y, at.x)):
            ref = self.part(yx, at.c)
            ref[...] += self.cross[(slice(None),) + yx]
        self.far().start()
        self.near().start()

    def pair_in(self):
        at = self.at
        self.far().wait_recv()
        ref = self.part(at.n1_yx, at.c)
        ref[...] += self.pair[0]
        self.first().start()
        self.near().wait_recv()
        ref = self.part((at.y, at.x), at.c)
        ref[...] += self.pair[1]

    def single_in(self):
        self.first().wait_recv()
        ref = self.part((self.at.y, self.at.x), self.at.c)
        ref[...] += self.single[...]
        for d in (1, 2, 3):
            self.along(d).start()

    def finish(self):
        at = self.at
        total = self.own[at.z, at.y, at.x, at.c]
        for d in (1, 2, 3):
            self.along(d).wait_recv()
            total = total + self.land[d]
        return total

    def drain(self):
        for copy in (self.across, self.far, self.near, self.first):
            copy().wait_send()
        for d in (1, 2, 3):
            self.along(d).wait_send()


CQ = 512


def backward_kernel(
    seg_ref, l_ref, dwo_ref, sg_ref, early_ref, dwf, abuf, dr1, qkv_in, o_in, do_in, x_in,
    dx, gf_ref, ga_ref, gs_ref,
    g_ref, dwa, w_ref, dr1_ref, dx_ref, small_ref, qkv_ref, o_ref, do_ref, x_ref,
    fown, fcross, fpair, fsingle, fcolumn, fland,
    across_ref, apair, asingle, acolumn, aland, wcross, wpair, wsingle,
    scross, spair, ssingle, sland,
    fsend, frecv, fzsend, fzrecv, asend, arecv, azsend, azrecv, wsend, wrecv, ssend, srecv, local_sem,
):
    t = x_ref.shape[0]
    at = Place()
    rows = w_ref.shape[4]
    n_small = sg_ref.shape[1] // 32
    f_along = Along(at, fcolumn, fland, fzsend, fzrecv)
    a_along = Along(at, acolumn, aland, azsend, azrecv)
    ffn = Scatter(
        at, LATE, lambda layer, yx: fown.at[(layer - 2,) + yx], fcross, fpair, fsingle, fcolumn.at[2:4], fsend, frecv
    )
    last = Scatter(
        at, (3,), lambda layer, yx: dwa.at[(3,) + yx + (at.c,)], wcross, wpair, wsingle, acolumn.at[3:4], wsend, wrecv
    )
    attn = ColumnScatter(at, dwa, across_ref, apair, asingle, acolumn, a_along, asend, arecv)
    small = SmallScatter(at, small_ref, scross, spair, ssingle, sland, ssend, srecv)

    def ffn_source(layer):
        return dwf.at[layer - 2, :, :, 1 - at.c]

    last_source = dwa.at[3, :, :, 1 - at.c]
    inputs = [
        pltpu.make_async_copy(src, dst, local_sem.at[5 + n])
        for n, (src, dst) in enumerate(((qkv_in, qkv_ref), (o_in, o_ref), (do_in, do_ref), (x_in, x_ref)))
    ]
    for copy in inputs:
        copy.start()
    loads = [
        pltpu.make_async_copy(dwf.at[layer - 2, :, :, at.c], fown.at[layer - 2], local_sem.at[layer - 2])
        for layer in LATE
    ]
    for copy in loads:
        copy.start()
    w_copy = pltpu.make_async_copy(abuf.at[0:3], w_ref, local_sem.at[2])
    w_copy.start()
    dr1_copy = pltpu.make_async_copy(dr1, dr1_ref, local_sem.at[3])
    dr1_copy.start()
    fcolumn[0:2] = early_ref[...]
    greet([at.at_layer((at.z + d) % LAYERS) for d in (1, 2, 3)] + [at.n1, at.n2, at.sib])
    for layer in LATE:
        ffn.across(layer, ffn_source(layer)).start()
    for y in range(2):
        for x in range(2):
            for c in range(2):
                i = y * 4 + x * 2 + c
                dwa[3, y, x, c] = dwo_ref[i * rows : (i + 1) * rows]
    last.across(3, last_source).start()
    for layer in EARLY:
        f_along.start(layer)

    def ffn_cross(layer):
        loads[layer - 2].wait()
        ffn.cross_in(layer)

    def ffn_single(layer):
        ffn.single_in(layer)
        f_along.start(layer)

    def last_single():
        last.single_in(3)
        a_along.start(3)

    ticks = {
        (0, 1): [lambda: ffn_cross(2)],
        (0, 2): [lambda: ffn_cross(3)],
        (1, 1): [lambda: ffn.pair_in(2), attn.far_out],
        (1, 2): [lambda: last.cross_in(3)],
        (2, 0): [lambda: ffn.pair_in(3)],
        (2, 1): [lambda: ffn_single(2), lambda: attn.neighbour_out(1)],
        (2, 2): [lambda: last.pair_in(3)],
        (3, 0): [lambda: ffn_single(3)],
        (3, 1): [lambda: attn.neighbour_out(2), last_single],
    }
    for copy in inputs:
        copy.wait()
    q_rows, k_rows = segment_rows(seg_ref[...])
    for g, (gy, gx) in enumerate(attn.columns):
        base = (2 * gy + gx) * 2 * rows

        def head(i, _, g=g, base=base):
            for k in range(3):
                if (g, k) in ticks:

                    @pl.when(i == k)
                    def _(k=k):
                        for event in ticks[g, k]:
                            event()

            h = base // HD + i
            hrows = rows_at(h, HD)
            krow = pl.ds(pl.multiple_of(D + h * HD, HD), HD)
            vrow = pl.ds(pl.multiple_of(2 * D + h * HD, HD), HD)
            q, k, v, do = qkv_ref[hrows, :], qkv_ref[krow, :], qkv_ref[vrow, :], do_ref[hrows, :]
            inner = jnp.sum(do.astype(f32) * o_ref[hrows, :].astype(f32), axis=0, keepdims=True)
            lrow = l_ref[h]
            keys = jnp.concatenate([k, k_rows], 0)
            queries = jnp.concatenate([q * bf(0.125), q_rows], 0)
            dv = dk = 0.0
            for n in range(t // CQ):
                cs = slice(n * CQ, (n + 1) * CQ)
                s = dot(keys, queries[:, cs], TN)
                p = jnp.exp2((s - lrow[:, cs]) * LOG2E)
                dp = dot(v, do[:, cs], TN)
                ds = (p * (dp - inner[:, cs])).astype(bf)
                dv = dv + dot(do[:, cs], p.astype(bf), NT)
                dk = dk + dot(q[:, cs], ds, NT)
                g_ref[hrows, cs] = (dot(k, ds, NN) * 0.125).astype(bf)
            g_ref[vrow, :] = dv.astype(bf)
            g_ref[krow, :] = (dk * 0.125).astype(bf)
            return 0

        lax.fori_loop(0, 3, head, 0)
        if g == 3:
            sums = [sg_ref[:, 0 : 4 * D]]
            for sec in (0, 2):
                sums.append(fold_row(lane_fold(g_ref[sec * D : (sec + 1) * D, :].astype(f32))))
            sums = jnp.concatenate(sums + [sg_ref[:, 6 * D :]], axis=1)
            pad = jnp.zeros((1, small_ref.shape[-1] - n_small), f32)
            for i in range(32):
                z, y, x, c = i // 8, (i // 4) % 2, (i // 2) % 2, i % 2
                small_ref[z, y, x, c] = jnp.concatenate([sums[:, i * n_small : (i + 1) * n_small], pad], axis=1)
            small.across().start()
        for sec in range(3):
            grad = g_ref[pl.ds(pl.multiple_of(sec * D + base, HD), 2 * rows), :]
            dw = dot(grad, x_ref[...], NN).astype(bf)
            for c in range(2):
                dwa[sec, gy, gx, c] = dw[c * rows : (c + 1) * rows]
        attn.across(g).start()
    small.cross_in()
    attn.own_out()
    w_copy.wait()
    dr1_copy.wait()
    lanes = 256

    def input_block(i, _):
        cs = rows_at(i, lanes)
        w = w_ref[...].reshape(3 * D, D)
        dx_ref[cs, :] = jnp.transpose(dr1_ref[:, cs]) + dot(g_ref[:, cs], w, TN)
        return 0

    lax.fori_loop(0, 1, input_block, 0)
    small.pair_in()
    lax.fori_loop(1, 3, input_block, 0)
    small.single_in()
    lax.fori_loop(3, t // lanes, input_block, 0)
    dx_copy = pltpu.make_async_copy(dx_ref, dx, local_sem.at[4])
    dx_copy.start()
    gf_ref[...] = f_along.finish()
    ga_ref[...] = a_along.finish()
    gs_ref[...] = small.finish()
    for layer in LATE:
        ffn.drain(layer, ffn_source(layer))
    last.drain(3, last_source)
    for stage in (attn, f_along, a_along, small):
        stage.drain()
    dx_copy.wait()


def backward_call(x, seg, qkv, o, logs, do, dwo, sg, early, dwf, abuf, dr1):
    t = x.shape[0]
    ra, rf = abuf.shape[4], dwf.shape[4]
    wide = -(-(sg.shape[1] // 32) // 128) * 128
    vm, anyw = pl.BlockSpec(memory_space=pltpu.VMEM), pl.BlockSpec(memory_space=pl.ANY)
    shape = jax.ShapeDtypeStruct
    sems = pltpu.SemaphoreType.DMA

    def half(*dims):
        return pltpu.VMEM(dims + (D,), bf)

    def small(*dims):
        return pltpu.VMEM(dims + (1, wide), f32)

    return pl.pallas_call(
        backward_kernel,
        name="backward_scatter",
        in_specs=[vm] * 5 + [anyw] * 7,
        out_specs=[anyw, vm, vm, vm],
        out_shape=[shape((t, D), f32), shape((rf, D), f32), shape((ra, D), f32), shape((1, wide), f32)],
        scratch_shapes=[
            pltpu.VMEM((3 * D, t), bf), half(4, 2, 2, 2, ra), half(3, 2, 2, 2, ra), pltpu.VMEM((D, t), f32),
            pltpu.VMEM((t, D), f32), small(4, 2, 2, 2),
            pltpu.VMEM((3 * D, t), bf), pltpu.VMEM((D, t), bf), pltpu.VMEM((D, t), bf), pltpu.VMEM((t, D), bf),
            half(2, 2, 2, rf), half(2, 2, 2, rf), half(2, 2, rf), half(2, rf), half(4, rf), half(4, rf),
            half(3, 2, 2, ra), half(2, 3, ra), half(3, ra), half(4, ra), half(4, ra), half(1, 2, 2, ra),
            half(1, 2, ra), half(1, ra),
            small(4, 2, 2), small(2, 4), small(4), small(4),
            sems((8,)), sems((8,)), sems((4,)), sems((4,)), sems((7,)), sems((7,)), sems((4,)), sems((4,)),
            sems((4,)), sems((4,)), sems((7,)), sems((7,)), sems((9,)),
        ],
        compiler_params=pltpu.CompilerParams(
            vmem_limit_bytes=VMEM_LIMIT, collective_id=1, has_side_effects=True
        ),
    )(seg, logs, dwo, sg, early, dwf, abuf, dr1, qkv, o, do, x)


def gradients_block(features, cotangent, segment_ids, attn_weights, ffn_weights, small_params):
    t, rows = features.shape[0], attn_weights.shape[0]
    seg = segment_ids.reshape(1, t)
    abuf, fbuf, sm, qkv, o, logs, xh, rs, low, r2, act, gp = forward_call(
        features, seg, attn_weights, ffn_weights, small_params.reshape(1, -1)
    )
    outputs, dr1, do, dwo, dwf, sg, early = middle_call(cotangent, seg, o, xh, rs, low, r2, sm, abuf, fbuf, act, gp)
    input_grad, gf, ga, gs = backward_call(
        features, seg, qkv, o, logs, do, dwo, sg, early, dwf, abuf, dr1
    )
    return outputs, input_grad, ga, gf.reshape(2, rows, D), gs[0, : small_params.shape[0]]


def local(
    gradients,
    features, cotangent, segment_ids, attn_weights, ffn_weights, small_params,
    attn_first, ffn_first, small_first, attn_second, ffn_second, small_second,
    attn_ema, ffn_ema, small_ema,
):
    outputs, input_grad, attn_sum, ffn_sum, small_sum = gradients(
        features, cotangent, segment_ids, attn_weights, ffn_weights, small_params
    )
    attn = adam_step(attn_weights, attn_sum, attn_first, attn_second, attn_ema, 0.01, 0.05)
    ffn = adam_step(ffn_weights, ffn_sum, ffn_first, ffn_second, ffn_ema, 0.01, 0.05)
    small = adam_step(small_params, small_sum, small_first, small_second, small_ema, 0.0, 0.3)
    return (outputs, input_grad) + tuple(x for trio in zip(attn, ffn, small) for x in trio)


def solution(mesh):
    block = mesh.shape["dp"] == 8 and mesh.shape["fsdp"] == 4
    gradients = gradients_block if block else gradients_general
    row = P(("dp", "fsdp"), None)
    wide = P(None, ("dp", "fsdp"), None)
    flat = P(("dp", "fsdp"))
    state = (row, wide, flat)
    return jax.shard_map(
        partial(local, gradients),
        mesh=mesh,
        in_specs=(row, row, flat) + state * 4,
        out_specs=(row, row) + state * 4,
        check_vma=False,
    )
```

```python
from functools import partial

import jax
import jax.numpy as jnp
from jax import lax
from jax.experimental import pallas as pl
from jax.experimental.pallas import tpu as pltpu
from jax.sharding import PartitionSpec as P

D = 768
HEADS = 12
HD = D // HEADS
STEP = 10
LOG2E = 1.4426950408889634
INV_SQRT2 = 0.7071067811865476
INV_SQRT2PI = 0.3989422804014327
BIG = 2.0**30
VMEM_LIMIT = 60 * 1024 * 1024

bf = jnp.bfloat16
f32 = jnp.float32
TN = (((0,), (0,)), ((), ()))
NN = (((1,), (0,)), ((), ()))
NT = (((1,), (1,)), ((), ()))


def dot(left, right, dims):
    return lax.dot_general(left, right, dims, preferred_element_type=f32)


def rows_at(i, size):
    return pl.ds(pl.multiple_of(i * size, size), size)


def column(row):
    return jnp.transpose(jnp.broadcast_to(row, (128, row.shape[1])))


def widen(col, width):
    return jnp.concatenate([col] * (width // 128), axis=1) if width > 128 else col


def lane_fold(x):
    total = x[:, :128]
    for i in range(1, x.shape[1] // 128):
        total = total + x[:, 128 * i : 128 * (i + 1)]
    return total


def fold_row(part):
    return jnp.sum(jnp.transpose(part), axis=0, keepdims=True)


def segment_rows(seg):
    ids = lax.broadcasted_iota(jnp.int32, (16, seg.shape[1]), 0) - 1
    same = jnp.where(ids == seg, 1.0, 0.0)
    return ((same - 1.0) * BIG).astype(bf), same.astype(bf)


def plain_forward_kernel(x_ref, seg_ref, w_ref, sm_ref, qkv_ref, o_ref, l_ref):
    t = x_ref.shape[0]
    block = 256

    def project_block(i, _):
        rows = rows_at(i, block)
        sec = i // (D // block)
        off = i - sec * (D // block)
        bias = sm_ref[:, pl.ds(pl.multiple_of((4 + sec // 2) * D + off * block, block), block)]
        keep = jnp.where(sec == 1, 0.0, 1.0)
        col = column(bias.astype(f32) * keep)
        qkv_ref[rows, :] = (dot(w_ref[rows, :], x_ref[...], NT) + widen(col, t)).astype(bf)
        return 0

    lax.fori_loop(0, 3 * D // block, project_block, 0)
    q_rows, k_rows = segment_rows(seg_ref[...])

    def head(h, _):
        rows = rows_at(h, HD)
        q = qkv_ref[rows, :] * bf(0.125)
        k = qkv_ref[pl.ds(pl.multiple_of(D + h * HD, HD), HD), :]
        v = qkv_ref[pl.ds(pl.multiple_of(2 * D + h * HD, HD), HD), :]
        s = dot(jnp.concatenate([k, k_rows], 0), jnp.concatenate([q, q_rows], 0), TN)
        top = jnp.max(s, axis=0, keepdims=True)
        e = jnp.exp2((s - top) * LOG2E)
        total = jnp.sum(e, axis=0, keepdims=True)
        o_ref[rows, :] = (dot(v, e.astype(bf), NN) * (1.0 / total)).astype(bf)
        l_ref[h] = top + jnp.log(total)
        return 0

    lax.fori_loop(0, HEADS, head, 0)


def gelu_both(h):
    cdf = 0.5 + 0.5 * lax.erf(h * INV_SQRT2)
    pdf = jnp.exp(h * h * -0.5) * INV_SQRT2PI
    return h * cdf, cdf + h * pdf


PLAIN_VECS = (0, 1, 2, 3, 6, 7)


def plain_middle_kernel(
    x_ref, o_ref, cot_ref, seg_ref, wo_ref, w1_ref, w2_ref, sm_ref,
    out_ref, dr1_ref, do_ref, dwo_ref, dw1_ref, dw2_ref, sg_ref,
    a1_ref, xh_ref, act_ref, gp_ref, rs_ref, low_ref, df_ref, vec_ref, part_ref,
):
    t = x_ref.shape[0]
    ff = w1_ref.shape[0]
    block, lanes = 256, 256
    for n, i in enumerate(PLAIN_VECS):
        vec_ref[n] = column(sm_ref[:, D * i : D * (i + 1)].astype(f32))
    part_ref[...] = jnp.zeros_like(part_ref)

    def vec(i):
        return widen(vec_ref[PLAIN_VECS.index(i)], lanes)

    def over_lanes(step):
        def body(c, _):
            step(rows_at(c, lanes))
            return 0

        lax.fori_loop(0, t // lanes, body, 0)

    def norm(r):
        centre = r - jnp.mean(r, axis=0, keepdims=True)
        scale = lax.rsqrt(jnp.mean(centre * centre, axis=0, keepdims=True) + 1e-5)
        return centre * scale, scale

    def norm_back(dy, xh, scale, gain):
        dx = dy * gain
        mean_one = jnp.mean(dx, axis=0, keepdims=True)
        mean_two = jnp.mean(dx * xh, axis=0, keepdims=True)
        return scale * (dx - mean_one - xh * mean_two)

    def first_norm(cs):
        r1 = jnp.transpose(x_ref[cs, :]).astype(f32) + dot(wo_ref[...], o_ref[:, cs], NN) + vec(6)
        xh, scale = norm(r1)
        xh_ref[:, cs] = xh
        rs_ref[:, cs] = scale
        a1 = xh * vec(0) + vec(1)
        a1_ref[:, cs] = a1 + vec(7)
        low_ref[:, cs] = a1.astype(bf)

    over_lanes(first_norm)

    def up_down(j, _):
        rows = rows_at(j, block)
        bias = sm_ref[:, pl.ds(pl.multiple_of(8 * D + j * block, block), block)]
        hid = dot(w1_ref[rows, :], low_ref[...], NN) + widen(column(bias.astype(f32)), t)
        act, slope = gelu_both(hid)
        act = act.astype(bf)
        act_ref[rows, :] = act
        gp_ref[rows, :] = slope.astype(gp_ref.dtype)
        a1_ref[...] += dot(w2_ref[rows, :], act, TN)
        return 0

    lax.fori_loop(0, ff // block, up_down, 0)

    def second_norm(cs):
        xh, scale = norm(a1_ref[:, cs])
        out_ref[cs, :] = jnp.transpose((xh * vec(2) + vec(3)).astype(bf))
        valid = jnp.where(seg_ref[:, cs] >= 0, 1.0, 0.0)
        dy = jnp.transpose(cot_ref[cs, :]).astype(f32) * valid
        dr = norm_back(dy, xh, scale, vec(2))
        a1_ref[:, cs] = dr
        df_ref[:, cs] = dr.astype(bf)
        part_ref[0] += lane_fold(dy * xh)
        part_ref[1] += lane_fold(dy)
        part_ref[2] += lane_fold(dr)

    over_lanes(second_norm)

    def back(j, _):
        rows = rows_at(j, block)
        dh = dot(w2_ref[rows, :], df_ref[...], NN) * gp_ref[rows, :].astype(f32)
        sg_ref[:, pl.ds(pl.multiple_of(8 * D + j * block, block), block)] = fold_row(lane_fold(dh))
        low = dh.astype(bf)
        dw2_ref[rows, :] = dot(act_ref[rows, :], df_ref[...], NT).astype(dw2_ref.dtype)
        dw1_ref[rows, :] = dot(low, low_ref[...], NT).astype(dw1_ref.dtype)
        a1_ref[...] += dot(w1_ref[rows, :], low, TN)
        return 0

    lax.fori_loop(0, ff // block, back, 0)

    def first_back(cs):
        dy = a1_ref[:, cs]
        xh = xh_ref[:, cs]
        dr = norm_back(dy, xh, rs_ref[:, cs], vec(0))
        dr1_ref[:, cs] = dr
        dz = dr.astype(bf)
        low_ref[:, cs] = dz
        part_ref[3] += lane_fold(dy * xh)
        part_ref[4] += lane_fold(dy)
        part_ref[5] += lane_fold(dr)
        do_ref[:, cs] = dot(wo_ref[...], dz, TN).astype(bf)

    over_lanes(first_back)
    dwo_ref[...] = dot(low_ref[...], o_ref[...], NT).astype(dwo_ref.dtype)
    for n, i in enumerate((2, 3, 7, 0, 1, 6)):
        sg_ref[:, D * i : D * (i + 1)] = fold_row(part_ref[n])
    sg_ref[:, 4 * D : 6 * D] = jnp.zeros((1, 2 * D), f32)


def plain_backward_kernel(
    x_ref, seg_ref, w_ref, qkv_ref, o_ref, l_ref, do_ref, dr1_ref,
    dx_ref, dw_ref, db_ref,
    g_ref,
):
    t = x_ref.shape[0]
    q_rows, k_rows = segment_rows(seg_ref[...])

    def head(h, _):
        rows = rows_at(h, HD)
        krow = pl.ds(pl.multiple_of(D + h * HD, HD), HD)
        vrow = pl.ds(pl.multiple_of(2 * D + h * HD, HD), HD)
        q, k, v, do = qkv_ref[rows, :], qkv_ref[krow, :], qkv_ref[vrow, :], do_ref[rows, :]
        inner = jnp.sum(do.astype(f32) * o_ref[rows, :].astype(f32), axis=0, keepdims=True)
        s = dot(
            jnp.concatenate([k, k_rows], 0), jnp.concatenate([q * bf(0.125), q_rows], 0), TN
        )
        p = jnp.exp2((s - l_ref[h]) * LOG2E)
        dp = dot(v, do, TN)
        ds = (p * (dp - inner)).astype(bf)
        g_ref[vrow, :] = dot(do, p.astype(bf), NT).astype(bf)
        g_ref[krow, :] = (dot(q, ds, NT) * 0.125).astype(bf)
        g_ref[rows, :] = (dot(k, ds, NN) * 0.125).astype(bf)
        return 0

    lax.fori_loop(0, HEADS, head, 0)
    block = 256

    def weight_block(i, _):
        rows = rows_at(i, block)
        g = g_ref[rows, :]
        dw_ref[rows, :] = dot(g, x_ref[...], NN).astype(dw_ref.dtype)
        db_ref[:, rows] = fold_row(lane_fold(g.astype(f32)))
        return 0

    lax.fori_loop(0, 3 * D // block, weight_block, 0)

    def input_block(i, _):
        rows = rows_at(i, block)
        dx_ref[rows, :] = jnp.transpose(dr1_ref[:, rows]) + dot(g_ref[:, rows], w_ref[...], TN)
        return 0

    lax.fori_loop(0, t // block, input_block, 0)


def call(kernel, name, outs, scratch, *args):
    return pl.pallas_call(
        kernel,
        out_shape=[jax.ShapeDtypeStruct(s, d) for s, d in outs],
        scratch_shapes=[pltpu.VMEM(s, d) for s, d in scratch],
        compiler_params=pltpu.CompilerParams(vmem_limit_bytes=VMEM_LIMIT),
        name=name,
    )(*args)


def adam_step(weight, grad_sum, first_mom, second_mom, average, decay, rate):
    first_new = 0.9 * first_mom + 0.1 * grad_sum
    second_new = 0.98 * second_mom + 0.02 * grad_sum * grad_sum
    corrected = first_new / (1.0 - 0.9**STEP)
    denominator = jnp.sqrt(second_new / (1.0 - 0.98**STEP)) + 1e-06
    weight_new = weight - rate * (corrected / denominator + decay * weight)
    average_new = 0.75 * average + 0.25 * weight_new
    return (weight_new, first_new, second_new, average_new)


def gradients_general(features, cotangent, segment_ids, attn_weights, ffn_weights, small_params):
    axes = ("dp", "fsdp")
    t = features.shape[0]
    attn_full = lax.all_gather(attn_weights.astype(bf), axes, axis=0, tiled=True)
    ffn_full = lax.all_gather(ffn_weights.astype(bf), axes, axis=1, tiled=True)
    small_full = lax.all_gather(small_params.astype(bf), axes, axis=0, tiled=True)
    ff = ffn_full.shape[1]
    smalls = small_full.reshape(1, -1)
    seg = segment_ids.reshape(1, t)
    qkv, mixed, logs = call(
        plain_forward_kernel, "attend_forward",
        [((3 * D, t), bf), ((D, t), bf), ((HEADS, 1, t), f32)], [],
        features, seg, attn_full[: 3 * D], smalls,
    )
    outputs, dr1, do, dwo, dw1, dw2, small_grad = call(
        plain_middle_kernel, "plain_middle",
        [((t, D), bf), ((D, t), f32), ((D, t), bf), ((D, D), bf), ((ff, D), bf), ((ff, D), bf),
         ((1, smalls.shape[1]), f32)],
        [((D, t), f32), ((D, t), f32), ((ff, t), bf), ((ff, t), bf), ((1, t), f32), ((D, t), bf),
         ((D, t), bf), ((6, D, 128), f32), ((6, D, 128), f32)],
        features, mixed, cotangent, seg, attn_full[3 * D :], ffn_full[0], ffn_full[1], smalls,
    )
    input_grad, dqkv, bias_grad = call(
        plain_backward_kernel, "attend_backward",
        [((t, D), f32), ((3 * D, D), bf), ((1, 3 * D), f32)], [((3 * D, t), bf)],
        features, seg, attn_full[: 3 * D], qkv, mixed, logs, do, dr1,
    )
    small_grad = small_grad.reshape(-1)
    small_grad = jnp.concatenate(
        [small_grad[: 4 * D], bias_grad[0, :D], bias_grad[0, 2 * D :], small_grad[6 * D :]]
    )
    attn_sum, ffn_sum, small_sum = (
        lax.psum_scatter(jnp.concatenate([dqkv, dwo]), axes, scatter_dimension=0, tiled=True),
        lax.psum_scatter(jnp.stack([dw1, dw2]), axes, scatter_dimension=1, tiled=True),
        lax.psum_scatter(small_grad, axes, scatter_dimension=0, tiled=True),
    )
    return outputs, input_grad, attn_sum.astype(f32), ffn_sum.astype(f32), small_sum


MESH = pl.DeviceIdType.MESH
LAYERS = 4


class Place:
    def __init__(self):
        zy, xc = lax.axis_index("dp"), lax.axis_index("fsdp")
        self.z, self.y, self.x, self.c = zy // 2, zy % 2, xc // 2, xc % 2
        z, y, x, c = self.z, self.y, self.x, self.c
        self.n1 = (z * 2 + (y + c) % 2, ((x + 1 - c) % 2) * 2 + c)
        self.n2 = (z * 2 + (y + 1 - c) % 2, ((x + c) % 2) * 2 + c)
        self.sib = (z * 2 + y, x * 2 + 1 - c)
        self.n1_yx = ((y + c) % 2, (x + 1 - c) % 2)
        self.n2_yx = ((y + 1 - c) % 2, (x + c) % 2)
        self.far_yx = (1 - y, 1 - x)
        self.is_z = ((3 - z) // 3, (z % 2) * (1 - z // 2), ((z + 1) % 2) * (z // 2), z // 3)

    def pick(self, table):
        return sum(t * e for t, e in zip(table, self.is_z) if t)

    def at_layer(self, layer):
        return (layer * 2 + self.y, self.x * 2 + self.c)


def greet(peers):
    barrier = pltpu.get_barrier_semaphore()
    for peer in peers:
        pl.semaphore_signal(barrier, inc=1, device_id=peer, device_id_type=MESH)
    pl.semaphore_wait(barrier, len(peers))


def remote(src, dst, send, recv, peer):
    return pltpu.make_async_remote_copy(
        src_ref=src, dst_ref=dst, send_sem=send, recv_sem=recv, device_id=peer, device_id_type=MESH
    )


class Gather:
    NEAR = ((0, 1, 2, 3), (1, 0, 1, 2), (2, 2, 3, 1), (3, 3, 0, 0))
    ONWARD = (None, (0, 2, 3, 0), (0, 0, 1, 0), (0, 0, 3, 0))

    def __init__(self, at, buf, send, recv):
        self.at, self.buf, self.send, self.recv = at, buf, send, recv
        self.layer = [at.pick(t) for t in self.NEAR]
        self.columns = [(at.y, at.x), at.n1_yx, at.n2_yx, at.far_yx]

    def copy(self, idx, src, dst, peer):
        ref = self.buf.at[idx]
        return remote(ref, ref, self.send.at[src], self.recv.at[dst], peer)

    def slot(self, layer, column):
        return (layer,) + self.columns[column] + (self.at.c,)

    def up(self, column):
        at = self.at
        return self.copy(self.slot(at.z, column), column, 4 * column + at.z, at.at_layer((at.z + 1) % LAYERS))

    def down(self, column):
        at = self.at
        return self.copy(
            self.slot(at.z, column), 2 + column, 4 * column + at.z, at.at_layer((at.z + LAYERS - 1) % LAYERS)
        )

    def onward(self, j, column):
        layer = self.layer[j]
        return self.copy(
            self.slot(layer, column), 3 + j + 3 * column, 4 * column + layer,
            self.at.at_layer(self.at.pick(self.ONWARD[j])),
        )

    def first(self):
        return self.copy(self.slot(self.at.z, 0), 10, 4 + self.at.z, self.at.n1)

    def second(self, j, column):
        layer = self.layer[j]
        return self.copy(self.slot(layer, column), 11 + 4 * column + j, 8 + 4 * column + layer, self.at.n2)

    def across(self, j):
        layer = self.layer[j]
        return self.copy((layer, slice(None), slice(None), self.at.c), 19 + j, 16 + layer, self.at.sib)

    def arrived(self, idx, dst):
        self.copy(idx, 0, dst, self.at.sib).wait_recv()

    def spread(self, column):
        pl.when(self.at.z < LAYERS - 1)(lambda: self.up(column).start())
        pl.when(self.at.z > 0)(lambda: self.down(column).start())
        self.second(0, column).start()

    def start(self):
        self.first().start()
        self.spread(0)

    def inner(self):
        return (self.at.z + 1) // 2 == 1

    def first_in(self):
        self.arrived(self.slot(self.at.z, 1), 4 + self.at.z)
        self.spread(1)

    def z_in(self, j, column):
        layer = self.layer[j]
        self.arrived(self.slot(layer, column), 4 * column + layer)
        pl.when(self.inner())(lambda: self.onward(j, column).start())
        self.second(j, column).start()

    def second_in(self, j):
        layer = self.layer[j]
        self.arrived(self.slot(layer, 2), 8 + layer)
        self.arrived(self.slot(layer, 3), 12 + layer)
        self.across(j).start()

    def done(self, j):
        layer = self.layer[j]
        self.arrived((layer, slice(None), slice(None), 1 - self.at.c), 16 + layer)

    def drain(self):
        self.first().wait_send()
        for n in range(2):
            pl.when(self.at.z < LAYERS - 1)(lambda n=n: self.up(n).wait_send())
            pl.when(self.at.z > 0)(lambda n=n: self.down(n).wait_send())
            for j in range(1, LAYERS):
                pl.when(self.inner())(lambda j=j, n=n: self.onward(j, n).wait_send())
            for j in range(LAYERS):
                self.second(j, n).wait_send()
        for j in range(LAYERS):
            self.across(j).wait_send()


class ColumnGather:
    NEAR = ((0, 1, 2, 2), (1, 0, 1, 1), (2, 2, 0, 0))

    def __init__(self, at, buf, send, recv):
        self.at, self.buf, self.send, self.recv = at, buf, send, recv
        self.near = [at.pick(t) for t in self.NEAR]
        self.columns = [(at.y, at.x), at.n1_yx, at.n2_yx, at.far_yx]

    def copy(self, idx, src, dst, peer):
        ref = self.buf.at[idx]
        return pltpu.make_async_remote_copy(
            src_ref=ref, dst_ref=ref, send_sem=self.send.at[src], recv_sem=self.recv.at[dst],
            device_id=peer, device_id_type=MESH,
        )

    def slot(self, layer, column, core=None):
        return (layer,) + self.columns[column] + (self.at.c if core is None else core,)

    def up(self, layer):
        return self.copy(self.slot(layer, 0), layer, layer, self.at.at_layer((self.at.z + 1) % LAYERS))

    def down(self, layer):
        return self.copy(
            self.slot(layer, 0), 4 + layer, layer, self.at.at_layer((self.at.z + LAYERS - 1) % LAYERS)
        )

    def first(self, layer):
        return self.copy(self.slot(layer, 0), 8 + layer, 4 + layer, self.at.n1)

    def second(self, layer):
        return self.copy(self.slot(layer, 0), 12 + layer, 8 + layer, self.at.n2)

    def third(self, layer):
        return self.copy(self.slot(layer, 1), 16 + layer, 12 + layer, self.at.n2)

    def own(self, layer):
        return self.copy(self.slot(layer, 0), 20 + layer, 16 + layer, self.at.sib)

    def across(self, column):
        y, x = self.columns[column]
        return self.copy((slice(0, 3), y, x, self.at.c), 23 + column, 20 + 2 * y + x, self.at.sib)

    def across_last(self):
        return self.copy((3, slice(None), slice(None), self.at.c), 23, 19, self.at.sib)

    def arrived(self, idx, dst):
        self.copy(idx, 0, dst, self.at.sib).wait_recv()

    def goes_up(self, layer):
        return jnp.logical_and(self.at.z >= layer, self.at.z < LAYERS - 1)

    def goes_down(self, layer):
        return jnp.logical_and(self.at.z <= layer, self.at.z > 0)

    def along(self, layer):
        pl.when(self.goes_up(layer))(lambda: self.up(layer).start())
        pl.when(self.goes_down(layer))(lambda: self.down(layer).start())

    def spread(self, layer):
        self.own(layer).start()
        self.first(layer).start()
        self.second(layer).start()

    def z_in(self, layer):
        self.arrived(self.slot(layer, 0), layer)

    def first_in(self, layer):
        self.arrived(self.slot(layer, 1), 4 + layer)
        self.third(layer).start()

    def second_in(self, layer):
        self.arrived(self.slot(layer, 2), 8 + layer)

    def third_in(self, layer):
        self.arrived(self.slot(layer, 3), 12 + layer)

    def own_in(self, layer):
        self.arrived(self.slot(layer, 0, 1 - self.at.c), 16 + layer)

    def across_in(self, column):
        y, x = self.columns[column]
        self.arrived((slice(0, 3), y, x, 1 - self.at.c), 20 + 2 * y + x)

    def last_in(self):
        self.arrived((3, slice(None), slice(None), 1 - self.at.c), 19)

    def drain(self):
        for layer in range(LAYERS):
            pl.when(self.goes_up(layer))(lambda layer=layer: self.up(layer).wait_send())
            pl.when(self.goes_down(layer))(lambda layer=layer: self.down(layer).wait_send())
            self.first(layer).wait_send()
            self.second(layer).wait_send()
            self.third(layer).wait_send()
        for n in range(3):
            self.own(n).wait_send()
            self.across(n + 1).wait_send()
        self.across_last().wait_send()


class SmallGather:
    def __init__(self, at, buf, send, recv):
        self.at, self.buf, self.send, self.recv = at, buf, send, recv

    def copy(self, idx, src, dst, peer):
        ref = self.buf.at[idx]
        return pltpu.make_async_remote_copy(
            src_ref=ref, dst_ref=ref, send_sem=self.send.at[src], recv_sem=self.recv.at[dst],
            device_id=peer, device_id_type=MESH,
        )

    def along(self, d):
        at = self.at
        return self.copy((at.z, at.y, at.x, at.c), d - 1, d - 1, at.at_layer((at.z + d) % LAYERS))

    def first(self):
        return self.copy((slice(None), self.at.y, self.at.x, self.at.c), 3, 3, self.at.n1)

    def second(self):
        return self.copy((slice(None), self.at.y, self.at.x, self.at.c), 4, 4, self.at.n2)

    def third(self):
        return self.copy((slice(None),) + self.at.n1_yx + (self.at.c,), 5, 5, self.at.n2)

    def across(self):
        return self.copy((slice(None), slice(None), slice(None), self.at.c), 6, 6, self.at.sib)

    def start(self):
        for d in (1, 2, 3):
            self.along(d).start()

    def spread(self):
        for d in (1, 2, 3):
            self.along(d).wait_recv()
        self.first().start()
        self.second().start()

    def forward(self):
        self.first().wait_recv()
        self.third().start()

    def cross(self):
        self.second().wait_recv()
        self.third().wait_recv()
        self.across().start()

    def done(self):
        self.across().wait_recv()

    def drain(self):
        for d in (1, 2, 3):
            self.along(d).wait_send()
        for copy in (self.first, self.second, self.third, self.across):
            copy().wait_send()


def norm(r):
    centre = r - jnp.mean(r, axis=0, keepdims=True)
    scale = lax.rsqrt(jnp.mean(centre * centre, axis=0, keepdims=True) + 1e-5)
    return centre * scale, scale


def forward_kernel(
    seg_ref, aw_ref, smw_ref, x, fw,
    aout, fout, sm_ref, qkv_out, o_out, l_ref, xh_out, rs_ref, low_out, r2_out, act_out, gp_out,
    abuf, fbuf, sbuf, qkv_ref, xh_ref, act_ref, gp_ref, vec_ref, bias_ref, x_ref, fw_ref, o_ref, low_ref, r2_ref,
    asend, arecv, fsend, frecv, ssend, srecv, local_sem,
):
    t = x_ref.shape[0]
    rows = aw_ref.shape[0]
    n_small = smw_ref.shape[0]
    at = Place()
    me = (at.z, at.y, at.x, at.c)
    fw_copy = pltpu.make_async_copy(fw, fw_ref, local_sem.at[11])
    fw_copy.start()
    x_copy = pltpu.make_async_copy(x, x_ref, local_sem.at[12])
    x_copy.start()
    abuf[me] = aw_ref[...].astype(bf)
    pad = jnp.zeros((1, sbuf.shape[-1] - n_small), f32)
    sbuf[me] = jnp.concatenate([smw_ref[...].reshape(1, n_small), pad], axis=1)
    attn = ColumnGather(at, abuf, asend, arecv)
    ffn = Gather(at, fbuf, fsend, frecv)
    small = SmallGather(at, sbuf, ssend, srecv)
    near = attn.near
    greet([at.at_layer((at.z + d) % LAYERS) for d in (1, 2, 3)] + [at.n1, at.n2, at.sib])
    pl.when(at.z == 3)(lambda: attn.along(3))
    small.start()
    pl.when(at.z == 3)(lambda: attn.z_in(2))
    attn.along(near[0])
    attn.spread(near[0])
    fw_copy.wait()
    fbuf[me + (slice(0, rows),)] = fw_ref[0].astype(bf)
    fbuf[me + (slice(rows, 2 * rows),)] = fw_ref[1].astype(bf)
    small.spread()
    small.forward()
    attn.z_in(near[1])
    attn.along(near[1])
    attn.spread(near[1])
    attn.first_in(near[0])
    pl.when(at.z == 2)(lambda: attn.z_in(3))
    pl.when(at.z == 2)(lambda: attn.along(3))
    small.cross()
    attn.z_in(near[2])
    attn.along(near[2])
    attn.spread(near[2])
    attn.first_in(near[1])
    pl.when(at.z == 1)(lambda: attn.z_in(3))
    pl.when(at.z == 1)(lambda: attn.along(3))
    small.done()
    for i in range(32):
        z, y, x, c = i // 8, (i // 4) % 2, (i // 2) % 2, i % 2
        piece = sbuf[z, y, x, c]
        sm_ref[:, n_small * i : n_small * (i + 1)] = piece[:, 0:n_small].astype(bf).astype(f32)
    for n in range(2):
        bias_ref[n] = column(sm_ref[:, (4 + n) * D : (5 + n) * D])
    ffn.start()
    for layer in range(3):
        attn.own_in(layer)

    def last_z():
        pl.when(at.z == 0)(lambda: attn.z_in(3))
        attn.first(3).start()
        attn.second(3).start()

    def firsts():
        attn.first_in(near[2])
        attn.across(1).start()

    def seconds():
        for layer in near:
            attn.second_in(layer)
        attn.across(2).start()

    def thirds():
        for layer in near:
            attn.third_in(layer)
        attn.across(3).start()

    def last_across():
        attn.second_in(3)
        attn.third_in(3)
        attn.across_last().start()

    def inner(j, n):
        return lambda: pl.when(ffn.inner())(lambda: ffn.z_in(j, n))

    def outer(j, n):
        return lambda: pl.when(jnp.logical_not(ffn.inner()))(lambda: ffn.z_in(j, n))

    def inner_second(j):
        return lambda: pl.when(ffn.inner())(lambda: ffn.second_in(j))

    def outer_second(j):
        return lambda: pl.when(jnp.logical_not(ffn.inner()))(lambda: ffn.second_in(j))

    ticks = {
        (0, 0): [firsts],
        (0, 1): [seconds, lambda: ffn.z_in(1, 0), inner(2, 0)],
        (0, 2): [last_z, ffn.first_in],
        (1, 0): [thirds],
        (1, 1): [inner(3, 0), lambda: attn.first_in(3), outer(2, 0)],
        (1, 2): [inner(1, 1), inner(2, 1)],
        (2, 0): [last_across, outer(1, 1), lambda: ffn.second_in(0)],
        (2, 1): [],
        (2, 2): [inner(3, 1), outer(3, 0)],
        (3, 0): [inner_second(1)],
        (3, 1): [outer_second(1), inner_second(2)],
        (3, 2): [outer(2, 1), lambda: ffn.done(0)],
    }
    x_copy.wait()
    q_rows, k_rows = segment_rows(seg_ref[...])
    for g, (gy, gx) in enumerate(attn.columns):
        if g:
            attn.across_in(g)
        base = (2 * gy + gx) * 2 * rows
        w = abuf[0:3, gy, gx].reshape(6 * rows, D)
        p = dot(w, x_ref[...], NT)
        for sec in range(3):
            part = p[2 * rows * sec : 2 * rows * (sec + 1)]
            if sec != 1:
                part = part + widen(bias_ref[sec // 2, pl.ds(pl.multiple_of(base, HD), 2 * rows), :], t)
            qkv_ref[pl.ds(pl.multiple_of(sec * D + base, HD), 2 * rows), :] = part.astype(bf)

        def head(i, _, g=g, base=base):
            for k in range(3):

                @pl.when(i == k)
                def _(k=k):
                    for event in ticks[g, k]:
                        event()

            h = base // HD + i
            r = rows_at(h, HD)
            q = qkv_ref[r, :] * bf(0.125)
            k = qkv_ref[pl.ds(pl.multiple_of(D + h * HD, HD), HD), :]
            v = qkv_ref[pl.ds(pl.multiple_of(2 * D + h * HD, HD), HD), :]
            s = dot(jnp.concatenate([k, k_rows], 0), jnp.concatenate([q, q_rows], 0), TN)
            top = jnp.max(s, axis=0, keepdims=True)
            e = jnp.exp2((s - top) * LOG2E)
            total = jnp.sum(e, axis=0, keepdims=True)
            o_ref[r, :] = (dot(v, e.astype(bf), NN) * (1.0 / total)).astype(bf)
            l_ref[h] = top + jnp.log(total)
            return 0

        lax.fori_loop(0, 3, head, 0)
    qkv_copy = pltpu.make_async_copy(qkv_ref, qkv_out, local_sem.at[1])
    qkv_copy.start()
    o_copy = pltpu.make_async_copy(o_ref, o_out, local_sem.at[13])
    o_copy.start()
    attn.last_in()
    aout_copy = pltpu.make_async_copy(abuf, aout, local_sem.at[0])
    aout_copy.start()
    for n, i in enumerate((0, 1, 6, 7)):
        vec_ref[n] = column(sm_ref[:, D * i : D * (i + 1)])
    lanes = 256

    def first_norm(i, _):
        cs = rows_at(i, lanes)
        wo = abuf[3].reshape(D, D)
        vec = [widen(vec_ref[n], lanes) for n in range(4)]
        r1 = jnp.transpose(x_ref[cs, :]).astype(f32) + dot(wo, o_ref[:, cs], NN) + vec[2]
        xh, scale = norm(r1)
        xh_ref[:, cs] = xh
        rs_ref[:, cs] = scale
        a1 = xh * vec[0] + vec[1]
        r2_ref[:, cs] = a1 + vec[3]
        low_ref[:, cs] = a1.astype(bf)
        return 0

    lax.fori_loop(0, t // lanes, first_norm, 0)
    xh_copy = pltpu.make_async_copy(xh_ref, xh_out, local_sem.at[2])
    xh_copy.start()
    low_copy = pltpu.make_async_copy(low_ref, low_out, local_sem.at[14])
    low_copy.start()
    half = 4 * rows

    def write_back(j, y):
        slot = (2 * j + y) % 2
        where = pl.ds(pl.multiple_of(ffn.layer[j] * 2 * half + y * half, half), half)
        return [
            pltpu.make_async_copy(act_ref.at[slot], act_out.at[where], local_sem.at[3 + slot]),
            pltpu.make_async_copy(gp_ref.at[slot], gp_out.at[where], local_sem.at[5 + slot]),
        ]

    fout_copies = []
    for j in range(LAYERS):
        layer = ffn.layer[j]
        if j == 1:
            inner_second(3)()
            outer_second(2)()
            outer(3, 1)()
        if j == 2:
            outer_second(3)()
        if j:
            ffn.done(j)
        fout_copies.append(pltpu.make_async_copy(fbuf.at[layer], fout.at[layer], local_sem.at[7 + j]))
        fout_copies[-1].start()
        for y in range(2):
            slot = (2 * j + y) % 2
            w1 = fbuf[layer, y, :, :, 0:rows, :].reshape(half, D)
            w2 = fbuf[layer, y, :, :, rows : 2 * rows, :].reshape(half, D)
            bias = sm_ref[:, pl.ds(pl.multiple_of(8 * D + layer * 2 * half + y * half, 128), half)]
            hid = dot(w1, low_ref[...], NN) + widen(column(bias), t)
            act, slope = gelu_both(hid)
            act = act.astype(bf)
            if 2 * j + y >= 2:
                for copy in write_back((2 * j + y - 2) // 2, y):
                    copy.wait()
            act_ref[slot] = act
            gp_ref[slot] = slope.astype(bf)
            for copy in write_back(j, y):
                copy.start()
            r2_ref[...] += dot(w2, act, TN)
    r2_copy = pltpu.make_async_copy(r2_ref, r2_out, local_sem.at[15])
    r2_copy.start()
    for y in range(2):
        for copy in write_back(LAYERS - 1, y):
            copy.wait()
    attn.drain()
    ffn.drain()
    small.drain()
    for copy in [aout_copy, qkv_copy, xh_copy, o_copy, low_copy, r2_copy] + fout_copies:
        copy.wait()


def forward_call(x, seg, aw, fw, smw):
    t, rows = x.shape[0], aw.shape[0]
    ff = 32 * rows
    n = 32 * smw.shape[0]
    wide = -(-smw.shape[0] // 128) * 128
    vm, anyw = pl.BlockSpec(memory_space=pltpu.VMEM), pl.BlockSpec(memory_space=pl.ANY)
    shape = jax.ShapeDtypeStruct
    sems = pltpu.SemaphoreType.DMA
    return pl.pallas_call(
        forward_kernel,
        name="gather_forward",
        in_specs=[vm] * 3 + [anyw] * 2,
        out_specs=[anyw, anyw, vm, anyw, anyw, vm, anyw, vm, anyw, anyw, anyw, anyw],
        out_shape=[
            shape((4, 2, 2, 2, rows, D), bf), shape((4, 2, 2, 2, 2 * rows, D), bf), shape((1, n), f32),
            shape((3 * D, t), bf), shape((D, t), bf), shape((HEADS, 1, t), f32), shape((D, t), f32),
            shape((1, t), f32), shape((D, t), bf), shape((D, t), f32), shape((ff, t), bf), shape((ff, t), bf),
        ],
        scratch_shapes=[
            pltpu.VMEM((4, 2, 2, 2, rows, D), bf), pltpu.VMEM((4, 2, 2, 2, 2 * rows, D), bf),
            pltpu.VMEM((4, 2, 2, 2, 1, wide), f32),
            pltpu.VMEM((3 * D, t), bf), pltpu.VMEM((D, t), f32), pltpu.VMEM((2, 4 * rows, t), bf),
            pltpu.VMEM((2, 4 * rows, t), bf), pltpu.VMEM((4, D, 128), f32), pltpu.VMEM((2, D, 128), f32),
            pltpu.VMEM((t, D), bf), pltpu.VMEM((2, rows, D), f32), pltpu.VMEM((D, t), bf), pltpu.VMEM((D, t), bf),
            pltpu.VMEM((D, t), f32),
            sems((27,)), sems((24,)), sems((23,)), sems((20,)), sems((7,)), sems((7,)), sems((16,)),
        ],
        compiler_params=pltpu.CompilerParams(
            vmem_limit_bytes=VMEM_LIMIT, collective_id=0, has_side_effects=True
        ),
    )(seg, aw, smw, x, fw)


def norm_back(dy, xh, scale, gain):
    dx = dy * gain
    mean_one = jnp.mean(dx, axis=0, keepdims=True)
    mean_two = jnp.mean(dx * xh, axis=0, keepdims=True)
    return scale * (dx - mean_one - xh * mean_two)


def accumulate(ref, term):
    ref[...] = ref[...] + term[...]


class Scatter:
    def __init__(self, at, layers, own, cross, pair, single, column, send, recv):
        self.at, self.layers, self.own, self.cross, self.pair, self.single = at, layers, own, cross, pair, single
        self.column, self.send, self.recv = column, send, recv
        self.p = (1 - at.c) * at.x + at.c * at.y

    def copy(self, src, dst, kind, layer, peer):
        n = kind * len(self.layers) + self.layers.index(layer)
        return remote(src, dst, self.send.at[n], self.recv.at[n], peer)

    def across(self, layer, src=None):
        dst = self.cross.at[self.layers.index(layer)]
        return self.copy(dst if src is None else src, dst, 0, layer, self.at.sib)

    def far(self, layer):
        dst = self.pair.at[self.layers.index(layer), 1 - self.p]
        return self.copy(self.own(layer, self.at.far_yx), dst, 1, layer, self.at.n2)

    def near(self, layer):
        dst = self.pair.at[self.layers.index(layer), self.p]
        return self.copy(self.own(layer, self.at.n2_yx), dst, 2, layer, self.at.n2)

    def first(self, layer):
        dst = self.single.at[self.layers.index(layer)]
        return self.copy(self.own(layer, self.at.n1_yx), dst, 3, layer, self.at.n1)

    def cross_in(self, layer):
        at, i = self.at, self.layers.index(layer)
        self.across(layer).wait_recv()
        for yx, copy in ((at.far_yx, self.far), (at.n2_yx, self.near), (at.n1_yx, None), ((at.y, at.x), None)):
            accumulate(self.own(layer, yx), self.cross.at[(i,) + yx])
            if copy is not None:
                copy(layer).start()

    def pair_in(self, layer):
        i = self.layers.index(layer)
        self.far(layer).wait_recv()
        accumulate(self.own(layer, self.at.n1_yx), self.pair.at[i, 1 - self.p])
        self.first(layer).start()
        self.near(layer).wait_recv()
        accumulate(self.own(layer, (self.at.y, self.at.x)), self.pair.at[i, self.p])

    def single_in(self, layer):
        self.first(layer).wait_recv()
        own = self.own(layer, (self.at.y, self.at.x))
        total = own[...].astype(f32) + self.single[self.layers.index(layer)].astype(f32)
        self.column[self.layers.index(layer)] = total.astype(bf)

    def drain(self, layer, src):
        self.across(layer, src).wait_send()
        for copy in (self.far, self.near, self.first):
            copy(layer).wait_send()


class Along:
    def __init__(self, at, column, land, send, recv):
        self.at, self.column, self.land, self.send, self.recv = at, column, land, send, recv

    def copy(self, layer):
        return remote(
            self.column.at[layer], self.land.at[self.at.z], self.send.at[layer], self.recv.at[self.at.z],
            self.at.at_layer(layer),
        )

    def start(self, layer):
        pl.when(self.at.z != layer)(lambda: self.copy(layer).start())

    def finish(self):
        total = self.column[self.at.z].astype(f32)
        for d in (1, 2, 3):
            layer = (self.at.z + d) % LAYERS
            ref = self.land.at[layer]
            remote(ref, ref, self.send.at[layer], self.recv.at[layer], self.at.sib).wait_recv()
            total = total + ref[...].astype(f32)
        return total

    def drain(self):
        for layer in range(LAYERS):
            pl.when(self.at.z != layer)(lambda layer=layer: self.copy(layer).wait_send())


VECS = (0, 2, 3)
EARLY = (0, 1)
LATE = (2, 3)


def middle_kernel(
    cot_ref, seg_ref, rs_ref, low_ref, r2_ref, sm_ref, w_ref, act_ref, gp_ref, o_in, xh_in, abuf,
    out_ref, dr1_ref, do_ref, dwo_ref, dw_out, sg_ref, column_ref,
    acc_ref, df_ref, vec_ref, part_ref, stage, cross, pair, single, o_ref, xh_ref, wo_ref,
    send, recv, local_sem,
):
    step = pl.program_id(0)
    t = cot_ref.shape[0]
    rows = w_ref.shape[4] // 2
    half = 4 * rows
    lanes = 256
    at = Place()

    def own(layer, yx):
        return stage.at[(layer,) + yx + (at.c,)]

    def source(layer):
        return stage.at[layer, :, :, 1 - at.c]

    ffn = Scatter(at, EARLY, own, cross, pair, single, column_ref, send, recv)
    late = [pltpu.make_async_copy(stage.at[layer], dw_out.at[layer - 2], local_sem.at[layer - 2]) for layer in LATE]

    tail_inputs = [
        pltpu.make_async_copy(o_in, o_ref, local_sem.at[2]), pltpu.make_async_copy(xh_in, xh_ref, local_sem.at[3]),
        pltpu.make_async_copy(abuf.at[3], wo_ref, local_sem.at[4]),
    ]

    def vec(i):
        return widen(vec_ref[VECS.index(i)], lanes)

    def over_lanes(piece):
        def body(c, _):
            piece(rows_at(c, lanes))
            return 0

        lax.fori_loop(0, t // lanes, body, 0)

    @pl.when(step == 0)
    def _():
        for copy in tail_inputs:
            copy.start()
        greet([at.n1, at.n2, at.sib])
        for n, i in enumerate(VECS):
            vec_ref[n] = column(sm_ref[:, D * i : D * (i + 1)])
        part_ref[...] = jnp.zeros_like(part_ref)

        def second_norm(cs):
            xh, scale = norm(r2_ref[:, cs])
            out_ref[cs, :] = jnp.transpose((xh * vec(2) + vec(3)).astype(bf))
            valid = jnp.where(seg_ref[:, cs] >= 0, 1.0, 0.0)
            dy = jnp.transpose(cot_ref[cs, :]).astype(f32) * valid
            dr = norm_back(dy, xh, scale, vec(2))
            acc_ref[:, cs] = dr
            df_ref[:, cs] = dr.astype(bf)
            part_ref[0] += lane_fold(dy * xh)
            part_ref[1] += lane_fold(dy)
            part_ref[2] += lane_fold(dr)

        over_lanes(second_norm)

    w1 = w_ref[0, 0, :, :, 0:rows, :].reshape(half, D)
    w2 = w_ref[0, 0, :, :, rows : 2 * rows, :].reshape(half, D)
    dh = dot(w2, df_ref[...], NN) * gp_ref[...].astype(f32)
    sg_ref[:, pl.ds(pl.multiple_of(8 * D + step * half, 128), half)] = fold_row(lane_fold(dh))
    low = dh.astype(bf)
    dw2 = dot(act_ref[...], df_ref[...], NT).astype(bf)
    dw1 = dot(low, low_ref[...], NT).astype(bf)

    for x in range(2):
        for c in range(2):
            part = slice((2 * x + c) * rows, (2 * x + c + 1) * rows)
            stage[step // 2, step % 2, x, c, 0:rows, :] = dw1[part]
            stage[step // 2, step % 2, x, c, rows : 2 * rows, :] = dw2[part]
    acc_ref[...] += dot(w1, low, TN)
    events = {
        1: [lambda: ffn.across(0, source(0)).start()],
        2: [lambda: ffn.cross_in(0)],
        3: [lambda: ffn.across(1, source(1)).start()],
        4: [lambda: ffn.pair_in(0), lambda: ffn.cross_in(1)],
        5: [lambda: ffn.single_in(0), late[0].start],
        6: [lambda: ffn.pair_in(1)],
        7: [late[1].start],
    }
    for k, todo in events.items():

        @pl.when(step == k)
        def _(todo=todo):
            for event in todo:
                event()

    @pl.when(step == pl.num_programs(0) - 1)
    def _():
        for copy in tail_inputs:
            copy.wait()
        wo = wo_ref[...].reshape(D, D)

        def first_back(cs):
            dy = acc_ref[:, cs]
            xh = xh_ref[:, cs]
            dr = norm_back(dy, xh, rs_ref[:, cs], vec(0))
            dr1_ref[:, cs] = dr
            dz = dr.astype(bf)
            df_ref[:, cs] = dz
            part_ref[3] += lane_fold(dy * xh)
            part_ref[4] += lane_fold(dy)
            part_ref[5] += lane_fold(dr)
            do_ref[:, cs] = dot(wo, dz, TN).astype(bf)

        over_lanes(first_back)
        dwo_ref[...] = dot(df_ref[...], o_ref[...], NT).astype(bf)
        for n, i in enumerate((2, 3, 7, 0, 1, 6)):
            sg_ref[:, D * i : D * (i + 1)] = fold_row(part_ref[n])
        sg_ref[:, 4 * D : 6 * D] = jnp.zeros((1, 2 * D), f32)
        ffn.single_in(1)
        for copy in late:
            copy.wait()
        for layer in EARLY:
            ffn.drain(layer, source(layer))


def middle_call(cot, seg, o, xh, rs, low, r2, sm, abuf, fbuf, act, gp):
    t = cot.shape[0]
    rf = fbuf.shape[4]
    half = 2 * rf
    shape = jax.ShapeDtypeStruct
    sems = pltpu.SemaphoreType.DMA

    def whole(a):
        return pl.BlockSpec(a.shape, lambda j: (0,) * len(a.shape))

    wspec = pl.BlockSpec((1, 1, 2, 2, rf, D), lambda j: (j // 2, j % 2, 0, 0, 0, 0))
    rspec = pl.BlockSpec((half, t), lambda j: (j, 0))
    outs = [
        shape((t, D), bf), shape((D, t), f32), shape((D, t), bf), shape((D, D), bf),
        shape((2, 2, 2, 2, rf, D), bf), shape(sm.shape, f32), shape((2, rf, D), bf),
    ]
    return pl.pallas_call(
        middle_kernel,
        name="middle_scatter",
        grid=(8,),
        in_specs=[whole(a) for a in (cot, seg, rs, low, r2, sm)]
        + [wspec, rspec, rspec]
        + [pl.BlockSpec(memory_space=pl.ANY)] * 3,
        out_specs=[whole(a) for a in outs[:4]] + [pl.BlockSpec(memory_space=pl.ANY)] + [whole(a) for a in outs[5:]],
        out_shape=outs,
        scratch_shapes=[
            pltpu.VMEM((D, t), f32), pltpu.VMEM((D, t), bf), pltpu.VMEM((3, D, 128), f32),
            pltpu.VMEM((6, D, 128), f32), pltpu.VMEM((4, 2, 2, 2, rf, D), bf), pltpu.VMEM((2, 2, 2, rf, D), bf),
            pltpu.VMEM((2, 2, rf, D), bf), pltpu.VMEM((2, rf, D), bf), pltpu.VMEM((D, t), bf), pltpu.VMEM((D, t), f32),
            pltpu.VMEM(abuf.shape[1:], bf), sems((8,)), sems((8,)), sems((5,)),
        ],
        compiler_params=pltpu.CompilerParams(
            vmem_limit_bytes=VMEM_LIMIT, collective_id=2, has_side_effects=True
        ),
    )(cot, seg, rs, low, r2, sm, fbuf, act, gp, o, xh, abuf)


class ColumnScatter:
    def __init__(self, at, own, cross, pair, single, column, along, send, recv):
        self.at, self.own, self.cross, self.pair, self.single = at, own, cross, pair, single
        self.column, self.along, self.send, self.recv = column, along, send, recv
        self.columns = [(1 - at.y, 1 - at.x), (at.y, 1 - at.x), (1 - at.y, at.x), (at.y, at.x)]

    def part(self, yx, core):
        return self.own.at[(slice(0, 3),) + yx + (core,)]

    def across(self, g):
        yx = self.columns[g]
        return remote(
            self.part(yx, 1 - self.at.c), self.cross.at[(slice(None),) + yx], self.send.at[g], self.recv.at[g],
            self.at.sib,
        )

    def hop(self, kind):
        at = self.at
        yx, dst, peer = (
            (at.far_yx, self.pair.at[0], at.n2), (at.n2_yx, self.pair.at[1], at.n2), (at.n1_yx, self.single, at.n1)
        )[kind]
        return remote(self.part(yx, at.c), dst, self.send.at[4 + kind], self.recv.at[4 + kind], peer)

    def add(self, yx, terms):
        for layer in range(3):
            accumulate(self.own.at[(layer,) + yx + (self.at.c,)], terms(layer))

    def cross_in(self, g):
        yx = self.columns[g]
        self.across(g).wait_recv()
        self.add(yx, lambda layer: self.cross.at[(layer,) + yx])

    def far_out(self):
        self.cross_in(0)
        self.hop(0).start()

    def first_out(self):
        self.hop(0).wait_recv()
        self.add(self.at.n1_yx, lambda layer: self.pair.at[0, layer])
        self.hop(2).start()

    def neighbour_out(self, g):
        self.cross_in(g)
        pl.when(self.at.c == g - 1)(self.first_out)
        pl.when(self.at.c != g - 1)(lambda: self.hop(1).start())

    def own_out(self):
        at = self.at
        self.across(3).wait_recv()
        self.hop(1).wait_recv()
        self.hop(2).wait_recv()
        for layer in range(3):
            total = self.own[layer, at.y, at.x, at.c].astype(f32) + self.cross[layer, at.y, at.x].astype(f32)
            total = total + self.pair[1, layer].astype(f32) + self.single[layer].astype(f32)
            self.column[layer] = total.astype(bf)
            self.along.start(layer)

    def drain(self):
        for g in range(4):
            self.across(g).wait_send()
        for kind in range(3):
            self.hop(kind).wait_send()


class SmallScatter:
    def __init__(self, at, own, cross, pair, single, land, send, recv):
        self.at, self.own, self.cross, self.pair, self.single, self.land = at, own, cross, pair, single, land
        self.send, self.recv = send, recv

    def part(self, yx, core):
        return self.own.at[(slice(None),) + yx + (core,)]

    def across(self):
        at = self.at
        return remote(
            self.own.at[:, :, :, 1 - at.c], self.cross, self.send.at[0], self.recv.at[0], at.sib
        )

    def far(self):
        return remote(self.part(self.at.far_yx, self.at.c), self.pair.at[0], self.send.at[1], self.recv.at[1], self.at.n2)

    def near(self):
        return remote(self.part(self.at.n2_yx, self.at.c), self.pair.at[1], self.send.at[2], self.recv.at[2], self.at.n2)

    def first(self):
        return remote(self.part(self.at.n1_yx, self.at.c), self.single, self.send.at[3], self.recv.at[3], self.at.n1)

    def along(self, d):
        at = self.at
        layer = (at.z + d) % LAYERS
        return remote(
            self.own.at[layer, at.y, at.x, at.c], self.land.at[d], self.send.at[3 + d], self.recv.at[3 + d],
            at.at_layer(layer),
        )

    def cross_in(self):
        at = self.at
        self.across().wait_recv()
        for yx in (at.far_yx, at.n2_yx, at.n1_yx, (at.y, at.x)):
            ref = self.part(yx, at.c)
            ref[...] += self.cross[(slice(None),) + yx]
        self.far().start()
        self.near().start()

    def pair_in(self):
        at = self.at
        self.far().wait_recv()
        ref = self.part(at.n1_yx, at.c)
        ref[...] += self.pair[0]
        self.first().start()
        self.near().wait_recv()
        ref = self.part((at.y, at.x), at.c)
        ref[...] += self.pair[1]

    def single_in(self):
        self.first().wait_recv()
        ref = self.part((self.at.y, self.at.x), self.at.c)
        ref[...] += self.single[...]
        for d in (1, 2, 3):
            self.along(d).start()

    def finish(self):
        at = self.at
        total = self.own[at.z, at.y, at.x, at.c]
        for d in (1, 2, 3):
            self.along(d).wait_recv()
            total = total + self.land[d]
        return total

    def drain(self):
        for copy in (self.across, self.far, self.near, self.first):
            copy().wait_send()
        for d in (1, 2, 3):
            self.along(d).wait_send()


CQ = 512


def backward_kernel(
    seg_ref, l_ref, dwo_ref, sg_ref, early_ref, dwf, abuf, dr1, qkv_in, o_in, do_in, x_in,
    dx, gf_ref, ga_ref, gs_ref,
    g_ref, dwa, w_ref, dr1_ref, dx_ref, small_ref, qkv_ref, o_ref, do_ref, x_ref,
    fown, fcross, fpair, fsingle, fcolumn, fland,
    across_ref, apair, asingle, acolumn, aland, wcross, wpair, wsingle,
    scross, spair, ssingle, sland,
    fsend, frecv, fzsend, fzrecv, asend, arecv, azsend, azrecv, wsend, wrecv, ssend, srecv, local_sem,
):
    t = x_ref.shape[0]
    at = Place()
    rows = w_ref.shape[4]
    n_small = sg_ref.shape[1] // 32
    f_along = Along(at, fcolumn, fland, fzsend, fzrecv)
    a_along = Along(at, acolumn, aland, azsend, azrecv)
    ffn = Scatter(
        at, LATE, lambda layer, yx: fown.at[(layer - 2,) + yx], fcross, fpair, fsingle, fcolumn.at[2:4], fsend, frecv
    )
    last = Scatter(
        at, (3,), lambda layer, yx: dwa.at[(3,) + yx + (at.c,)], wcross, wpair, wsingle, acolumn.at[3:4], wsend, wrecv
    )
    attn = ColumnScatter(at, dwa, across_ref, apair, asingle, acolumn, a_along, asend, arecv)
    small = SmallScatter(at, small_ref, scross, spair, ssingle, sland, ssend, srecv)

    def ffn_source(layer):
        return dwf.at[layer - 2, :, :, 1 - at.c]

    last_source = dwa.at[3, :, :, 1 - at.c]
    inputs = [
        pltpu.make_async_copy(src, dst, local_sem.at[5 + n])
        for n, (src, dst) in enumerate(((qkv_in, qkv_ref), (o_in, o_ref), (do_in, do_ref), (x_in, x_ref)))
    ]
    for copy in inputs:
        copy.start()
    loads = [
        pltpu.make_async_copy(dwf.at[layer - 2, :, :, at.c], fown.at[layer - 2], local_sem.at[layer - 2])
        for layer in LATE
    ]
    for copy in loads:
        copy.start()
    w_copy = pltpu.make_async_copy(abuf.at[0:3], w_ref, local_sem.at[2])
    w_copy.start()
    dr1_copy = pltpu.make_async_copy(dr1, dr1_ref, local_sem.at[3])
    dr1_copy.start()
    fcolumn[0:2] = early_ref[...]
    greet([at.at_layer((at.z + d) % LAYERS) for d in (1, 2, 3)] + [at.n1, at.n2, at.sib])
    for layer in LATE:
        ffn.across(layer, ffn_source(layer)).start()
    for y in range(2):
        for x in range(2):
            for c in range(2):
                i = y * 4 + x * 2 + c
                dwa[3, y, x, c] = dwo_ref[i * rows : (i + 1) * rows]
    last.across(3, last_source).start()
    for layer in EARLY:
        f_along.start(layer)

    def ffn_cross(layer):
        loads[layer - 2].wait()
        ffn.cross_in(layer)

    def ffn_single(layer):
        ffn.single_in(layer)
        f_along.start(layer)

    def last_single():
        last.single_in(3)
        a_along.start(3)

    ticks = {
        (0, 1): [lambda: ffn_cross(2)],
        (0, 2): [lambda: ffn_cross(3)],
        (1, 1): [attn.far_out, lambda: ffn.pair_in(2)],
        (1, 2): [lambda: last.cross_in(3)],
        (2, 0): [lambda: ffn.pair_in(3)],
        (2, 1): [lambda: attn.neighbour_out(1), lambda: ffn_single(2)],
        (2, 2): [lambda: last.pair_in(3)],
        (3, 0): [lambda: ffn_single(3)],
        (3, 1): [lambda: attn.neighbour_out(2), last_single],
    }
    for copy in inputs:
        copy.wait()
    q_rows, k_rows = segment_rows(seg_ref[...])
    for g, (gy, gx) in enumerate(attn.columns):
        base = (2 * gy + gx) * 2 * rows

        def head(i, _, g=g, base=base):
            for k in range(3):
                if (g, k) in ticks:

                    @pl.when(i == k)
                    def _(k=k):
                        for event in ticks[g, k]:
                            event()

            h = base // HD + i
            hrows = rows_at(h, HD)
            krow = pl.ds(pl.multiple_of(D + h * HD, HD), HD)
            vrow = pl.ds(pl.multiple_of(2 * D + h * HD, HD), HD)
            q, k, v, do = qkv_ref[hrows, :], qkv_ref[krow, :], qkv_ref[vrow, :], do_ref[hrows, :]
            inner = jnp.sum(do.astype(f32) * o_ref[hrows, :].astype(f32), axis=0, keepdims=True)
            lrow = l_ref[h]
            keys = jnp.concatenate([k, k_rows], 0)
            queries = jnp.concatenate([q * bf(0.125), q_rows], 0)
            dv = dk = 0.0
            for n in range(t // CQ):
                cs = slice(n * CQ, (n + 1) * CQ)
                s = dot(keys, queries[:, cs], TN)
                p = jnp.exp2((s - lrow[:, cs]) * LOG2E)
                dp = dot(v, do[:, cs], TN)
                ds = (p * (dp - inner[:, cs])).astype(bf)
                dv = dv + dot(do[:, cs], p.astype(bf), NT)
                dk = dk + dot(q[:, cs], ds, NT)
                g_ref[hrows, cs] = (dot(k, ds, NN) * 0.125).astype(bf)
            g_ref[vrow, :] = dv.astype(bf)
            g_ref[krow, :] = (dk * 0.125).astype(bf)
            return 0

        lax.fori_loop(0, 3, head, 0)
        if g == 3:
            sums = [sg_ref[:, 0 : 4 * D]]
            for sec in (0, 2):
                sums.append(fold_row(lane_fold(g_ref[sec * D : (sec + 1) * D, :].astype(f32))))
            sums = jnp.concatenate(sums + [sg_ref[:, 6 * D :]], axis=1)
            pad = jnp.zeros((1, small_ref.shape[-1] - n_small), f32)
            for i in range(32):
                z, y, x, c = i // 8, (i // 4) % 2, (i // 2) % 2, i % 2
                small_ref[z, y, x, c] = jnp.concatenate([sums[:, i * n_small : (i + 1) * n_small], pad], axis=1)
            small.across().start()
        for sec in range(3):
            grad = g_ref[pl.ds(pl.multiple_of(sec * D + base, HD), 2 * rows), :]
            dw = dot(grad, x_ref[...], NN).astype(bf)
            for c in range(2):
                dwa[sec, gy, gx, c] = dw[c * rows : (c + 1) * rows]
        attn.across(g).start()
    small.cross_in()
    attn.own_out()
    w_copy.wait()
    dr1_copy.wait()
    lanes = 256

    def input_block(i, _):
        cs = rows_at(i, lanes)
        w = w_ref[...].reshape(3 * D, D)
        dx_ref[cs, :] = jnp.transpose(dr1_ref[:, cs]) + dot(g_ref[:, cs], w, TN)
        return 0

    lax.fori_loop(0, 1, input_block, 0)
    small.pair_in()
    lax.fori_loop(1, 3, input_block, 0)
    small.single_in()
    lax.fori_loop(3, t // lanes, input_block, 0)
    dx_copy = pltpu.make_async_copy(dx_ref, dx, local_sem.at[4])
    dx_copy.start()
    gf_ref[...] = f_along.finish()
    ga_ref[...] = a_along.finish()
    gs_ref[...] = small.finish()
    for layer in LATE:
        ffn.drain(layer, ffn_source(layer))
    last.drain(3, last_source)
    for stage in (attn, f_along, a_along, small):
        stage.drain()
    dx_copy.wait()


def backward_call(x, seg, qkv, o, logs, do, dwo, sg, early, dwf, abuf, dr1):
    t = x.shape[0]
    ra, rf = abuf.shape[4], dwf.shape[4]
    wide = -(-(sg.shape[1] // 32) // 128) * 128
    vm, anyw = pl.BlockSpec(memory_space=pltpu.VMEM), pl.BlockSpec(memory_space=pl.ANY)
    shape = jax.ShapeDtypeStruct
    sems = pltpu.SemaphoreType.DMA

    def half(*dims):
        return pltpu.VMEM(dims + (D,), bf)

    def small(*dims):
        return pltpu.VMEM(dims + (1, wide), f32)

    return pl.pallas_call(
        backward_kernel,
        name="backward_scatter",
        in_specs=[vm] * 5 + [anyw] * 7,
        out_specs=[anyw, vm, vm, vm],
        out_shape=[shape((t, D), f32), shape((rf, D), f32), shape((ra, D), f32), shape((1, wide), f32)],
        scratch_shapes=[
            pltpu.VMEM((3 * D, t), bf), half(4, 2, 2, 2, ra), half(3, 2, 2, 2, ra), pltpu.VMEM((D, t), f32),
            pltpu.VMEM((t, D), f32), small(4, 2, 2, 2),
            pltpu.VMEM((3 * D, t), bf), pltpu.VMEM((D, t), bf), pltpu.VMEM((D, t), bf), pltpu.VMEM((t, D), bf),
            half(2, 2, 2, rf), half(2, 2, 2, rf), half(2, 2, rf), half(2, rf), half(4, rf), half(4, rf),
            half(3, 2, 2, ra), half(2, 3, ra), half(3, ra), half(4, ra), half(4, ra), half(1, 2, 2, ra),
            half(1, 2, ra), half(1, ra),
            small(4, 2, 2), small(2, 4), small(4), small(4),
            sems((8,)), sems((8,)), sems((4,)), sems((4,)), sems((7,)), sems((7,)), sems((4,)), sems((4,)),
            sems((4,)), sems((4,)), sems((7,)), sems((7,)), sems((9,)),
        ],
        compiler_params=pltpu.CompilerParams(
            vmem_limit_bytes=VMEM_LIMIT, collective_id=1, has_side_effects=True
        ),
    )(seg, logs, dwo, sg, early, dwf, abuf, dr1, qkv, o, do, x)


def gradients_block(features, cotangent, segment_ids, attn_weights, ffn_weights, small_params):
    t, rows = features.shape[0], attn_weights.shape[0]
    seg = segment_ids.reshape(1, t)
    abuf, fbuf, sm, qkv, o, logs, xh, rs, low, r2, act, gp = forward_call(
        features, seg, attn_weights, ffn_weights, small_params
    )
    outputs, dr1, do, dwo, dwf, sg, early = middle_call(cotangent, seg, o, xh, rs, low, r2, sm, abuf, fbuf, act, gp)
    input_grad, gf, ga, gs = backward_call(
        features, seg, qkv, o, logs, do, dwo, sg, early, dwf, abuf, dr1
    )
    return outputs, input_grad, ga, gf.reshape(2, rows, D), gs[0, : small_params.shape[0]]


def local(
    gradients,
    features, cotangent, segment_ids, attn_weights, ffn_weights, small_params,
    attn_first, ffn_first, small_first, attn_second, ffn_second, small_second,
    attn_ema, ffn_ema, small_ema,
):
    outputs, input_grad, attn_sum, ffn_sum, small_sum = gradients(
        features, cotangent, segment_ids, attn_weights, ffn_weights, small_params
    )
    attn = adam_step(attn_weights, attn_sum, attn_first, attn_second, attn_ema, 0.01, 0.05)
    ffn = adam_step(ffn_weights, ffn_sum, ffn_first, ffn_second, ffn_ema, 0.01, 0.05)
    small = adam_step(small_params, small_sum, small_first, small_second, small_ema, 0.0, 0.3)
    return (outputs, input_grad) + tuple(x for trio in zip(attn, ffn, small) for x in trio)


def solution(mesh):
    block = mesh.shape["dp"] == 8 and mesh.shape["fsdp"] == 4
    gradients = gradients_block if block else gradients_general
    row = P(("dp", "fsdp"), None)
    wide = P(None, ("dp", "fsdp"), None)
    flat = P(("dp", "fsdp"))
    state = (row, wide, flat)
    return jax.shard_map(
        partial(local, gradients),
        mesh=mesh,
        in_specs=(row, row, flat) + state * 4,
        out_specs=(row, row) + state * 4,
        check_vma=False,
    )
```
